512 devices in a mesh: dom: 128 (over z, x, core), member: 4 (over y).
Axes of the slice: x: 4, y: 4, z: 16, core: 2. Of those that a mesh axis runs over, the one named last changes fastest.
Arguments:
- node_latents: bfloat16 [4, 4096, 512], P('member', 'dom'), may hold values from -24 to 24
- edge_latents: bfloat16 [4, 32768, 512], P('member', 'dom'), may hold values from -24 to 24
- node_cotangent: bfloat16 [4, 4096, 512], P('member', 'dom'), may hold values from -6 to 6
- w_in: bfloat16 [1536, 512], replicated, may hold values from -0.15625 to 0.15625
- bias: float32 [512], replicated, may hold values from -3 to 3
- gain: float32 [512], replicated, may hold values from 0.5 to 1.5
- receivers: int32 [32768], P('dom'), may hold values from 0 to 31, as said below
- senders: int32 [32768], P('dom'), may hold values from 0 to 287, as said below
- send_rows: int32 [128, 128, 2], P('dom'), may hold values from 0 to 31, as said below
- node_count: int32 [128], P('dom'), may hold values from 16 to 32
- edge_count: int32 [128], P('dom'), may hold values from 32 to 256
Outputs:
- new_nodes: bfloat16 [4, 4096, 512], P('member', 'dom')
- grad_nodes: bfloat16 [4, 4096, 512], P('member', 'dom')
- grad_edges: bfloat16 [4, 32768, 512], P('member', 'dom')
- grad_weights: float32 [1536, 512], P('dom')
- grad_bias: float32 [512], replicated
- grad_gain: float32 [512], replicated
The draws below stay inside these ranges and needn't reach their ends.
Inputs may be any that keep to these rules, and one draw needn't show every extreme that they name: Within each partition's 256 edge slots the receivers never fall and lie below that partition's node count. `senders`: A partition's node table is its own 32 node rows followed by the 2 rows received from each partition in partition order; an own row named by a live edge lies below the partition's node count. `send_rows`: entry [p, q, k] is the k-th of the exactly 2 node rows that partition p sends to partition q, below p's node count.
All inputs are finite; a program needn't handle non-finite values.
Results may differ from the reference program's by a relative error of at most 0.014.
Values may be sent and summed in bfloat16 or wider, within the bound.
A program may use at most 64 MiB of HBM per device.

```python
import jax
import jax.numpy as jnp
from jax import lax

D = 512
NODE_DEV = 32
SLOT = 2
EDGE_DEV = 256
PARTITIONS = 128
MEMBERS = 4
NODES = 4096
EDGES = 32768


def shared_counts(key):
    node_count = jax.random.randint(jax.random.fold_in(key, 101), (PARTITIONS,), NODE_DEV // 2, NODE_DEV + 1)
    full_node = jax.random.randint(jax.random.fold_in(key, 102), (), 0, PARTITIONS)
    node_count = jnp.where(jnp.arange(PARTITIONS) == full_node, NODE_DEV, node_count)
    edge_count = jax.random.randint(jax.random.fold_in(key, 103), (PARTITIONS,), EDGE_DEV // 8, EDGE_DEV + 1)
    full_edge = jax.random.randint(jax.random.fold_in(key, 104), (), 0, PARTITIONS)
    edge_count = jnp.where(jnp.arange(PARTITIONS) == full_edge, EDGE_DEV, edge_count)
    return (node_count.astype(jnp.int32), edge_count.astype(jnp.int32))


def draw_node_count(key, part):
    counts = shared_counts(key)
    return counts[0]


def draw_edge_count(key, part):
    counts = shared_counts(key)
    return counts[1]


def draw_receivers(key, part):
    node_count, edge_count = shared_counts(key)
    key = jax.random.fold_in(key, 3)
    drawn = jax.random.randint(key, (PARTITIONS, EDGE_DEV), 0, node_count[:, None])
    drawn = jnp.sort(drawn, axis=1)
    position = jnp.arange(EDGE_DEV)[None, :]
    drawn = jnp.where(position >= edge_count[:, None] - 1, node_count[:, None] - 1, drawn)
    return drawn.reshape(-1).astype(jnp.int32)


def draw_senders(key, part):
    node_count, edge_count = shared_counts(key)
    key = jax.random.fold_in(key, 4)
    choose = jax.random.randint(jax.random.fold_in(key, 1), (PARTITIONS, EDGE_DEV), 0, 2)
    local_rows = jax.random.randint(jax.random.fold_in(key, 2), (PARTITIONS, EDGE_DEV), 0, node_count[:, None])
    remote_rows = NODE_DEV + jax.random.randint(jax.random.fold_in(key, 3), (PARTITIONS, EDGE_DEV), 0, PARTITIONS * SLOT)
    drawn = jnp.where(choose == 0, local_rows, remote_rows)
    drawn = drawn.at[0, 0].set(NODE_DEV + PARTITIONS * SLOT - 1)
    drawn = drawn.at[0, 1].set(0)
    return drawn.reshape(-1).astype(jnp.int32)


def draw_send_rows(key, part):
    node_count, edge_count = shared_counts(key)
    key = jax.random.fold_in(key, 5)
    drawn = jax.random.randint(key, (PARTITIONS, PARTITIONS, SLOT), 0, node_count[:, None, None])
    diagonal = (jnp.arange(PARTITIONS)[:, None, None] == jnp.arange(PARTITIONS)[None, :, None]) & (jnp.arange(SLOT)[None, None, :] == 0)
    drawn = jnp.where(diagonal, node_count[:, None, None] - 1, drawn)
    return drawn.astype(jnp.int32)


def strengthened(result, stream_key, source, target, parts, factor):
    owner, partner = [(jnp.arange(result.shape[axis_at]) // (result.shape[axis_at] // parts)).reshape([-1 if axis == axis_at else 1 for axis in range(result.ndim)]) for axis_at in (source, target)]
    chosen = jax.random.permutation(stream_key, parts)[partner]
    strong = (owner == chosen) | (owner == (partner + parts // 2) % parts)
    return jnp.where(strong, factor * result, result)


def levels(key, dims, split, least, high):
    def one(axis_at, blocks):
        steps = jax.random.uniform(jax.random.fold_in(jax.random.fold_in(key, 6), axis_at), (blocks,), jnp.float32, least / len(split), high / len(split))
        return jnp.repeat(jnp.exp(steps), dims[axis_at] // blocks).reshape((-1,) + (1,) * (len(dims) - axis_at - 1))

    level = one(*split[0])
    for cut in split[1:]:
        level = level * one(*cut)
    return level


def noise(own_key, shape, scale, limit, pieces=(), kind=jnp.bfloat16):
    values = jax.random.normal(own_key, shape, jnp.float32) * scale
    if len(pieces) > 0:
        values = levels(own_key, shape, pieces, -0.22, 0.18) * values
    return jnp.clip(values, min=-limit, max=limit).astype(kind)


def gaussian_with(own_key, dims, deviation, bound, split, heavy, held_as=jnp.bfloat16):
    values = deviation * jax.random.normal(own_key, dims, jnp.float32)
    if split:
        values = values * levels(own_key, dims, split, -0.22, 0.18)
    return jnp.clip(strengthened(values, jax.random.fold_in(own_key, 3), *heavy), -bound, bound).astype(held_as)


def setup_inputs(seed: int = 0) -> dict:
    splits = jax.random.split(jax.random.key(seed), 12)
    node_latents = gaussian_with(splits[0], (MEMBERS, NODES, D), 1.0, 24.0, ((0, 4), (1, 128)), (1, 2, 128, 5.5))
    edge_latents = gaussian_with(splits[1], (MEMBERS, EDGES, D), 1.0, 24.0, ((0, 4), (1, 128)), (1, 2, 128, 5.5))
    node_cotangent = noise(splits[2], (MEMBERS, NODES, D), 1.0, 6.0, ((0, 4), (1, 128)))
    w_in = noise(splits[3], (3 * D, D), (3 * D) ** -0.5, 0.15625)
    bias = noise(splits[4], (D,), 0.5, 3.0, (), jnp.float32)
    gain = jnp.clip(jax.random.uniform(splits[5], (D,), jnp.float32, 0.5, 1.5), 0.5, 1.5)
    receivers = draw_receivers(jax.random.fold_in(splits[11], 71), 0)
    senders = draw_senders(jax.random.fold_in(splits[11], 71), 0)
    send_rows = draw_send_rows(jax.random.fold_in(splits[11], 71), 0)
    node_count = draw_node_count(jax.random.fold_in(splits[11], 71), 0)
    edge_count = draw_edge_count(jax.random.fold_in(splits[11], 71), 0)
    return {"node_latents": node_latents, "edge_latents": edge_latents, "node_cotangent": node_cotangent, "w_in": w_in, "bias": bias, "gain": gain, "receivers": receivers, "senders": senders, "send_rows": send_rows, "node_count": node_count, "edge_count": edge_count}


epsilon = 1e-05

def contract_rows(left, right):
    return lax.dot_general(left, right, (((0,), (0,)), ((), ())), preferred_element_type=jnp.float32)

def apply_transpose(left, right):
    return lax.dot_general(left, right, (((1,), (1,)), ((), ())), preferred_element_type=jnp.float32)

def reference(node_latents, edge_latents, node_cotangent, w_in, bias, gain, receivers, senders, send_rows, node_count, edge_count):
    w_send = w_in[:D]
    w_recv = w_in[D:2 * D]
    w_edge = w_in[2 * D:]
    edge_index = jnp.arange(EDGES, dtype=jnp.int32)
    device = edge_index // EDGE_DEV
    recv_global = device * NODE_DEV + receivers
    remote = senders - NODE_DEV
    peer = jnp.clip(remote // SLOT, 0, PARTITIONS - 1)
    slot_index = jnp.maximum(remote, 0) % SLOT
    owner_row = send_rows[peer, device, slot_index]
    send_global = jnp.where(senders < NODE_DEV, device * NODE_DEV + senders, peer * NODE_DEV + owner_row).astype(jnp.int32)
    edge_mask = edge_index % EDGE_DEV < edge_count[device]
    node_index = jnp.arange(NODES, dtype=jnp.int32)
    node_mask = node_index % NODE_DEV < node_count[node_index // NODE_DEV]

    def one_member(inputs):
        own_nodes, own_edges, cotangent = inputs
        sender_rows = own_nodes[send_global]
        receiver_rows = own_nodes[recv_global]
        preact = jnp.dot(sender_rows, w_send, preferred_element_type=jnp.float32) + jnp.dot(receiver_rows, w_recv, preferred_element_type=jnp.float32) + jnp.dot(own_edges, w_edge, preferred_element_type=jnp.float32) + bias
        sigmoid = jax.nn.sigmoid(preact)
        activated = preact * sigmoid
        average = lax.optimization_barrier(jnp.mean(activated, axis=1, keepdims=True))
        centred = activated - average
        variance = lax.optimization_barrier(jnp.mean(centred * centred, axis=1, keepdims=True))
        inverse = lax.rsqrt(variance + epsilon)
        normed = centred * inverse
        new_edges = jnp.where(edge_mask[:, None], own_edges.astype(jnp.float32) + normed * gain, 0.0).astype(jnp.bfloat16)
        aggregate = jax.ops.segment_sum(new_edges.astype(jnp.float32), recv_global, num_segments=NODES)
        new_nodes = (own_nodes.astype(jnp.float32) + aggregate).astype(jnp.bfloat16)
        upstream = jnp.where(edge_mask[:, None], cotangent[recv_global].astype(jnp.float32), 0.0)
        gain_term = lax.optimization_barrier(jnp.sum(upstream * normed, axis=0))
        normed_grad = upstream * gain
        activated_grad = inverse * (normed_grad - lax.optimization_barrier(jnp.mean(normed_grad, axis=1, keepdims=True)) - normed * lax.optimization_barrier(jnp.mean(normed_grad * normed, axis=1, keepdims=True)))
        preact_grad = (activated_grad * sigmoid * (1.0 + preact * (1.0 - sigmoid))).astype(jnp.bfloat16)
        bias_term = lax.optimization_barrier(jnp.sum(preact_grad.astype(jnp.float32), axis=0))
        grad_edges = (upstream + apply_transpose(preact_grad, w_edge)).astype(jnp.bfloat16)
        to_senders = jax.ops.segment_sum(apply_transpose(preact_grad, w_send), send_global, num_segments=NODES)
        to_receivers = jax.ops.segment_sum(apply_transpose(preact_grad, w_recv), recv_global, num_segments=NODES)
        grad_nodes = (jnp.where(node_mask[:, None], cotangent.astype(jnp.float32), 0.0) + to_receivers + to_senders).astype(jnp.bfloat16)
        weight_term = jnp.concatenate([contract_rows(sender_rows, preact_grad), contract_rows(receiver_rows, preact_grad), contract_rows(own_edges, preact_grad)], axis=0)
        return (new_nodes, grad_nodes, grad_edges, weight_term, bias_term, gain_term)
    results = lax.map(one_member, (node_latents, edge_latents, node_cotangent))
    return (results[0], results[1], results[2], lax.optimization_barrier(jnp.sum(results[3], axis=0)), lax.optimization_barrier(jnp.sum(results[4], axis=0)), lax.optimization_barrier(jnp.sum(results[5], axis=0)))
```

```python
import functools

import jax
import jax.numpy as jnp
from jax import lax
from jax.experimental import pallas as pl
from jax.experimental.pallas import tpu as pltpu
from jax.sharding import PartitionSpec as P

epsilon = 1e-05
CORES = 2
LANES = 128
F32 = jnp.float32
BF16 = jnp.bfloat16

FWD_PLANE, FWD_LINE, BWD_LINE, BWD_PLANE, FIRST_A, FIRST_B, SECOND_A, SECOND_B, LINE_W, FINAL_PLANE, FINAL_Y = range(11)
SUM_PLANE, SUM_Y, SUM_LINE = range(11, 14)
PAIR = 14


def dot(left, right):
    return jnp.dot(left, right, preferred_element_type=F32)


def contract_rows(left, right):
    return lax.dot_general(left, right, (((0,), (0,)), ((), ())), preferred_element_type=F32)


def apply_transpose(left, right):
    return lax.dot_general(left, right, (((1,), (1,)), ((), ())), preferred_element_type=F32)


def one_hot_rows(rows, index):
    return lax.broadcasted_iota(jnp.int32, (rows, index.shape[1]), 0) == index


def total(ref, count):
    acc = ref[0].astype(F32)
    for slot in range(1, count):
        acc = acc + ref[slot].astype(F32)
    return acc


def split_transpose(rows, weights):
    high = rows.astype(BF16)
    low = (rows - high.astype(F32)).astype(BF16)
    return apply_transpose(high, weights) + apply_transpose(low, weights)


def kernel(
    sizes,
    nodes_ref,
    cot_ref,
    bias_ref,
    gain_ref,
    recv_ref,
    send_ref,
    outgoing_ref,
    edges_hbm,
    w_hbm,
    node_count_ref,
    edge_count_ref,
    new_nodes_ref,
    grad_nodes_ref,
    gw_ref,
    gb_ref,
    gg_ref,
    grad_edges_hbm,
    w_ref,
    x_ref,
    pre_ref,
    up_ref,
    p_ref,
    ne_ref,
    ge_ref,
    outb,
    fwd1,
    fwd2,
    table,
    bwd0,
    bwd1,
    bwd2,
    back,
    wb,
    pair_in,
    a1,
    a1_in,
    b1,
    b1_in,
    a2,
    a2_in,
    b2,
    b2_in,
    zw,
    zw_in,
    fin,
    fin_in,
    fin_y,
    bg0,
    bg1,
    bg1_in,
    bg2,
    bg2_in,
    bg_in,
    local_sem,
    send_sem,
    recv_sem,
):
    Z, X, Y, D, NODE, EDGE = sizes
    PLANE = X * CORES
    TABLE = Z * PLANE * 2
    JJ = Z // X
    JA = JJ // 2
    HALF = 3 * D // Z // CORES
    PIECES = PLANE // CORES
    OWN = HALF // PIECES
    dom = lax.axis_index("dom")
    y = lax.axis_index("member")
    z = dom // PLANE
    plane = dom % PLANE
    x = plane // CORES
    core = plane % CORES

    def remote(src, dst, step, to_dom, to_y):
        return pltpu.make_async_remote_copy(
            src_ref=src,
            dst_ref=dst,
            send_sem=send_sem.at[step],
            recv_sem=recv_sem.at[step],
            device_id={"dom": to_dom, "member": to_y},
            device_id_type=pl.DeviceIdType.MESH,
        )

    def arrived(ref, step):
        pltpu.make_async_copy(ref, ref, recv_sem.at[step]).wait()

    def sent(ref, step):
        pltpu.make_async_copy(ref, ref, send_sem.at[step]).wait()

    def each_plane(act):
        def body(i, carry):
            peer = lax.rem(plane + PLANE // 2 + jnp.where(i < PLANE // 2, i, i + 1), PLANE)
            act(peer, z * PLANE + peer)
            return carry

        lax.fori_loop(0, PLANE - 1, body, 0)

    def each_line(act):
        def body(i, carry):
            off = Z // 2 + (1 - 2 * lax.rem(i, 2)) * ((i + 1) // 2)
            peer = lax.rem(z + off, Z)
            act(peer, peer * PLANE + plane)
            return carry

        lax.fori_loop(0, Z - 1, body, 0)

    def each_x(act):
        def body(i, carry):
            peer = lax.rem(x + 1 + i, X)
            act(peer, z * PLANE + peer * CORES + core)
            return carry

        lax.fori_loop(0, X - 1, body, 0)

    def each_y(act):
        def body(i, carry):
            act(lax.rem(y + 1 + i, Y))
            return carry

        lax.fori_loop(0, Y - 1, body, 0)

    copy_edges = pltpu.make_async_copy(edges_hbm, x_ref.at[:, pl.ds(2 * D, D)], local_sem.at[0])
    copy_w = pltpu.make_async_copy(w_hbm, w_ref, local_sem.at[1])
    copy_edges.start()
    copy_w.start()

    barrier = pltpu.get_barrier_semaphore()

    def greet(to_dom, to_y):
        pl.semaphore_signal(
            barrier,
            inc=1,
            device_id={"dom": to_dom, "member": to_y},
            device_id_type=pl.DeviceIdType.MESH,
        )

    each_plane(lambda peer, to: greet(to, y))
    each_line(lambda peer, to: greet(to, y))
    each_y(lambda peer: greet(dom, peer))

    nodes = nodes_ref[...]
    out_hot = one_hot_rows(NODE, outgoing_ref[...]).astype(BF16)
    outb[...] = contract_rows(out_hot, nodes).astype(BF16).reshape(PLANE, Z * 2, D)

    pl.semaphore_wait(barrier, (PLANE - 1) + (Z - 1) + (Y - 1))

    each_plane(lambda peer, to: remote(outb.at[peer], fwd1.at[plane], FWD_PLANE, to, y).start())
    fwd1[plane] = outb[plane]

    live = lax.broadcasted_iota(jnp.int32, (NODE, EDGE), 1) < edge_count_ref[0]
    incidence = (one_hot_rows(NODE, recv_ref[...]) & live).astype(BF16)
    x_ref[:, D : 2 * D] = contract_rows(incidence, nodes).astype(BF16)
    up_ref[...] = contract_rows(incidence, cot_ref[...])
    copy_edges.wait()
    copy_w.wait()
    pre_ref[...] = dot(x_ref[:, D:], w_ref[D:, :]) + bias_ref[...]

    to_row = lax.broadcasted_iota(jnp.int32, (TABLE, TABLE), 0)
    from_row = lax.broadcasted_iota(jnp.int32, (TABLE, TABLE), 1)
    width = PLANE * 2
    source = ((to_row % width) // 2) * (Z * 2) + (to_row // width) * 2 + to_row % 2
    regroup = (source == from_row).astype(BF16)

    arrived(fwd1.at[pl.ds(0, PLANE - 1)], FWD_PLANE)
    fwd2[...] = dot(regroup, fwd1[...].reshape(TABLE, D)).astype(BF16).reshape(Z, width, D)
    each_line(lambda peer, to: remote(fwd2.at[peer], table.at[z], FWD_LINE, to, y).start())
    table[z] = fwd2[z]

    senders = send_ref[...]
    own_hot = one_hot_rows(NODE, senders).astype(BF16)
    table_hot = one_hot_rows(TABLE, senders - NODE).astype(BF16)
    own_rows = contract_rows(own_hot, nodes)

    arrived(table.at[pl.ds(0, Z - 1)], FWD_LINE)
    x_ref[:, 0:D] = (own_rows + contract_rows(table_hot, table[...].reshape(TABLE, D))).astype(BF16)
    pre_ref[...] += dot(x_ref[:, 0:D], w_ref[0:D, :])

    gain = gain_ref[...]
    bias_term = jnp.zeros((1, D), F32)
    gain_term = jnp.zeros((1, D), F32)
    chunk = min(64, EDGE)
    for start in range(0, EDGE, chunk):
        rows = slice(start, start + chunk)
        preact = pre_ref[rows, :]
        upstream = up_ref[rows, :]
        sigmoid = jax.nn.sigmoid(preact)
        activated = preact * sigmoid
        average = jnp.mean(activated, axis=1, keepdims=True)
        centred = activated - average
        variance = jnp.mean(centred * centred, axis=1, keepdims=True)
        inverse = lax.rsqrt(variance + epsilon)
        normed = centred * inverse
        ne_ref[rows, :] = (x_ref[rows, 2 * D :].astype(F32) + normed * gain).astype(BF16)
        gain_term += jnp.sum(upstream * normed, axis=0, keepdims=True)
        normed_grad = upstream * gain
        activated_grad = inverse * (
            normed_grad
            - jnp.mean(normed_grad, axis=1, keepdims=True)
            - normed * jnp.mean(normed_grad * normed, axis=1, keepdims=True)
        )
        preact_grad = (activated_grad * sigmoid * (1.0 + preact * (1.0 - sigmoid))).astype(BF16)
        p_ref[rows, :] = preact_grad
        bias_term += jnp.sum(preact_grad.astype(F32), axis=0, keepdims=True)

    grad = p_ref[...]
    bwd0[...] = dot(table_hot, grad).astype(BF16).reshape(Z, width, D)
    each_line(lambda peer, to: remote(bwd0.at[peer], bwd1.at[z], BWD_LINE, to, y).start())
    bwd1[z] = bwd0[z]

    partner = z * PLANE + x * CORES + (1 - core)

    def pair_copy(j):
        return remote(wb.at[j, 1 - core], pair_in.at[j], PAIR + j, partner, y)

    group = X * HALF * CORES
    for j in range(JJ):
        term = contract_rows(x_ref[:, j * group : (j + 1) * group], grad).astype(BF16)
        term = term.reshape(X, CORES, HALF, D)
        for c in range(CORES):
            wb[j, c] = term[:, c]
        pair_copy(j).start()

    tiles = D // LANES
    for i in range(tiles):
        cols = slice(i * LANES, (i + 1) * LANES)
        bg0[i : i + 1, :] = bias_term[:, cols]
        bg0[tiles + i : tiles + i + 1, :] = gain_term[:, cols]
    each_plane(lambda peer, to: remote(bg0, bg1_in.at[plane], SUM_PLANE, to, y).start())
    bg1_in[plane] = bg0[...]

    for j in range(JA):
        pair_copy(j).wait_recv()
        both = (wb[j, core].astype(F32) + pair_in[j].astype(F32)).astype(BF16)
        for to in range(Y):
            a1[to, j] = both[:, :, to * (D // Y) : (to + 1) * (D // Y)]
    each_y(lambda peer: remote(a1.at[peer], a1_in.at[y], FIRST_A, dom, peer).start())
    a1_in[y] = a1[y]
    for j in range(JA, JJ):
        pair_copy(j).wait_recv()
        both = (wb[j, core].astype(F32) + pair_in[j].astype(F32)).astype(BF16)
        for to in range(X):
            b1[to, j - JA] = both[to]
    each_x(lambda peer, to: remote(b1.at[peer], b1_in.at[x], FIRST_B, to, y).start())
    b1_in[x] = b1[x]

    ge_ref[...] = (up_ref[...] + apply_transpose(grad, w_ref[2 * D :, :])).astype(BF16)
    copy_ge = pltpu.make_async_copy(ge_ref, grad_edges_hbm, local_sem.at[2])
    copy_ge.start()
    new_nodes_ref[...] = (nodes.astype(F32) + dot(incidence, ne_ref[...])).astype(BF16)

    arrived(bg1_in.at[pl.ds(0, PLANE - 1)], SUM_PLANE)
    bg1[...] = total(bg1_in, PLANE)
    each_y(lambda peer: remote(bg1, bg2_in.at[y], SUM_Y, dom, peer).start())
    bg2_in[y] = bg1[...]

    arrived(a1_in.at[pl.ds(0, Y - 1)], FIRST_A)
    summed = total(a1_in, Y).astype(BF16)
    for to in range(X):
        a2[to] = summed[:, to]
    each_x(lambda peer, to: remote(a2.at[peer], a2_in.at[x], SECOND_A, to, y).start())
    a2_in[x] = a2[x]
    arrived(b1_in.at[pl.ds(0, X - 1)], FIRST_B)
    summed = total(b1_in, X).astype(BF16)
    for to in range(Y):
        b2[to] = summed[:, :, to * (D // Y) : (to + 1) * (D // Y)]
    each_y(lambda peer: remote(b2.at[peer], b2_in.at[y], SECOND_B, dom, peer).start())
    b2_in[y] = b2[y]

    arrived(bg2_in.at[pl.ds(0, Y - 1)], SUM_Y)
    bg2[...] = total(bg2_in, Y)
    each_line(lambda peer, to: remote(bg2, bg_in.at[z], SUM_LINE, to, y).start())
    bg_in[z] = bg2[...]

    node_live = lax.broadcasted_iota(jnp.int32, (NODE, D), 0) < node_count_ref[0]
    node_grad = jnp.where(node_live, cot_ref[...].astype(F32), 0.0)
    node_grad += split_transpose(dot(incidence, grad), w_ref[D : 2 * D, :])
    own_sum = dot(own_hot, grad)

    arrived(a2_in.at[pl.ds(0, X - 1)], SECOND_A)
    zw[0:JA] = total(a2_in, X).astype(BF16)
    arrived(b2_in.at[pl.ds(0, Y - 1)], SECOND_B)
    zw[JA:JJ] = total(b2_in, Y).astype(BF16)

    def line_copy(j):
        return remote(zw.at[j], zw_in.at[z], LINE_W, (j * X + x) * PLANE + plane, y)

    def line_start(j, carry):
        @pl.when(j * X + x != z)
        def _():
            line_copy(j).start()

        return carry

    lax.fori_loop(0, JJ, line_start, 0)

    arrived(bwd1.at[pl.ds(0, Z - 1)], BWD_LINE)
    bwd2[...] = (
        contract_rows(regroup, bwd1[...].reshape(TABLE, D)).astype(BF16).reshape(PLANE, Z * 2, D)
    )
    each_plane(lambda peer, to: remote(bwd2.at[peer], back.at[plane], BWD_PLANE, to, y).start())
    back[plane] = bwd2[plane]

    owner = lax.rem(z, X) == x

    def final_copy(piece):
        return remote(
            fin.at[piece], fin_in, FINAL_PLANE, z * PLANE + core * PIECES + piece, y
        )

    @pl.when(owner)
    def _():
        zw_in[z] = zw[z // X]
        arrived(zw_in.at[pl.ds(0, Z - 1)], LINE_W)
        rows = total(zw_in, Z)
        fin[...] = jnp.zeros_like(fin)
        for piece in range(PIECES):
            fin[piece, 0:OWN, :] = rows[piece * OWN : (piece + 1) * OWN, :]
        for piece in range(PIECES):

            @pl.when(core * PIECES + piece != plane)
            def _():
                final_copy(piece).start()

            @pl.when(core * PIECES + piece == plane)
            def _():
                fin_in[0:OWN, :] = fin[piece, 0:OWN, :]

    arrived(back.at[pl.ds(0, PLANE - 1)], BWD_PLANE)
    own_sum += dot(out_hot, back[...].reshape(TABLE, D))
    grad_nodes_ref[...] = (node_grad + split_transpose(own_sum, w_ref[0:D, :])).astype(BF16)

    arrived(bg_in.at[pl.ds(0, Z - 1)], SUM_LINE)
    terms = total(bg_in, Z)
    for i in range(tiles):
        cols = slice(i * LANES, (i + 1) * LANES)
        gb_ref[:, cols] = terms[i : i + 1, :]
        gg_ref[:, cols] = terms[tiles + i : tiles + i + 1, :]

    @pl.when(lax.rem(z, X) * CORES + plane // PIECES != plane)
    def _():
        arrived(fin_in, FINAL_PLANE)

    each_y(lambda peer: remote(fin_in, fin_y.at[y], FINAL_Y, dom, peer).start())
    fin_y[y] = fin_in[...]
    arrived(fin_y.at[pl.ds(0, Y - 1)], FINAL_Y)
    for i in range(Y):
        gw_ref[:, i * (D // Y) : (i + 1) * (D // Y)] = fin_y[i, 0:OWN, :]

    sent(outb.at[pl.ds(0, PLANE - 1)], FWD_PLANE)
    sent(fwd2.at[pl.ds(0, Z - 1)], FWD_LINE)
    sent(bwd0.at[pl.ds(0, Z - 1)], BWD_LINE)
    sent(bwd2.at[pl.ds(0, PLANE - 1)], BWD_PLANE)
    for j in range(JJ):
        pair_copy(j).wait_send()
    sent(a1.at[pl.ds(0, Y - 1)], FIRST_A)
    sent(b1.at[pl.ds(0, X - 1)], FIRST_B)
    sent(a2.at[pl.ds(0, X - 1)], SECOND_A)
    sent(b2.at[pl.ds(0, Y - 1)], SECOND_B)
    sent(bg1_in.at[pl.ds(0, PLANE - 1)], SUM_PLANE)
    sent(bg2_in.at[pl.ds(0, Y - 1)], SUM_Y)
    sent(bg_in.at[pl.ds(0, Z - 1)], SUM_LINE)
    sent(fin_y.at[pl.ds(0, Y - 1)], FINAL_Y)

    def line_done(j, carry):
        @pl.when(j * X + x != z)
        def _():
            line_copy(j).wait_send()

        return carry

    lax.fori_loop(0, JJ, line_done, 0)

    @pl.when(owner)
    def _():
        for piece in range(PIECES):

            @pl.when(core * PIECES + piece != plane)
            def _():
                final_copy(piece).wait_send()

    copy_ge.wait()


def shards(
    Z,
    X,
    Y,
    node_latents,
    edge_latents,
    node_cotangent,
    w_in,
    bias,
    gain,
    receivers,
    senders,
    send_rows,
    node_count,
    edge_count,
):
    _, NODE, D = node_latents.shape
    EDGE = edge_latents.shape[1]
    PLANE = X * CORES
    TABLE = Z * PLANE * 2
    JJ = Z // X
    JA = JJ // 2
    JB = JJ - JA
    HALF = 3 * D // Z // CORES
    PIECES = PLANE // CORES
    OWN = HALF // PIECES
    OWN_PAD = (OWN + 15) // 16 * 16
    COLS = D // Y
    SUMS = 2 * D // LANES
    outgoing = send_rows[0].reshape(Z, PLANE, 2).transpose(1, 0, 2).reshape(1, TABLE)

    vmem = pl.BlockSpec(memory_space=pltpu.VMEM)
    anywhere = pl.BlockSpec(memory_space=pl.ANY)
    smem = pl.BlockSpec(memory_space=pltpu.SMEM)
    scratch = [
        pltpu.VMEM((3 * D, D), BF16),
        pltpu.VMEM((EDGE, 3 * D), BF16),
        pltpu.VMEM((EDGE, D), F32),
        pltpu.VMEM((EDGE, D), F32),
        pltpu.VMEM((EDGE, D), BF16),
        pltpu.VMEM((EDGE, D), BF16),
        pltpu.VMEM((EDGE, D), BF16),
        pltpu.VMEM((PLANE, Z * 2, D), BF16),
        pltpu.VMEM((PLANE, Z * 2, D), BF16),
        pltpu.VMEM((Z, PLANE * 2, D), BF16),
        pltpu.VMEM((Z, PLANE * 2, D), BF16),
        pltpu.VMEM((Z, PLANE * 2, D), BF16),
        pltpu.VMEM((Z, PLANE * 2, D), BF16),
        pltpu.VMEM((PLANE, Z * 2, D), BF16),
        pltpu.VMEM((PLANE, Z * 2, D), BF16),
        pltpu.VMEM((JJ, CORES, X, HALF, D), BF16),
        pltpu.VMEM((JJ, X, HALF, D), BF16),
        pltpu.VMEM((Y, JA, X, HALF, COLS), BF16),
        pltpu.VMEM((Y, JA, X, HALF, COLS), BF16),
        pltpu.VMEM((X, JB, HALF, D), BF16),
        pltpu.VMEM((X, JB, HALF, D), BF16),
        pltpu.VMEM((X, JA, HALF, COLS), BF16),
        pltpu.VMEM((X, JA, HALF, COLS), BF16),
        pltpu.VMEM((Y, JB, HALF, COLS), BF16),
        pltpu.VMEM((Y, JB, HALF, COLS), BF16),
        pltpu.VMEM((JJ, HALF, COLS), BF16),
        pltpu.VMEM((Z, HALF, COLS), BF16),
        pltpu.VMEM((PIECES, OWN_PAD, COLS), F32),
        pltpu.VMEM((OWN_PAD, COLS), F32),
        pltpu.VMEM((Y, OWN_PAD, COLS), F32),
        pltpu.VMEM((SUMS, LANES), F32),
        pltpu.VMEM((SUMS, LANES), F32),
        pltpu.VMEM((PLANE, SUMS, LANES), F32),
        pltpu.VMEM((SUMS, LANES), F32),
        pltpu.VMEM((Y, SUMS, LANES), F32),
        pltpu.VMEM((Z, SUMS, LANES), F32),
        pltpu.SemaphoreType.DMA((3,)),
        pltpu.SemaphoreType.DMA((PAIR + JJ,)),
        pltpu.SemaphoreType.DMA((PAIR + JJ,)),
    ]
    new_nodes, grad_nodes, grad_weights, grad_bias, grad_gain, grad_edges = pl.pallas_call(
        functools.partial(kernel, (Z, X, Y, D, NODE, EDGE)),
        out_shape=(
            jax.ShapeDtypeStruct((NODE, D), BF16),
            jax.ShapeDtypeStruct((NODE, D), BF16),
            jax.ShapeDtypeStruct((OWN, D), F32),
            jax.ShapeDtypeStruct((1, D), F32),
            jax.ShapeDtypeStruct((1, D), F32),
            jax.ShapeDtypeStruct((EDGE, D), BF16),
        ),
        in_specs=[vmem] * 7 + [anywhere] * 2 + [smem] * 2,
        out_specs=(vmem,) * 5 + (anywhere,),
        scratch_shapes=scratch,
        compiler_params=pltpu.CompilerParams(
            collective_id=0, has_side_effects=True, vmem_limit_bytes=48 * 1024 * 1024
        ),
        name="edge_update",
    )(
        node_latents[0],
        node_cotangent[0],
        bias.reshape(1, D),
        gain.reshape(1, D),
        receivers.reshape(1, EDGE),
        senders.reshape(1, EDGE),
        outgoing,
        edge_latents[0],
        w_in,
        node_count,
        edge_count,
    )
    return (
        new_nodes[None],
        grad_nodes[None],
        grad_edges[None],
        grad_weights,
        grad_bias.reshape(D),
        grad_gain.reshape(D),
    )


def solution(mesh, x_chips=4):
    Y = mesh.shape["member"]
    Z = mesh.shape["dom"] // (x_chips * CORES)
    return jax.shard_map(
        functools.partial(shards, Z, x_chips, Y),
        mesh=mesh,
        in_specs=(
            P("member", "dom", None),
            P("member", "dom", None),
            P("member", "dom", None),
            P(),
            P(),
            P(),
            P("dom"),
            P("dom"),
            P("dom", None, None),
            P("dom"),
            P("dom"),
        ),
        out_specs=(
            P("member", "dom", None),
            P("member", "dom", None),
            P("member", "dom", None),
            P("dom", None),
            P(),
            P(),
        ),
        check_vma=False,
    )
```

```python
import functools

import jax
import jax.numpy as jnp
from jax import lax
from jax.experimental import pallas as pl
from jax.experimental.pallas import tpu as pltpu
from jax.sharding import PartitionSpec as P

epsilon = 1e-05
CORES = 2
LANES = 128
VMEM_BYTES = 63 * 1024 * 1024
F32 = jnp.float32
BF16 = jnp.bfloat16

FWD_PLANE, FWD_LINE, BWD_LINE, BWD_PLANE, FIRST_A, FIRST_B, SECOND_A, SECOND_B, LINE_W, FINAL_PLANE, FINAL_Y = range(11)
SUM_PLANE, SUM_Y, SUM_LINE = range(11, 14)
PAIR = 14


def dot(left, right):
    return jnp.dot(left, right, preferred_element_type=F32)


def contract_rows(left, right):
    return lax.dot_general(left, right, (((0,), (0,)), ((), ())), preferred_element_type=F32)


def apply_transpose(left, right):
    return lax.dot_general(left, right, (((1,), (1,)), ((), ())), preferred_element_type=F32)


def one_hot_rows(rows, index):
    return lax.broadcasted_iota(jnp.int32, (rows, index.shape[1]), 0) == index


def total(ref, count):
    acc = ref[0].astype(F32)
    for slot in range(1, count):
        acc = acc + ref[slot].astype(F32)
    return acc


def split_transpose(rows, weights):
    high = rows.astype(BF16)
    low = (rows - high.astype(F32)).astype(BF16)
    return apply_transpose(high, weights) + apply_transpose(low, weights)


def kernel(
    sizes,
    nodes_hbm,
    outgoing_hbm,
    edges_hbm,
    w_hbm,
    bias_hbm,
    recv_hbm,
    cot_hbm,
    send_hbm,
    gain_hbm,
    node_count_ref,
    edge_count_ref,
    new_nodes_hbm,
    grad_nodes_hbm,
    grad_edges_hbm,
    gw_hbm,
    gb_hbm,
    gg_hbm,
    nodes_ref,
    outgoing_ref,
    bias_ref,
    recv_ref,
    cot_ref,
    send_ref,
    gain_ref,
    new_nodes_ref,
    grad_nodes_ref,
    gw_ref,
    gb_ref,
    gg_ref,
    w_ref,
    x_ref,
    pre_ref,
    up_ref,
    p_ref,
    ne_ref,
    ge_ref,
    outb,
    fwd1,
    fwd2,
    table,
    bwd0,
    bwd1,
    bwd2,
    back,
    wb,
    pair_in,
    a1,
    a1_in,
    b1,
    b1_in,
    a2,
    a2_in,
    b2,
    b2_in,
    zw,
    zw_in,
    fin,
    fin_in,
    fin_y,
    bg0,
    bg1,
    bg1_in,
    bg2,
    bg2_in,
    bg_in,
    local_sem,
    send_sem,
    recv_sem,
):
    Z, X, Y, D, NODE, EDGE = sizes
    PLANE = X * CORES
    TABLE = Z * PLANE * 2
    JJ = Z // X
    JA = JJ // 2
    HALF = 3 * D // Z // CORES
    PIECES = PLANE // CORES
    OWN = HALF // PIECES
    dom = lax.axis_index("dom")
    y = lax.axis_index("member")
    z = dom // PLANE
    plane = dom % PLANE
    x = plane // CORES
    core = plane % CORES

    def remote(src, dst, step, to_dom, to_y):
        return pltpu.make_async_remote_copy(
            src_ref=src,
            dst_ref=dst,
            send_sem=send_sem.at[step],
            recv_sem=recv_sem.at[step],
            device_id={"dom": to_dom, "member": to_y},
            device_id_type=pl.DeviceIdType.MESH,
        )

    def arrived(ref, step):
        pltpu.make_async_copy(ref, ref, recv_sem.at[step]).wait()

    def sent(ref, step):
        pltpu.make_async_copy(ref, ref, send_sem.at[step]).wait()

    def each_plane(act):
        def body(i, carry):
            peer = lax.rem(plane + PLANE // 2 + jnp.where(i < PLANE // 2, i, i + 1), PLANE)
            act(peer, z * PLANE + peer)
            return carry

        lax.fori_loop(0, PLANE - 1, body, 0)

    def each_line(act):
        def body(i, carry):
            off = Z // 2 + (1 - 2 * lax.rem(i, 2)) * ((i + 1) // 2)
            peer = lax.rem(z + off, Z)
            act(peer, peer * PLANE + plane)
            return carry

        lax.fori_loop(0, Z - 1, body, 0)

    def each_x(act):
        def body(i, carry):
            peer = lax.rem(x + 1 + i, X)
            act(peer, z * PLANE + peer * CORES + core)
            return carry

        lax.fori_loop(0, X - 1, body, 0)

    def each_y(act):
        def body(i, carry):
            act(lax.rem(y + 1 + i, Y))
            return carry

        lax.fori_loop(0, Y - 1, body, 0)

    loads = [
        pltpu.make_async_copy(src, dst, local_sem.at[i])
        for i, (src, dst) in enumerate(
            (
                (nodes_hbm, nodes_ref),
                (outgoing_hbm, outgoing_ref),
                (recv_hbm, recv_ref),
                (cot_hbm, cot_ref),
                (edges_hbm, x_ref.at[:, pl.ds(2 * D, D)]),
                (w_hbm.at[pl.ds(D, 2 * D)], w_ref.at[pl.ds(D, 2 * D)]),
                (bias_hbm, bias_ref),
                (send_hbm, send_ref),
                (gain_hbm, gain_ref),
                (w_hbm.at[pl.ds(0, D)], w_ref.at[pl.ds(0, D)]),
            )
        )
    ]
    stores = [
        pltpu.make_async_copy(src, dst, local_sem.at[len(loads) + i])
        for i, (src, dst) in enumerate(
            (
                (ge_ref, grad_edges_hbm),
                (new_nodes_ref, new_nodes_hbm),
                (grad_nodes_ref, grad_nodes_hbm),
                (gb_ref, gb_hbm),
                (gg_ref, gg_hbm),
                (gw_ref, gw_hbm),
            )
        )
    ]
    pending = []

    def finish():
        for wait in pending:
            wait()

    def store(i):
        stores[i].start()
        pending.append(stores[i].wait)

    for load in loads[:2]:
        load.start()

    barrier = pltpu.get_barrier_semaphore()

    def greet(to_dom, to_y):
        pl.semaphore_signal(
            barrier,
            inc=1,
            device_id={"dom": to_dom, "member": to_y},
            device_id_type=pl.DeviceIdType.MESH,
        )

    each_plane(lambda peer, to: greet(to, y))
    each_line(lambda peer, to: greet(to, y))
    each_y(lambda peer: greet(dom, peer))

    for load in loads[2:]:
        load.start()

    parts = Z * PLANE
    given = lax.broadcasted_iota(jnp.int32, (TABLE, TABLE), 0)
    placed = lax.broadcasted_iota(jnp.int32, (TABLE, TABLE), 1)
    wanted = (placed % 2) * parts + (placed // 2 % Z) * PLANE + placed // (2 * Z)
    reorder = (given == wanted).astype(BF16)
    for load in loads[:2]:
        load.wait()
    nodes = nodes_ref[...]
    outgoing = outgoing_ref[...]
    out_hot = jnp.concatenate([one_hot_rows(NODE, outgoing[k : k + 1]) for k in range(2)], axis=1)
    out_hot = dot(out_hot.astype(BF16), reorder).astype(BF16)
    outb[...] = contract_rows(out_hot, nodes).astype(BF16).reshape(PLANE, Z * 2, D)

    pl.semaphore_wait(barrier, (PLANE - 1) + (Z - 1) + (Y - 1))

    each_plane(lambda peer, to: remote(outb.at[peer], fwd1.at[plane], FWD_PLANE, to, y).start())
    pending.append(lambda: sent(outb.at[pl.ds(0, PLANE - 1)], FWD_PLANE))
    fwd1[plane] = outb[plane]

    live = lax.broadcasted_iota(jnp.int32, (NODE, EDGE), 1) < edge_count_ref[0]
    for load in loads[2:]:
        load.wait()
    incidence = (one_hot_rows(NODE, recv_ref[...]) & live).astype(BF16)
    x_ref[:, D : 2 * D] = contract_rows(incidence, nodes).astype(BF16)
    up_ref[...] = contract_rows(incidence, cot_ref[...])
    pre_ref[...] = dot(x_ref[:, D:], w_ref[D:, :]) + bias_ref[...]

    to_row = lax.broadcasted_iota(jnp.int32, (TABLE, TABLE), 0)
    from_row = lax.broadcasted_iota(jnp.int32, (TABLE, TABLE), 1)
    width = PLANE * 2
    source = ((to_row % width) // 2) * (Z * 2) + (to_row // width) * 2 + to_row % 2
    regroup = (source == from_row).astype(BF16)

    arrived(fwd1.at[pl.ds(0, PLANE - 1)], FWD_PLANE)
    fwd2[...] = dot(regroup, fwd1[...].reshape(TABLE, D)).astype(BF16).reshape(Z, width, D)
    each_line(lambda peer, to: remote(fwd2.at[peer], table.at[z], FWD_LINE, to, y).start())
    pending.append(lambda: sent(fwd2.at[pl.ds(0, Z - 1)], FWD_LINE))
    table[z] = fwd2[z]

    senders = send_ref[...]
    own_hot = one_hot_rows(NODE, senders).astype(BF16)
    table_hot = one_hot_rows(TABLE, senders - NODE).astype(BF16)
    own_rows = contract_rows(own_hot, nodes)

    arrived(table.at[pl.ds(0, Z - 1)], FWD_LINE)
    x_ref[:, 0:D] = (own_rows + contract_rows(table_hot, table[...].reshape(TABLE, D))).astype(BF16)
    pre_ref[...] += dot(x_ref[:, 0:D], w_ref[0:D, :])

    gain = gain_ref[...]
    bias_term = jnp.zeros((1, D), F32)
    gain_term = jnp.zeros((1, D), F32)
    chunk = min(64, EDGE)
    for start in range(0, EDGE, chunk):
        rows = slice(start, start + chunk)
        preact = pre_ref[rows, :]
        upstream = up_ref[rows, :]
        sigmoid = jax.nn.sigmoid(preact)
        activated = preact * sigmoid
        average = jnp.mean(activated, axis=1, keepdims=True)
        centred = activated - average
        variance = jnp.mean(centred * centred, axis=1, keepdims=True)
        inverse = lax.rsqrt(variance + epsilon)
        normed = centred * inverse
        ne_ref[rows, :] = (x_ref[rows, 2 * D :].astype(F32) + normed * gain).astype(BF16)
        gain_term += jnp.sum(upstream * normed, axis=0, keepdims=True)
        normed_grad = upstream * gain
        activated_grad = inverse * (
            normed_grad
            - jnp.mean(normed_grad, axis=1, keepdims=True)
            - normed * jnp.mean(normed_grad * normed, axis=1, keepdims=True)
        )
        preact_grad = (activated_grad * sigmoid * (1.0 + preact * (1.0 - sigmoid))).astype(BF16)
        p_ref[rows, :] = preact_grad
        bias_term += jnp.sum(preact_grad.astype(F32), axis=0, keepdims=True)

    grad = p_ref[...]
    bwd0[...] = dot(table_hot, grad).astype(BF16).reshape(Z, width, D)
    each_line(lambda peer, to: remote(bwd0.at[peer], bwd1.at[z], BWD_LINE, to, y).start())
    pending.append(lambda: sent(bwd0.at[pl.ds(0, Z - 1)], BWD_LINE))
    bwd1[z] = bwd0[z]

    partner = z * PLANE + x * CORES + (1 - core)

    def pair_copy(j):
        return remote(wb.at[j, 1 - core], pair_in.at[j], PAIR + j, partner, y)

    group = X * HALF * CORES
    for j in range(JJ):
        term = contract_rows(x_ref[:, j * group : (j + 1) * group], grad).astype(BF16)
        term = term.reshape(X, CORES, HALF, D)
        for c in range(CORES):
            wb[j, c] = term[:, c]
        pair_copy(j).start()
        pending.append(pair_copy(j).wait_send)

    tiles = D // LANES
    for i in range(tiles):
        cols = slice(i * LANES, (i + 1) * LANES)
        bg0[i : i + 1, :] = bias_term[:, cols]
        bg0[tiles + i : tiles + i + 1, :] = gain_term[:, cols]
    each_plane(lambda peer, to: remote(bg0, bg1_in.at[plane], SUM_PLANE, to, y).start())
    pending.append(lambda: sent(bg1_in.at[pl.ds(0, PLANE - 1)], SUM_PLANE))
    bg1_in[plane] = bg0[...]

    for j in range(JA):
        pair_copy(j).wait_recv()
        both = (wb[j, core].astype(F32) + pair_in[j].astype(F32)).astype(BF16)
        for to in range(Y):
            a1[to, j] = both[:, :, to * (D // Y) : (to + 1) * (D // Y)]
    each_y(lambda peer: remote(a1.at[peer], a1_in.at[y], FIRST_A, dom, peer).start())
    pending.append(lambda: sent(a1.at[pl.ds(0, Y - 1)], FIRST_A))
    a1_in[y] = a1[y]
    for j in range(JA, JJ):
        pair_copy(j).wait_recv()
        both = (wb[j, core].astype(F32) + pair_in[j].astype(F32)).astype(BF16)
        for to in range(X):
            b1[to, j - JA] = both[to]
    each_x(lambda peer, to: remote(b1.at[peer], b1_in.at[x], FIRST_B, to, y).start())
    pending.append(lambda: sent(b1.at[pl.ds(0, X - 1)], FIRST_B))
    b1_in[x] = b1[x]

    ge_ref[...] = (up_ref[...] + apply_transpose(grad, w_ref[2 * D :, :])).astype(BF16)
    store(0)
    new_nodes_ref[...] = (nodes.astype(F32) + dot(incidence, ne_ref[...])).astype(BF16)
    store(1)

    arrived(bg1_in.at[pl.ds(0, PLANE - 1)], SUM_PLANE)
    bg1[...] = total(bg1_in, PLANE)
    each_y(lambda peer: remote(bg1, bg2_in.at[y], SUM_Y, dom, peer).start())
    pending.append(lambda: sent(bg2_in.at[pl.ds(0, Y - 1)], SUM_Y))
    bg2_in[y] = bg1[...]

    arrived(a1_in.at[pl.ds(0, Y - 1)], FIRST_A)
    summed = total(a1_in, Y).astype(BF16)
    for to in range(X):
        a2[to] = summed[:, to]
    each_x(lambda peer, to: remote(a2.at[peer], a2_in.at[x], SECOND_A, to, y).start())
    pending.append(lambda: sent(a2.at[pl.ds(0, X - 1)], SECOND_A))
    a2_in[x] = a2[x]
    arrived(b1_in.at[pl.ds(0, X - 1)], FIRST_B)
    summed = total(b1_in, X).astype(BF16)
    for to in range(Y):
        b2[to] = summed[:, :, to * (D // Y) : (to + 1) * (D // Y)]
    each_y(lambda peer: remote(b2.at[peer], b2_in.at[y], SECOND_B, dom, peer).start())
    pending.append(lambda: sent(b2.at[pl.ds(0, Y - 1)], SECOND_B))
    b2_in[y] = b2[y]

    arrived(bg2_in.at[pl.ds(0, Y - 1)], SUM_Y)
    bg2[...] = total(bg2_in, Y)
    each_line(lambda peer, to: remote(bg2, bg_in.at[z], SUM_LINE, to, y).start())
    pending.append(lambda: sent(bg_in.at[pl.ds(0, Z - 1)], SUM_LINE))
    bg_in[z] = bg2[...]

    node_live = lax.broadcasted_iota(jnp.int32, (NODE, D), 0) < node_count_ref[0]
    node_grad = jnp.where(node_live, cot_ref[...].astype(F32), 0.0)
    node_grad += split_transpose(dot(incidence, grad), w_ref[D : 2 * D, :])
    own_sum = dot(own_hot, grad)

    arrived(a2_in.at[pl.ds(0, X - 1)], SECOND_A)
    zw[0:JA] = total(a2_in, X).astype(BF16)
    arrived(b2_in.at[pl.ds(0, Y - 1)], SECOND_B)
    zw[JA:JJ] = total(b2_in, Y).astype(BF16)

    def line_copy(j):
        return remote(zw.at[j], zw_in.at[z], LINE_W, (j * X + x) * PLANE + plane, y)

    def line_start(j, carry):
        @pl.when(j * X + x != z)
        def _():
            line_copy(j).start()

        return carry

    lax.fori_loop(0, JJ, line_start, 0)

    def line_done(j, carry):
        @pl.when(j * X + x != z)
        def _():
            line_copy(j).wait_send()

        return carry

    pending.append(lambda: lax.fori_loop(0, JJ, line_done, 0))

    arrived(bwd1.at[pl.ds(0, Z - 1)], BWD_LINE)
    bwd2[...] = (
        contract_rows(regroup, bwd1[...].reshape(TABLE, D)).astype(BF16).reshape(PLANE, Z * 2, D)
    )
    each_plane(lambda peer, to: remote(bwd2.at[peer], back.at[plane], BWD_PLANE, to, y).start())
    pending.append(lambda: sent(bwd2.at[pl.ds(0, PLANE - 1)], BWD_PLANE))
    back[plane] = bwd2[plane]

    owner = lax.rem(z, X) == x

    def final_copy(piece):
        return remote(
            fin.at[piece], fin_in, FINAL_PLANE, z * PLANE + core * PIECES + piece, y
        )

    @pl.when(owner)
    def _():
        zw_in[z] = zw[z // X]
        arrived(zw_in.at[pl.ds(0, Z - 1)], LINE_W)
        rows = total(zw_in, Z)
        fin[...] = jnp.zeros_like(fin)
        for piece in range(PIECES):
            fin[piece, 0:OWN, :] = rows[piece * OWN : (piece + 1) * OWN, :]
        for piece in range(PIECES):

            @pl.when(core * PIECES + piece != plane)
            def _():
                final_copy(piece).start()

            @pl.when(core * PIECES + piece == plane)
            def _():
                fin_in[0:OWN, :] = fin[piece, 0:OWN, :]

    arrived(back.at[pl.ds(0, PLANE - 1)], BWD_PLANE)
    own_sum += dot(out_hot, back[...].reshape(TABLE, D))
    grad_nodes_ref[...] = (node_grad + split_transpose(own_sum, w_ref[0:D, :])).astype(BF16)
    store(2)

    arrived(bg_in.at[pl.ds(0, Z - 1)], SUM_LINE)
    terms = total(bg_in, Z)
    for i in range(tiles):
        cols = slice(i * LANES, (i + 1) * LANES)
        gb_ref[:, cols] = terms[i : i + 1, :]
        gg_ref[:, cols] = terms[tiles + i : tiles + i + 1, :]
    store(3)
    store(4)

    @pl.when(lax.rem(z, X) * CORES + plane // PIECES != plane)
    def _():
        arrived(fin_in, FINAL_PLANE)

    each_y(lambda peer: remote(fin_in, fin_y.at[y], FINAL_Y, dom, peer).start())
    pending.append(lambda: sent(fin_y.at[pl.ds(0, Y - 1)], FINAL_Y))
    fin_y[y] = fin_in[...]
    arrived(fin_y.at[pl.ds(0, Y - 1)], FINAL_Y)
    for i in range(Y):
        gw_ref[:, i * (D // Y) : (i + 1) * (D // Y)] = fin_y[i, 0:OWN, :]

    store(5)

    def final_done():
        @pl.when(owner)
        def _():
            for piece in range(PIECES):

                @pl.when(core * PIECES + piece != plane)
                def _():
                    final_copy(piece).wait_send()

    pending.append(final_done)
    finish()


def copy_out(*refs):
    count = len(refs) // 2
    sems = refs[-1]
    copies = [
        pltpu.make_async_copy(refs[i], refs[count + i], sems.at[i]) for i in range(count)
    ]
    for copy in copies:
        copy.start()
    for copy in copies:
        copy.wait()


def shards(
    Z,
    X,
    Y,
    node_latents,
    edge_latents,
    node_cotangent,
    w_in,
    bias,
    gain,
    receivers,
    senders,
    send_rows,
    node_count,
    edge_count,
):
    _, NODE, D = node_latents.shape
    EDGE = edge_latents.shape[1]
    PLANE = X * CORES
    TABLE = Z * PLANE * 2
    JJ = Z // X
    JA = JJ // 2
    JB = JJ - JA
    HALF = 3 * D // Z // CORES
    PIECES = PLANE // CORES
    OWN = HALF // PIECES
    OWN_PAD = (OWN + 15) // 16 * 16
    COLS = D // Y
    SUMS = 2 * D // LANES
    outgoing = send_rows[0].T

    anywhere = pl.BlockSpec(memory_space=pl.ANY)
    smem = pl.BlockSpec(memory_space=pltpu.SMEM)
    scratch = [
        pltpu.VMEM((NODE, D), BF16),
        pltpu.VMEM((2, Z * PLANE), jnp.int32),
        pltpu.VMEM((1, D), F32),
        pltpu.VMEM((1, EDGE), jnp.int32),
        pltpu.VMEM((NODE, D), BF16),
        pltpu.VMEM((1, EDGE), jnp.int32),
        pltpu.VMEM((1, D), F32),
        pltpu.VMEM((NODE, D), BF16),
        pltpu.VMEM((NODE, D), BF16),
        pltpu.VMEM((OWN, D), F32),
        pltpu.VMEM((1, D), F32),
        pltpu.VMEM((1, D), F32),
        pltpu.VMEM((3 * D, D), BF16),
        pltpu.VMEM((EDGE, 3 * D), BF16),
        pltpu.VMEM((EDGE, D), F32),
        pltpu.VMEM((EDGE, D), F32),
        pltpu.VMEM((EDGE, D), BF16),
        pltpu.VMEM((EDGE, D), BF16),
        pltpu.VMEM((EDGE, D), BF16),
        pltpu.VMEM((PLANE, Z * 2, D), BF16),
        pltpu.VMEM((PLANE, Z * 2, D), BF16),
        pltpu.VMEM((Z, PLANE * 2, D), BF16),
        pltpu.VMEM((Z, PLANE * 2, D), BF16),
        pltpu.VMEM((Z, PLANE * 2, D), BF16),
        pltpu.VMEM((Z, PLANE * 2, D), BF16),
        pltpu.VMEM((PLANE, Z * 2, D), BF16),
        pltpu.VMEM((PLANE, Z * 2, D), BF16),
        pltpu.VMEM((JJ, CORES, X, HALF, D), BF16),
        pltpu.VMEM((JJ, X, HALF, D), BF16),
        pltpu.VMEM((Y, JA, X, HALF, COLS), BF16),
        pltpu.VMEM((Y, JA, X, HALF, COLS), BF16),
        pltpu.VMEM((X, JB, HALF, D), BF16),
        pltpu.VMEM((X, JB, HALF, D), BF16),
        pltpu.VMEM((X, JA, HALF, COLS), BF16),
        pltpu.VMEM((X, JA, HALF, COLS), BF16),
        pltpu.VMEM((Y, JB, HALF, COLS), BF16),
        pltpu.VMEM((Y, JB, HALF, COLS), BF16),
        pltpu.VMEM((JJ, HALF, COLS), BF16),
        pltpu.VMEM((Z, HALF, COLS), BF16),
        pltpu.VMEM((PIECES, OWN_PAD, COLS), F32),
        pltpu.VMEM((OWN_PAD, COLS), F32),
        pltpu.VMEM((Y, OWN_PAD, COLS), F32),
        pltpu.VMEM((SUMS, LANES), F32),
        pltpu.VMEM((SUMS, LANES), F32),
        pltpu.VMEM((PLANE, SUMS, LANES), F32),
        pltpu.VMEM((SUMS, LANES), F32),
        pltpu.VMEM((Y, SUMS, LANES), F32),
        pltpu.VMEM((Z, SUMS, LANES), F32),
        pltpu.SemaphoreType.DMA((16,)),
        pltpu.SemaphoreType.DMA((PAIR + JJ,)),
        pltpu.SemaphoreType.DMA((PAIR + JJ,)),
    ]
    shapes = (
        jax.ShapeDtypeStruct((NODE, D), BF16),
        jax.ShapeDtypeStruct((NODE, D), BF16),
        jax.ShapeDtypeStruct((EDGE, D), BF16),
        jax.ShapeDtypeStruct((OWN, D), F32),
        jax.ShapeDtypeStruct((1, D), F32),
        jax.ShapeDtypeStruct((1, D), F32),
    )
    results = pl.pallas_call(
        functools.partial(kernel, (Z, X, Y, D, NODE, EDGE)),
        out_shape=shapes,
        in_specs=[anywhere] * 9 + [smem] * 2,
        out_specs=(anywhere,) * 6,
        scratch_shapes=scratch,
        compiler_params=pltpu.CompilerParams(
            collective_id=0, has_side_effects=True, vmem_limit_bytes=VMEM_BYTES
        ),
        name="edge_update",
    )(
        node_latents[0],
        outgoing,
        edge_latents[0],
        w_in,
        bias.reshape(1, D),
        receivers.reshape(1, EDGE),
        node_cotangent[0],
        senders.reshape(1, EDGE),
        gain.reshape(1, D),
        node_count,
        edge_count,
    )
    new_nodes, grad_nodes, grad_edges, grad_weights, grad_bias, grad_gain = pl.pallas_call(
        copy_out,
        out_shape=shapes,
        in_specs=[anywhere] * 6,
        out_specs=(anywhere,) * 6,
        scratch_shapes=[pltpu.SemaphoreType.DMA((6,))],
        compiler_params=pltpu.CompilerParams(vmem_limit_bytes=VMEM_BYTES),
        name="copy_out",
    )(*results)
    return (
        new_nodes[None],
        grad_nodes[None],
        grad_edges[None],
        grad_weights,
        grad_bias.reshape(D),
        grad_gain.reshape(D),
    )


def solution(mesh, x_chips=4):
    Y = mesh.shape["member"]
    Z = mesh.shape["dom"] // (x_chips * CORES)
    return jax.shard_map(
        functools.partial(shards, Z, x_chips, Y),
        mesh=mesh,
        in_specs=(
            P("member", "dom", None),
            P("member", "dom", None),
            P("member", "dom", None),
            P(),
            P(),
            P(),
            P("dom"),
            P("dom"),
            P("dom", None, None),
            P("dom"),
            P("dom"),
        ),
        out_specs=(
            P("member", "dom", None),
            P("member", "dom", None),
            P("member", "dom", None),
            P("dom", None),
            P(),
            P(),
        ),
        check_vma=False,
    )
```

```python
import functools

import jax
import jax.numpy as jnp
from jax import lax
from jax.experimental import pallas as pl
from jax.experimental.pallas import tpu as pltpu
from jax.sharding import PartitionSpec as P

epsilon = 1e-05
CORES = 2
LANES = 128
VMEM_BYTES = 63 * 1024 * 1024
F32 = jnp.float32
BF16 = jnp.bfloat16

FWD_PLANE, FWD_LINE, BWD_LINE, BWD_PLANE, FIRST_A, FIRST_B, SECOND_A, SECOND_B, OWNER, FINAL_Y = range(10)
SUM_PLANE, SUM_Y, SUM_LINE, PAIR_EARLY, PAIR_LATE, PAIR_P = range(10, 16)
STEPS = 16


def dot(left, right):
    return jnp.dot(left, right, preferred_element_type=F32)


def contract_rows(left, right):
    return lax.dot_general(left, right, (((0,), (0,)), ((), ())), preferred_element_type=F32)


def apply_transpose(left, right):
    return lax.dot_general(left, right, (((1,), (1,)), ((), ())), preferred_element_type=F32)


def one_hot_rows(rows, index):
    return lax.broadcasted_iota(jnp.int32, (rows, index.shape[1]), 0) == index


def total(ref, count):
    acc = ref[0].astype(F32)
    for slot in range(1, count):
        acc = acc + ref[slot].astype(F32)
    return acc


def split_transpose(rows, weights):
    high = rows.astype(BF16)
    low = (rows - high.astype(F32)).astype(BF16)
    return apply_transpose(high, weights) + apply_transpose(low, weights)


def kernel(
    sizes,
    nodes_hbm,
    outgoing_hbm,
    edges_hbm,
    w_hbm,
    bias_hbm,
    recv_hbm,
    cot_hbm,
    send_hbm,
    gain_hbm,
    node_count_ref,
    edge_count_ref,
    new_nodes_hbm,
    grad_nodes_hbm,
    grad_edges_hbm,
    gw_hbm,
    gb_hbm,
    gg_hbm,
    nodes_ref,
    outgoing_ref,
    bias_ref,
    recv_ref,
    cot_ref,
    send_ref,
    gain_ref,
    new_nodes_ref,
    grad_nodes_ref,
    gw_ref,
    gb_ref,
    gg_ref,
    w_ref,
    x_ref,
    pre_ref,
    up_ref,
    p_ref,
    ne_ref,
    ge_ref,
    outb,
    fwd1,
    fwd2,
    table,
    bwd0,
    bwd1,
    bwd2,
    back,
    pair_x,
    pair_p,
    wt,
    a1,
    a1_in,
    b1,
    b1_in,
    a2,
    a2_in,
    b2,
    b2_in,
    zw,
    zw_in,
    fin,
    fin_y,
    bg0,
    bg1,
    bg1_in,
    bg2,
    bg2_in,
    bg_in,
    local_sem,
    send_sem,
    recv_sem,
):
    Z, X, Y, D, NODE, EDGE = sizes
    PLANE = X * CORES
    TABLE = Z * PLANE * 2
    ROWS = 3 * D // Z
    OWN = ROWS // PLANE
    GROUP = X * ROWS
    BANDS = Z // X // CORES
    dom = lax.axis_index("dom")
    y = lax.axis_index("member")
    z = dom // PLANE
    plane = dom % PLANE
    x = plane // CORES
    core = plane % CORES

    def remote(src, dst, step, to_dom, to_y):
        return pltpu.make_async_remote_copy(
            src_ref=src,
            dst_ref=dst,
            send_sem=send_sem.at[step],
            recv_sem=recv_sem.at[step],
            device_id={"dom": to_dom, "member": to_y},
            device_id_type=pl.DeviceIdType.MESH,
        )

    def arrived(ref, step):
        pltpu.make_async_copy(ref, ref, recv_sem.at[step]).wait()

    def sent(ref, step):
        pltpu.make_async_copy(ref, ref, send_sem.at[step]).wait()

    def each_plane(act):
        def body(i, carry):
            peer = lax.rem(plane + PLANE // 2 + jnp.where(i < PLANE // 2, i, i + 1), PLANE)
            act(peer, z * PLANE + peer)
            return carry

        lax.fori_loop(0, PLANE - 1, body, 0)

    def each_line(act):
        def body(i, carry):
            off = Z // 2 + (1 - 2 * lax.rem(i, 2)) * ((i + 1) // 2)
            peer = lax.rem(z + off, Z)
            act(peer, peer * PLANE + plane)
            return carry

        lax.fori_loop(0, Z - 1, body, 0)

    def each_x(act):
        def body(i, carry):
            peer = lax.rem(x + 1 + i, X)
            act(peer, z * PLANE + peer * CORES + core)
            return carry

        lax.fori_loop(0, X - 1, body, 0)

    def each_y(act):
        def body(i, carry):
            act(lax.rem(y + 1 + i, Y))
            return carry

        lax.fori_loop(0, Y - 1, body, 0)

    loads = [
        pltpu.make_async_copy(src, dst, local_sem.at[i])
        for i, (src, dst) in enumerate(
            (
                (nodes_hbm, nodes_ref),
                (outgoing_hbm, outgoing_ref),
                (recv_hbm, recv_ref),
                (cot_hbm, cot_ref),
                (edges_hbm, x_ref.at[:, pl.ds(2 * D, D)]),
                (w_hbm.at[pl.ds(D, 2 * D)], w_ref.at[pl.ds(D, 2 * D)]),
                (bias_hbm, bias_ref),
                (send_hbm, send_ref),
                (gain_hbm, gain_ref),
                (w_hbm.at[pl.ds(0, D)], w_ref.at[pl.ds(0, D)]),
            )
        )
    ]
    stores = [
        pltpu.make_async_copy(src, dst, local_sem.at[len(loads) + i])
        for i, (src, dst) in enumerate(
            (
                (ge_ref, grad_edges_hbm),
                (new_nodes_ref, new_nodes_hbm),
                (grad_nodes_ref, grad_nodes_hbm),
                (gb_ref, gb_hbm),
                (gg_ref, gg_hbm),
                (gw_ref, gw_hbm),
            )
        )
    ]
    pending = []

    def finish():
        for wait in pending:
            wait()

    def store(i):
        stores[i].start()
        pending.append(stores[i].wait)

    for load in loads[:2]:
        load.start()

    barrier = pltpu.get_barrier_semaphore()

    def greet(to_dom, to_y):
        pl.semaphore_signal(
            barrier,
            inc=1,
            device_id={"dom": to_dom, "member": to_y},
            device_id_type=pl.DeviceIdType.MESH,
        )

    each_plane(lambda peer, to: greet(to, y))
    each_line(lambda peer, to: greet(to, y))
    each_y(lambda peer: greet(dom, peer))

    feeder = lax.rem(z, X) * CORES + z // X // BANDS
    feeds_self = feeder == plane

    def greet_feeder(i, carry):
        source = i * PLANE + feeder

        @pl.when(source != dom)
        def _():
            greet(source, y)

        return carry

    lax.fori_loop(0, Z, greet_feeder, 0)

    for load in loads[2:]:
        load.start()

    parts = Z * PLANE
    given = lax.broadcasted_iota(jnp.int32, (TABLE, TABLE), 0)
    placed = lax.broadcasted_iota(jnp.int32, (TABLE, TABLE), 1)
    wanted = (placed % 2) * parts + (placed // 2 % Z) * PLANE + placed // (2 * Z)
    reorder = (given == wanted).astype(BF16)
    for load in loads[:2]:
        load.wait()
    nodes = nodes_ref[...]
    outgoing = outgoing_ref[...]
    out_hot = jnp.concatenate([one_hot_rows(NODE, outgoing[k : k + 1]) for k in range(2)], axis=1)
    out_hot = dot(out_hot.astype(BF16), reorder).astype(BF16)
    outb[...] = contract_rows(out_hot, nodes).astype(BF16).reshape(PLANE, Z * 2, D)

    pl.semaphore_wait(
        barrier,
        (PLANE - 1) + (Z - 1) + (Y - 1) + BANDS * PLANE - feeds_self.astype(jnp.int32),
    )

    each_plane(lambda peer, to: remote(outb.at[peer], fwd1.at[plane], FWD_PLANE, to, y).start())
    pending.append(lambda: sent(outb.at[pl.ds(0, PLANE - 1)], FWD_PLANE))
    fwd1[plane] = outb[plane]

    live = lax.broadcasted_iota(jnp.int32, (NODE, EDGE), 1) < edge_count_ref[0]
    for load in loads[2:]:
        load.wait()
    incidence = (one_hot_rows(NODE, recv_ref[...]) & live).astype(BF16)
    x_ref[:, D : 2 * D] = contract_rows(incidence, nodes).astype(BF16)
    up_ref[...] = contract_rows(incidence, cot_ref[...])
    partner = z * PLANE + x * CORES + (1 - core)
    early = remote(
        x_ref.at[:, pl.ds(pl.multiple_of(D + (1 - core) * (D // 2), LANES), D // 2)],
        pair_x.at[:, pl.ds(pl.multiple_of(core * D, LANES), D // 2)],
        PAIR_EARLY,
        partner,
        y,
    )
    early.start()
    pending.append(early.wait_send)
    pre_ref[...] = dot(x_ref[:, D:], w_ref[D:, :]) + bias_ref[...]

    to_row = lax.broadcasted_iota(jnp.int32, (TABLE, TABLE), 0)
    from_row = lax.broadcasted_iota(jnp.int32, (TABLE, TABLE), 1)
    width = PLANE * 2
    source = ((to_row % width) // 2) * (Z * 2) + (to_row // width) * 2 + to_row % 2
    regroup = (source == from_row).astype(BF16)

    arrived(fwd1.at[pl.ds(0, PLANE - 1)], FWD_PLANE)
    fwd2[...] = dot(regroup, fwd1[...].reshape(TABLE, D)).astype(BF16).reshape(Z, width, D)
    each_line(lambda peer, to: remote(fwd2.at[peer], table.at[z], FWD_LINE, to, y).start())
    pending.append(lambda: sent(fwd2.at[pl.ds(0, Z - 1)], FWD_LINE))
    table[z] = fwd2[z]

    senders = send_ref[...]
    own_hot = one_hot_rows(NODE, senders).astype(BF16)
    table_hot = one_hot_rows(TABLE, senders - NODE).astype(BF16)
    own_rows = contract_rows(own_hot, nodes)

    arrived(table.at[pl.ds(0, Z - 1)], FWD_LINE)
    x_ref[:, 0:D] = (own_rows + contract_rows(table_hot, table[...].reshape(TABLE, D))).astype(BF16)
    late = remote(
        x_ref.at[:, pl.ds(pl.multiple_of((1 - core) * 2 * D, LANES), D)],
        pair_x.at[:, pl.ds(pl.multiple_of((1 - core) * (D // 2), LANES), D)],
        PAIR_LATE,
        partner,
        y,
    )
    late.start()
    pending.append(late.wait_send)
    pre_ref[...] += dot(x_ref[:, 0:D], w_ref[0:D, :])

    gain = gain_ref[...]
    bias_term = jnp.zeros((1, D), F32)
    gain_term = jnp.zeros((1, D), F32)
    chunk = min(64, EDGE)
    for start in range(0, EDGE, chunk):
        rows = slice(start, start + chunk)
        preact = pre_ref[rows, :]
        upstream = up_ref[rows, :]
        sigmoid = jax.nn.sigmoid(preact)
        activated = preact * sigmoid
        average = jnp.mean(activated, axis=1, keepdims=True)
        centred = activated - average
        variance = jnp.mean(centred * centred, axis=1, keepdims=True)
        inverse = lax.rsqrt(variance + epsilon)
        normed = centred * inverse
        ne_ref[rows, :] = (x_ref[rows, 2 * D :].astype(F32) + normed * gain).astype(BF16)
        gain_term += jnp.sum(upstream * normed, axis=0, keepdims=True)
        normed_grad = upstream * gain
        activated_grad = inverse * (
            normed_grad
            - jnp.mean(normed_grad, axis=1, keepdims=True)
            - normed * jnp.mean(normed_grad * normed, axis=1, keepdims=True)
        )
        preact_grad = (activated_grad * sigmoid * (1.0 + preact * (1.0 - sigmoid))).astype(BF16)
        p_ref[rows, :] = preact_grad
        bias_term += jnp.sum(preact_grad.astype(F32), axis=0, keepdims=True)

    other = remote(p_ref, pair_p, PAIR_P, partner, y)
    other.start()
    pending.append(other.wait_send)
    grad = p_ref[...]
    bwd0[...] = dot(table_hot, grad).astype(BF16).reshape(Z, width, D)
    each_line(lambda peer, to: remote(bwd0.at[peer], bwd1.at[z], BWD_LINE, to, y).start())
    pending.append(lambda: sent(bwd0.at[pl.ds(0, Z - 1)], BWD_LINE))
    bwd1[z] = bwd0[z]

    half = core * (BANDS * GROUP)
    for j in range(BANDS):
        cols = pl.ds(pl.multiple_of(half + j * GROUP, LANES), GROUP)
        wt[j] = contract_rows(x_ref[:, cols], grad)
    early.wait_recv()
    late.wait_recv()
    other.wait_recv()
    other_grad = pair_p[...]

    def band(j):
        term = wt[j] + contract_rows(pair_x[:, j * GROUP : (j + 1) * GROUP], other_grad)
        return term.astype(BF16).reshape(X, ROWS, D)

    term = band(0)
    for to in range(Y):
        a1[to] = term[:, :, to * (D // Y) : (to + 1) * (D // Y)]
    each_y(lambda peer: remote(a1.at[peer], a1_in.at[y], FIRST_A, dom, peer).start())
    pending.append(lambda: sent(a1.at[pl.ds(0, Y - 1)], FIRST_A))
    a1_in[y] = a1[y]
    b1[...] = band(1)
    each_x(lambda peer, to: remote(b1.at[peer], b1_in.at[x], FIRST_B, to, y).start())
    pending.append(lambda: sent(b1.at[pl.ds(0, X - 1)], FIRST_B))
    b1_in[x] = b1[x]

    tiles = D // LANES
    for i in range(tiles):
        cols = slice(i * LANES, (i + 1) * LANES)
        bg0[i : i + 1, :] = bias_term[:, cols]
        bg0[tiles + i : tiles + i + 1, :] = gain_term[:, cols]
    each_plane(lambda peer, to: remote(bg0, bg1_in.at[plane], SUM_PLANE, to, y).start())
    pending.append(lambda: sent(bg1_in.at[pl.ds(0, PLANE - 1)], SUM_PLANE))
    bg1_in[plane] = bg0[...]

    ge_ref[...] = (up_ref[...] + apply_transpose(grad, w_ref[2 * D :, :])).astype(BF16)
    store(0)
    new_nodes_ref[...] = (nodes.astype(F32) + dot(incidence, ne_ref[...])).astype(BF16)
    store(1)

    arrived(bg1_in.at[pl.ds(0, PLANE - 1)], SUM_PLANE)
    bg1[...] = total(bg1_in, PLANE)
    each_y(lambda peer: remote(bg1, bg2_in.at[y], SUM_Y, dom, peer).start())
    pending.append(lambda: sent(bg2_in.at[pl.ds(0, Y - 1)], SUM_Y))
    bg2_in[y] = bg1[...]

    arrived(a1_in.at[pl.ds(0, Y - 1)], FIRST_A)
    a2[...] = total(a1_in, Y).astype(BF16)
    each_x(lambda peer, to: remote(a2.at[peer], a2_in.at[x], SECOND_A, to, y).start())
    pending.append(lambda: sent(a2.at[pl.ds(0, X - 1)], SECOND_A))
    a2_in[x] = a2[x]
    arrived(b1_in.at[pl.ds(0, X - 1)], FIRST_B)
    summed = total(b1_in, X).astype(BF16)
    for to in range(Y):
        b2[to] = summed[:, to * (D // Y) : (to + 1) * (D // Y)]
    each_y(lambda peer: remote(b2.at[peer], b2_in.at[y], SECOND_B, dom, peer).start())
    pending.append(lambda: sent(b2.at[pl.ds(0, Y - 1)], SECOND_B))
    b2_in[y] = b2[y]

    arrived(bg2_in.at[pl.ds(0, Y - 1)], SUM_Y)
    bg2[...] = total(bg2_in, Y)
    each_line(lambda peer, to: remote(bg2, bg_in.at[z], SUM_LINE, to, y).start())
    pending.append(lambda: sent(bg_in.at[pl.ds(0, Z - 1)], SUM_LINE))
    bg_in[z] = bg2[...]

    node_live = lax.broadcasted_iota(jnp.int32, (NODE, D), 0) < node_count_ref[0]
    node_grad = jnp.where(node_live, cot_ref[...].astype(F32), 0.0)
    node_grad += split_transpose(dot(incidence, grad), w_ref[D : 2 * D, :])
    own_sum = dot(own_hot, grad)

    def pieces(j, rows):
        pad = jnp.zeros((zw.shape[2] - OWN, rows.shape[1]), F32)
        for piece in range(PLANE):
            block = rows[piece * OWN : (piece + 1) * OWN, :]
            zw[j, piece] = jnp.concatenate([block, pad], axis=0).astype(BF16)

    arrived(a2_in.at[pl.ds(0, X - 1)], SECOND_A)
    pieces(0, total(a2_in, X))
    arrived(b2_in.at[pl.ds(0, Y - 1)], SECOND_B)
    pieces(1, total(b2_in, Y))

    def each_owner(act):
        def body(i, carry):
            j = lax.rem(i, BANDS)
            piece = lax.rem(i // BANDS + plane + 1, PLANE)
            to = ((core * BANDS + j) * X + x) * PLANE + piece

            @pl.when(to != dom)
            def _():
                act(remote(zw.at[j, piece], zw_in.at[z], OWNER, to, y))

            return carry

        lax.fori_loop(0, BANDS * PLANE, body, 0)

    each_owner(lambda copy: copy.start())
    pending.append(lambda: each_owner(lambda copy: copy.wait_send()))

    @pl.when(feeds_self)
    def _():
        zw_in[z] = zw[lax.rem(z // X, BANDS), plane]

    arrived(bwd1.at[pl.ds(0, Z - 1)], BWD_LINE)
    bwd2[...] = (
        contract_rows(regroup, bwd1[...].reshape(TABLE, D)).astype(BF16).reshape(PLANE, Z * 2, D)
    )
    each_plane(lambda peer, to: remote(bwd2.at[peer], back.at[plane], BWD_PLANE, to, y).start())
    pending.append(lambda: sent(bwd2.at[pl.ds(0, PLANE - 1)], BWD_PLANE))
    back[plane] = bwd2[plane]

    @pl.when(feeds_self)
    def _():
        arrived(zw_in.at[pl.ds(0, Z - 1)], OWNER)

    @pl.when(jnp.logical_not(feeds_self))
    def _():
        arrived(zw_in, OWNER)

    fin[...] = total(zw_in, Z)
    each_y(lambda peer: remote(fin, fin_y.at[y], FINAL_Y, dom, peer).start())
    pending.append(lambda: sent(fin_y.at[pl.ds(0, Y - 1)], FINAL_Y))
    fin_y[y] = fin[...]

    arrived(back.at[pl.ds(0, PLANE - 1)], BWD_PLANE)
    own_sum += dot(out_hot, back[...].reshape(TABLE, D))
    grad_nodes_ref[...] = (node_grad + split_transpose(own_sum, w_ref[0:D, :])).astype(BF16)
    store(2)

    arrived(bg_in.at[pl.ds(0, Z - 1)], SUM_LINE)
    terms = total(bg_in, Z)
    for i in range(tiles):
        cols = slice(i * LANES, (i + 1) * LANES)
        gb_ref[:, cols] = terms[i : i + 1, :]
        gg_ref[:, cols] = terms[tiles + i : tiles + i + 1, :]
    store(3)
    store(4)

    arrived(fin_y.at[pl.ds(0, Y - 1)], FINAL_Y)
    for i in range(Y):
        gw_ref[:, i * (D // Y) : (i + 1) * (D // Y)] = fin_y[i, 0:OWN, :]

    store(5)

    finish()


def copy_out(*refs):
    count = (len(refs) - 1) // 3
    source, result, held, sems = refs[:count], refs[count : 2 * count], refs[2 * count : -1], refs[-1]
    loads = [pltpu.make_async_copy(source[i], held[i], sems.at[i]) for i in range(count)]
    stores = [pltpu.make_async_copy(held[i], result[i], sems.at[count + i]) for i in range(count)]
    for load in loads:
        load.start()
    for load, store in zip(loads, stores):
        load.wait()
        store.start()
    for store in stores:
        store.wait()


def shards(
    Z,
    X,
    Y,
    node_latents,
    edge_latents,
    node_cotangent,
    w_in,
    bias,
    gain,
    receivers,
    senders,
    send_rows,
    node_count,
    edge_count,
):
    _, NODE, D = node_latents.shape
    EDGE = edge_latents.shape[1]
    PLANE = X * CORES
    TABLE = Z * PLANE * 2
    ROWS = 3 * D // Z
    OWN = ROWS // PLANE
    GROUP = X * ROWS
    BANDS = Z // X // CORES
    OWN_PAD = (OWN + 15) // 16 * 16
    COLS = D // Y
    SUMS = 2 * D // LANES
    outgoing = send_rows[0].T

    anywhere = pl.BlockSpec(memory_space=pl.ANY)
    smem = pl.BlockSpec(memory_space=pltpu.SMEM)
    scratch = [
        pltpu.VMEM((NODE, D), BF16),
        pltpu.VMEM((2, Z * PLANE), jnp.int32),
        pltpu.VMEM((1, D), F32),
        pltpu.VMEM((1, EDGE), jnp.int32),
        pltpu.VMEM((NODE, D), BF16),
        pltpu.VMEM((1, EDGE), jnp.int32),
        pltpu.VMEM((1, D), F32),
        pltpu.VMEM((NODE, D), BF16),
        pltpu.VMEM((NODE, D), BF16),
        pltpu.VMEM((OWN, D), F32),
        pltpu.VMEM((1, D), F32),
        pltpu.VMEM((1, D), F32),
        pltpu.VMEM((3 * D, D), BF16),
        pltpu.VMEM((EDGE, 3 * D), BF16),
        pltpu.VMEM((EDGE, D), F32),
        pltpu.VMEM((EDGE, D), F32),
        pltpu.VMEM((EDGE, D), BF16),
        pltpu.VMEM((EDGE, D), BF16),
        pltpu.VMEM((EDGE, D), BF16),
        pltpu.VMEM((PLANE, Z * 2, D), BF16),
        pltpu.VMEM((PLANE, Z * 2, D), BF16),
        pltpu.VMEM((Z, PLANE * 2, D), BF16),
        pltpu.VMEM((Z, PLANE * 2, D), BF16),
        pltpu.VMEM((Z, PLANE * 2, D), BF16),
        pltpu.VMEM((Z, PLANE * 2, D), BF16),
        pltpu.VMEM((PLANE, Z * 2, D), BF16),
        pltpu.VMEM((PLANE, Z * 2, D), BF16),
        pltpu.VMEM((EDGE, BANDS * GROUP), BF16),
        pltpu.VMEM((EDGE, D), BF16),
        pltpu.VMEM((BANDS, GROUP, D), F32),
        pltpu.VMEM((Y, X, ROWS, COLS), BF16),
        pltpu.VMEM((Y, X, ROWS, COLS), BF16),
        pltpu.VMEM((X, ROWS, D), BF16),
        pltpu.VMEM((X, ROWS, D), BF16),
        pltpu.VMEM((X, ROWS, COLS), BF16),
        pltpu.VMEM((X, ROWS, COLS), BF16),
        pltpu.VMEM((Y, ROWS, COLS), BF16),
        pltpu.VMEM((Y, ROWS, COLS), BF16),
        pltpu.VMEM((BANDS, PLANE, OWN_PAD, COLS), BF16),
        pltpu.VMEM((Z, OWN_PAD, COLS), BF16),
        pltpu.VMEM((OWN_PAD, COLS), F32),
        pltpu.VMEM((Y, OWN_PAD, COLS), F32),
        pltpu.VMEM((SUMS, LANES), F32),
        pltpu.VMEM((SUMS, LANES), F32),
        pltpu.VMEM((PLANE, SUMS, LANES), F32),
        pltpu.VMEM((SUMS, LANES), F32),
        pltpu.VMEM((Y, SUMS, LANES), F32),
        pltpu.VMEM((Z, SUMS, LANES), F32),
        pltpu.SemaphoreType.DMA((16,)),
        pltpu.SemaphoreType.DMA((STEPS,)),
        pltpu.SemaphoreType.DMA((STEPS,)),
    ]
    shapes = (
        jax.ShapeDtypeStruct((NODE, D), BF16),
        jax.ShapeDtypeStruct((NODE, D), BF16),
        jax.ShapeDtypeStruct((EDGE, D), BF16),
        jax.ShapeDtypeStruct((OWN, D), F32),
        jax.ShapeDtypeStruct((1, D), F32),
        jax.ShapeDtypeStruct((1, D), F32),
    )
    results = pl.pallas_call(
        functools.partial(kernel, (Z, X, Y, D, NODE, EDGE)),
        out_shape=shapes,
        in_specs=[anywhere] * 9 + [smem] * 2,
        out_specs=(anywhere,) * 6,
        scratch_shapes=scratch,
        compiler_params=pltpu.CompilerParams(
            collective_id=0, has_side_effects=True, vmem_limit_bytes=VMEM_BYTES
        ),
        name="edge_update",
    )(
        node_latents[0],
        outgoing,
        edge_latents[0],
        w_in,
        bias.reshape(1, D),
        receivers.reshape(1, EDGE),
        node_cotangent[0],
        senders.reshape(1, EDGE),
        gain.reshape(1, D),
        node_count,
        edge_count,
    )
    new_nodes, grad_nodes, grad_edges, grad_weights, grad_bias, grad_gain = pl.pallas_call(
        copy_out,
        out_shape=shapes,
        in_specs=[anywhere] * 6,
        out_specs=(anywhere,) * 6,
        scratch_shapes=[pltpu.VMEM(s.shape, s.dtype) for s in shapes]
        + [pltpu.SemaphoreType.DMA((12,))],
        compiler_params=pltpu.CompilerParams(vmem_limit_bytes=VMEM_BYTES),
        name="copy_out",
    )(*results)
    return (
        new_nodes[None],
        grad_nodes[None],
        grad_edges[None],
        grad_weights,
        grad_bias.reshape(D),
        grad_gain.reshape(D),
    )


def solution(mesh, x_chips=4):
    Y = mesh.shape["member"]
    Z = mesh.shape["dom"] // (x_chips * CORES)
    return jax.shard_map(
        functools.partial(shards, Z, x_chips, Y),
        mesh=mesh,
        in_specs=(
            P("member", "dom", None),
            P("member", "dom", None),
            P("member", "dom", None),
            P(),
            P(),
            P(),
            P("dom"),
            P("dom"),
            P("dom", None, None),
            P("dom"),
            P("dom"),
        ),
        out_specs=(
            P("member", "dom", None),
            P("member", "dom", None),
            P("member", "dom", None),
            P("dom", None),
            P(),
            P(),
        ),
        check_vma=False,
    )
```

```python
import functools

import jax
import jax.numpy as jnp
from jax import lax
from jax.experimental import pallas as pl
from jax.experimental.pallas import tpu as pltpu
from jax.sharding import PartitionSpec as P

epsilon = 1e-05
CORES = 2
LANES = 128
VMEM_BYTES = 63 * 1024 * 1024
F32 = jnp.float32
BF16 = jnp.bfloat16

FWD_PLANE, FWD_LINE, BWD_LINE, BWD_PLANE, FIRST_A, FIRST_B, SECOND_A, SECOND_B, OWNER, FINAL_Y = range(10)
SUM_PLANE, SUM_Y, SUM_LINE, PAIR_EARLY, PAIR_LATE, PAIR_P = range(10, 16)
FWD_LINE_B, FWD_PLANE_B = range(16, 18)
STEPS = 18


def dot(left, right):
    return jnp.dot(left, right, preferred_element_type=F32)


def contract_rows(left, right):
    return lax.dot_general(left, right, (((0,), (0,)), ((), ())), preferred_element_type=F32)


def apply_transpose(left, right):
    return lax.dot_general(left, right, (((1,), (1,)), ((), ())), preferred_element_type=F32)


def one_hot_rows(rows, index):
    return lax.broadcasted_iota(jnp.int32, (rows, index.shape[1]), 0) == index


def total(ref, count):
    acc = ref[0].astype(F32)
    for slot in range(1, count):
        acc = acc + ref[slot].astype(F32)
    return acc


def split_transpose(rows, weights):
    high = rows.astype(BF16)
    low = (rows - high.astype(F32)).astype(BF16)
    return apply_transpose(high, weights) + apply_transpose(low, weights)


def kernel(
    sizes,
    nodes_hbm,
    outgoing_hbm,
    edges_hbm,
    w_hbm,
    bias_hbm,
    recv_hbm,
    cot_hbm,
    send_hbm,
    gain_hbm,
    node_count_ref,
    edge_count_ref,
    new_nodes_hbm,
    grad_nodes_hbm,
    grad_edges_hbm,
    gw_hbm,
    gb_hbm,
    gg_hbm,
    nodes_ref,
    outgoing_ref,
    bias_ref,
    recv_ref,
    cot_ref,
    send_ref,
    gain_ref,
    new_nodes_ref,
    grad_nodes_ref,
    gw_ref,
    gb_ref,
    gg_ref,
    w_ref,
    x_ref,
    pre_ref,
    up_ref,
    p_ref,
    ne_ref,
    ge_ref,
    outa,
    fwd1,
    fwd2,
    table,
    outb,
    mid1,
    mid2,
    table_b,
    bwd0,
    bwd1,
    bwd2,
    back,
    pair_x,
    pair_p,
    wt,
    a1,
    a1_in,
    b1,
    b1_in,
    a2,
    a2_in,
    b2,
    b2_in,
    zw,
    zw_in,
    fin,
    fin_y,
    bg0,
    bg1,
    bg1_in,
    bg2,
    bg2_in,
    bg_in,
    local_sem,
    send_sem,
    recv_sem,
):
    Z, X, Y, D, NODE, EDGE = sizes
    PLANE = X * CORES
    TABLE = Z * PLANE * 2
    ROWS = 3 * D // Z
    OWN = ROWS // PLANE
    GROUP = X * ROWS
    BANDS = Z // X // CORES
    dom = lax.axis_index("dom")
    y = lax.axis_index("member")
    z = dom // PLANE
    plane = dom % PLANE
    x = plane // CORES
    core = plane % CORES

    def remote(src, dst, step, to_dom, to_y):
        return pltpu.make_async_remote_copy(
            src_ref=src,
            dst_ref=dst,
            send_sem=send_sem.at[step],
            recv_sem=recv_sem.at[step],
            device_id={"dom": to_dom, "member": to_y},
            device_id_type=pl.DeviceIdType.MESH,
        )

    def arrived(ref, step):
        pltpu.make_async_copy(ref, ref, recv_sem.at[step]).wait()

    def sent(ref, step):
        pltpu.make_async_copy(ref, ref, send_sem.at[step]).wait()

    def each_plane(act):
        def body(i, carry):
            peer = lax.rem(plane + PLANE // 2 + jnp.where(i < PLANE // 2, i, i + 1), PLANE)
            act(peer, z * PLANE + peer)
            return carry

        lax.fori_loop(0, PLANE - 1, body, 0)

    def each_line(act):
        def body(i, carry):
            off = Z // 2 + (1 - 2 * lax.rem(i, 2)) * ((i + 1) // 2)
            peer = lax.rem(z + off, Z)
            act(peer, peer * PLANE + plane)
            return carry

        lax.fori_loop(0, Z - 1, body, 0)

    def each_x(act):
        def body(i, carry):
            peer = lax.rem(x + 1 + i, X)
            act(peer, z * PLANE + peer * CORES + core)
            return carry

        lax.fori_loop(0, X - 1, body, 0)

    def each_y(act):
        def body(i, carry):
            act(lax.rem(y + 1 + i, Y))
            return carry

        lax.fori_loop(0, Y - 1, body, 0)

    loads = [
        pltpu.make_async_copy(src, dst, local_sem.at[i])
        for i, (src, dst) in enumerate(
            (
                (nodes_hbm, nodes_ref),
                (outgoing_hbm, outgoing_ref),
                (recv_hbm, recv_ref),
                (cot_hbm, cot_ref),
                (edges_hbm, x_ref.at[:, pl.ds(2 * D, D)]),
                (w_hbm.at[pl.ds(D, 2 * D)], w_ref.at[pl.ds(D, 2 * D)]),
                (bias_hbm, bias_ref),
                (send_hbm, send_ref),
                (gain_hbm, gain_ref),
                (w_hbm.at[pl.ds(0, D)], w_ref.at[pl.ds(0, D)]),
            )
        )
    ]
    stores = [
        pltpu.make_async_copy(src, dst, local_sem.at[len(loads) + i])
        for i, (src, dst) in enumerate(
            (
                (ge_ref, grad_edges_hbm),
                (new_nodes_ref, new_nodes_hbm),
                (grad_nodes_ref, grad_nodes_hbm),
                (gb_ref, gb_hbm),
                (gg_ref, gg_hbm),
                (gw_ref, gw_hbm),
            )
        )
    ]
    pending = []

    def finish():
        for wait in pending:
            wait()

    def store(i):
        stores[i].start()
        pending.append(stores[i].wait)

    for load in loads[:2]:
        load.start()

    barrier = pltpu.get_barrier_semaphore()

    def greet(to_dom, to_y):
        pl.semaphore_signal(
            barrier,
            inc=1,
            device_id={"dom": to_dom, "member": to_y},
            device_id_type=pl.DeviceIdType.MESH,
        )

    each_plane(lambda peer, to: greet(to, y))
    each_line(lambda peer, to: greet(to, y))
    each_y(lambda peer: greet(dom, peer))

    feeder = lax.rem(z, X) * CORES + z // X // BANDS
    feeds_self = feeder == plane

    def greet_feeder(i, carry):
        source = i * PLANE + feeder

        @pl.when(source != dom)
        def _():
            greet(source, y)

        return carry

    lax.fori_loop(0, Z, greet_feeder, 0)

    for load in loads[2:]:
        load.start()

    parts = Z * PLANE
    width = PLANE * 2
    left, right = slice(0, D // 2), slice(D // 2, D)
    given = lax.broadcasted_iota(jnp.int32, (TABLE, TABLE), 0)
    placed = lax.broadcasted_iota(jnp.int32, (TABLE, TABLE), 1)
    slots = (placed % 2) * parts
    reorder = (given == slots + (placed // 2 % Z) * PLANE + placed // (2 * Z)).astype(BF16)
    in_order = (given == slots + placed // 2).astype(BF16)
    for load in loads[:2]:
        load.wait()
    nodes = nodes_ref[...]
    outgoing = outgoing_ref[...]
    slot_hot = jnp.concatenate([one_hot_rows(NODE, outgoing[k : k + 1]) for k in range(2)], axis=1)
    slot_hot = slot_hot.astype(BF16)
    order_hot = dot(slot_hot, in_order).astype(BF16)
    outb[...] = contract_rows(order_hot, nodes[:, right]).astype(BF16).reshape(Z, width, D // 2)
    out_hot = dot(slot_hot, reorder).astype(BF16)
    outa[...] = contract_rows(out_hot, nodes[:, left]).astype(BF16).reshape(PLANE, Z * 2, D // 2)

    pl.semaphore_wait(
        barrier,
        (PLANE - 1) + (Z - 1) + (Y - 1) + BANDS * PLANE - feeds_self.astype(jnp.int32),
    )

    each_line(lambda peer, to: remote(outb.at[peer], mid1.at[z], FWD_LINE_B, to, y).start())
    pending.append(lambda: sent(outb.at[pl.ds(0, Z - 1)], FWD_LINE_B))
    each_plane(lambda peer, to: remote(outa.at[peer], fwd1.at[plane], FWD_PLANE, to, y).start())
    pending.append(lambda: sent(outa.at[pl.ds(0, PLANE - 1)], FWD_PLANE))
    mid1[z] = outb[z]
    fwd1[plane] = outa[plane]

    live = lax.broadcasted_iota(jnp.int32, (NODE, EDGE), 1) < edge_count_ref[0]
    for load in loads[2:]:
        load.wait()
    incidence = (one_hot_rows(NODE, recv_ref[...]) & live).astype(BF16)
    x_ref[:, D : 2 * D] = contract_rows(incidence, nodes).astype(BF16)
    up_ref[...] = contract_rows(incidence, cot_ref[...])
    partner = z * PLANE + x * CORES + (1 - core)
    early = remote(
        x_ref.at[:, pl.ds(pl.multiple_of(D + (1 - core) * (D // 2), LANES), D // 2)],
        pair_x.at[:, pl.ds(pl.multiple_of(core * D, LANES), D // 2)],
        PAIR_EARLY,
        partner,
        y,
    )
    early.start()
    pending.append(early.wait_send)
    pre_ref[...] = dot(x_ref[:, D:], w_ref[D:, :]) + bias_ref[...]

    to_row = lax.broadcasted_iota(jnp.int32, (TABLE, TABLE), 0)
    from_row = lax.broadcasted_iota(jnp.int32, (TABLE, TABLE), 1)
    source = ((to_row % width) // 2) * (Z * 2) + (to_row // width) * 2 + to_row % 2
    regroup = (source == from_row).astype(BF16)

    arrived(fwd1.at[pl.ds(0, PLANE - 1)], FWD_PLANE)
    fwd2[...] = dot(regroup, fwd1[...].reshape(TABLE, D // 2)).astype(BF16).reshape(Z, width, D // 2)
    each_line(lambda peer, to: remote(fwd2.at[peer], table.at[z], FWD_LINE, to, y).start())
    pending.append(lambda: sent(fwd2.at[pl.ds(0, Z - 1)], FWD_LINE))
    table[z] = fwd2[z]

    senders = send_ref[...]
    own_hot = one_hot_rows(NODE, senders).astype(BF16)
    table_hot = one_hot_rows(TABLE, senders - NODE).astype(BF16)
    table_hot_b = contract_rows(regroup, table_hot).astype(BF16)
    own_rows = contract_rows(own_hot, nodes)

    arrived(mid1.at[pl.ds(0, Z - 1)], FWD_LINE_B)
    swapped = contract_rows(regroup, mid1[...].reshape(TABLE, D // 2)).astype(BF16)
    mid2[...] = swapped.reshape(PLANE, Z * 2, D // 2)
    each_plane(lambda peer, to: remote(mid2.at[peer], table_b.at[plane], FWD_PLANE_B, to, y).start())
    pending.append(lambda: sent(mid2.at[pl.ds(0, PLANE - 1)], FWD_PLANE_B))
    table_b[plane] = mid2[plane]

    arrived(table_b.at[pl.ds(0, PLANE - 1)], FWD_PLANE_B)
    theirs = contract_rows(table_hot_b, table_b[...].reshape(TABLE, D // 2))
    x_ref[:, right] = (own_rows[:, right] + theirs).astype(BF16)
    arrived(table.at[pl.ds(0, Z - 1)], FWD_LINE)
    theirs = contract_rows(table_hot, table[...].reshape(TABLE, D // 2))
    x_ref[:, left] = (own_rows[:, left] + theirs).astype(BF16)
    late = remote(
        x_ref.at[:, pl.ds(pl.multiple_of((1 - core) * 2 * D, LANES), D)],
        pair_x.at[:, pl.ds(pl.multiple_of((1 - core) * (D // 2), LANES), D)],
        PAIR_LATE,
        partner,
        y,
    )
    late.start()
    pending.append(late.wait_send)
    pre_ref[...] += dot(x_ref[:, 0:D], w_ref[0:D, :])

    gain = gain_ref[...]
    bias_term = jnp.zeros((1, D), F32)
    gain_term = jnp.zeros((1, D), F32)
    chunk = EDGE // 4
    for start in range(0, EDGE, chunk):
        rows = slice(start, start + chunk)
        preact = pre_ref[rows, :]
        upstream = up_ref[rows, :]
        sigmoid = jax.nn.sigmoid(preact)
        activated = preact * sigmoid
        average = jnp.mean(activated, axis=1, keepdims=True)
        centred = activated - average
        variance = jnp.mean(centred * centred, axis=1, keepdims=True)
        inverse = lax.rsqrt(variance + epsilon)
        normed = centred * inverse
        ne_ref[rows, :] = (x_ref[rows, 2 * D :].astype(F32) + normed * gain).astype(BF16)
        gain_term += jnp.sum(upstream * normed, axis=0, keepdims=True)
        normed_grad = upstream * gain
        activated_grad = inverse * (
            normed_grad
            - jnp.mean(normed_grad, axis=1, keepdims=True)
            - normed * jnp.mean(normed_grad * normed, axis=1, keepdims=True)
        )
        preact_grad = (activated_grad * sigmoid * (1.0 + preact * (1.0 - sigmoid))).astype(BF16)
        p_ref[rows, :] = preact_grad
        near = pl.ds(start, chunk)
        remote(p_ref.at[near], pair_p.at[near], PAIR_P, partner, y).start()
        bias_term += jnp.sum(preact_grad.astype(F32), axis=0, keepdims=True)

    pending.append(lambda: sent(p_ref, PAIR_P))

    tiles = D // LANES
    for i in range(tiles):
        cols = slice(i * LANES, (i + 1) * LANES)
        bg0[i : i + 1, :] = bias_term[:, cols]
        bg0[tiles + i : tiles + i + 1, :] = gain_term[:, cols]
    each_plane(lambda peer, to: remote(bg0, bg1_in.at[plane], SUM_PLANE, to, y).start())
    pending.append(lambda: sent(bg1_in.at[pl.ds(0, PLANE - 1)], SUM_PLANE))
    bg1_in[plane] = bg0[...]

    grad = p_ref[...]
    bwd0[...] = dot(table_hot, grad).astype(BF16).reshape(Z, width, D)
    each_line(lambda peer, to: remote(bwd0.at[peer], bwd1.at[z], BWD_LINE, to, y).start())
    pending.append(lambda: sent(bwd0.at[pl.ds(0, Z - 1)], BWD_LINE))
    bwd1[z] = bwd0[z]

    half = core * (BANDS * GROUP)
    for j in range(BANDS):
        cols = pl.ds(pl.multiple_of(half + j * GROUP, LANES), GROUP)
        wt[j] = contract_rows(x_ref[:, cols], grad)
    early.wait_recv()
    late.wait_recv()
    arrived(pair_p, PAIR_P)
    other_grad = pair_p[...]

    def band(j):
        term = wt[j] + contract_rows(pair_x[:, j * GROUP : (j + 1) * GROUP], other_grad)
        return term.astype(BF16).reshape(X, ROWS, D)

    term = band(0)
    for to in range(Y):
        a1[to] = term[:, :, to * (D // Y) : (to + 1) * (D // Y)]
    each_y(lambda peer: remote(a1.at[peer], a1_in.at[y], FIRST_A, dom, peer).start())
    pending.append(lambda: sent(a1.at[pl.ds(0, Y - 1)], FIRST_A))
    a1_in[y] = a1[y]
    b1[...] = band(1)
    each_x(lambda peer, to: remote(b1.at[peer], b1_in.at[x], FIRST_B, to, y).start())
    pending.append(lambda: sent(b1.at[pl.ds(0, X - 1)], FIRST_B))
    b1_in[x] = b1[x]

    ge_ref[...] = (up_ref[...] + apply_transpose(grad, w_ref[2 * D :, :])).astype(BF16)
    store(0)
    new_nodes_ref[...] = (nodes.astype(F32) + dot(incidence, ne_ref[...])).astype(BF16)
    store(1)

    arrived(a1_in.at[pl.ds(0, Y - 1)], FIRST_A)
    a2[...] = total(a1_in, Y).astype(BF16)
    each_x(lambda peer, to: remote(a2.at[peer], a2_in.at[x], SECOND_A, to, y).start())
    pending.append(lambda: sent(a2.at[pl.ds(0, X - 1)], SECOND_A))
    a2_in[x] = a2[x]
    arrived(b1_in.at[pl.ds(0, X - 1)], FIRST_B)
    summed = total(b1_in, X).astype(BF16)
    for to in range(Y):
        b2[to] = summed[:, to * (D // Y) : (to + 1) * (D // Y)]
    each_y(lambda peer: remote(b2.at[peer], b2_in.at[y], SECOND_B, dom, peer).start())
    pending.append(lambda: sent(b2.at[pl.ds(0, Y - 1)], SECOND_B))
    b2_in[y] = b2[y]

    arrived(bg1_in.at[pl.ds(0, PLANE - 1)], SUM_PLANE)
    bg1[...] = total(bg1_in, PLANE)
    each_y(lambda peer: remote(bg1, bg2_in.at[y], SUM_Y, dom, peer).start())
    pending.append(lambda: sent(bg2_in.at[pl.ds(0, Y - 1)], SUM_Y))
    bg2_in[y] = bg1[...]

    node_live = lax.broadcasted_iota(jnp.int32, (NODE, D), 0) < node_count_ref[0]
    node_grad = jnp.where(node_live, cot_ref[...].astype(F32), 0.0)
    node_grad += split_transpose(dot(incidence, grad), w_ref[D : 2 * D, :])
    own_sum = dot(own_hot, grad)

    def pieces(j, rows):
        pad = jnp.zeros((zw.shape[2] - OWN, rows.shape[1]), F32)
        for piece in range(PLANE):
            block = rows[piece * OWN : (piece + 1) * OWN, :]
            zw[j, piece] = jnp.concatenate([block, pad], axis=0).astype(BF16)

    arrived(a2_in.at[pl.ds(0, X - 1)], SECOND_A)
    pieces(0, total(a2_in, X))
    arrived(b2_in.at[pl.ds(0, Y - 1)], SECOND_B)
    pieces(1, total(b2_in, Y))

    def each_owner(act):
        def body(i, carry):
            j = lax.rem(i, BANDS)
            piece = lax.rem(i // BANDS + plane + 1, PLANE)
            to = ((core * BANDS + j) * X + x) * PLANE + piece

            @pl.when(to != dom)
            def _():
                act(remote(zw.at[j, piece], zw_in.at[z], OWNER, to, y))

            return carry

        lax.fori_loop(0, BANDS * PLANE, body, 0)

    each_owner(lambda copy: copy.start())
    pending.append(lambda: each_owner(lambda copy: copy.wait_send()))

    arrived(bg2_in.at[pl.ds(0, Y - 1)], SUM_Y)
    bg2[...] = total(bg2_in, Y)
    each_line(lambda peer, to: remote(bg2, bg_in.at[z], SUM_LINE, to, y).start())
    pending.append(lambda: sent(bg_in.at[pl.ds(0, Z - 1)], SUM_LINE))
    bg_in[z] = bg2[...]

    @pl.when(feeds_self)
    def _():
        zw_in[z] = zw[lax.rem(z // X, BANDS), plane]

    arrived(bwd1.at[pl.ds(0, Z - 1)], BWD_LINE)
    bwd2[...] = (
        contract_rows(regroup, bwd1[...].reshape(TABLE, D)).astype(BF16).reshape(PLANE, Z * 2, D)
    )
    each_plane(lambda peer, to: remote(bwd2.at[peer], back.at[plane], BWD_PLANE, to, y).start())
    pending.append(lambda: sent(bwd2.at[pl.ds(0, PLANE - 1)], BWD_PLANE))
    back[plane] = bwd2[plane]

    @pl.when(feeds_self)
    def _():
        arrived(zw_in.at[pl.ds(0, Z - 1)], OWNER)

    @pl.when(jnp.logical_not(feeds_self))
    def _():
        arrived(zw_in, OWNER)

    fin[...] = total(zw_in, Z)
    each_y(lambda peer: remote(fin, fin_y.at[y], FINAL_Y, dom, peer).start())
    pending.append(lambda: sent(fin_y.at[pl.ds(0, Y - 1)], FINAL_Y))
    fin_y[y] = fin[...]

    arrived(back.at[pl.ds(0, PLANE - 1)], BWD_PLANE)
    own_sum += dot(out_hot, back[...].reshape(TABLE, D))
    grad_nodes_ref[...] = (node_grad + split_transpose(own_sum, w_ref[0:D, :])).astype(BF16)
    store(2)

    arrived(bg_in.at[pl.ds(0, Z - 1)], SUM_LINE)
    terms = total(bg_in, Z)
    for i in range(tiles):
        cols = slice(i * LANES, (i + 1) * LANES)
        gb_ref[:, cols] = terms[i : i + 1, :]
        gg_ref[:, cols] = terms[tiles + i : tiles + i + 1, :]
    store(3)
    store(4)

    arrived(fin_y.at[pl.ds(0, Y - 1)], FINAL_Y)
    for i in range(Y):
        gw_ref[:, i * (D // Y) : (i + 1) * (D // Y)] = fin_y[i, 0:OWN, :]

    store(5)

    finish()


def copy_out(*refs):
    count = (len(refs) - 1) // 3
    source, result, held, sems = refs[:count], refs[count : 2 * count], refs[2 * count : -1], refs[-1]
    loads = [pltpu.make_async_copy(source[i], held[i], sems.at[i]) for i in range(count)]
    stores = [pltpu.make_async_copy(held[i], result[i], sems.at[count + i]) for i in range(count)]
    for load in loads:
        load.start()
    for load, store in zip(loads, stores):
        load.wait()
        store.start()
    for store in stores:
        store.wait()


def shards(
    Z,
    X,
    Y,
    node_latents,
    edge_latents,
    node_cotangent,
    w_in,
    bias,
    gain,
    receivers,
    senders,
    send_rows,
    node_count,
    edge_count,
):
    _, NODE, D = node_latents.shape
    EDGE = edge_latents.shape[1]
    PLANE = X * CORES
    TABLE = Z * PLANE * 2
    ROWS = 3 * D // Z
    OWN = ROWS // PLANE
    GROUP = X * ROWS
    BANDS = Z // X // CORES
    OWN_PAD = (OWN + 15) // 16 * 16
    COLS = D // Y
    SUMS = 2 * D // LANES
    outgoing = send_rows[0].T

    anywhere = pl.BlockSpec(memory_space=pl.ANY)
    smem = pl.BlockSpec(memory_space=pltpu.SMEM)
    scratch = [
        pltpu.VMEM((NODE, D), BF16),
        pltpu.VMEM((2, Z * PLANE), jnp.int32),
        pltpu.VMEM((1, D), F32),
        pltpu.VMEM((1, EDGE), jnp.int32),
        pltpu.VMEM((NODE, D), BF16),
        pltpu.VMEM((1, EDGE), jnp.int32),
        pltpu.VMEM((1, D), F32),
        pltpu.VMEM((NODE, D), BF16),
        pltpu.VMEM((NODE, D), BF16),
        pltpu.VMEM((OWN, D), F32),
        pltpu.VMEM((1, D), F32),
        pltpu.VMEM((1, D), F32),
        pltpu.VMEM((3 * D, D), BF16),
        pltpu.VMEM((EDGE, 3 * D), BF16),
        pltpu.VMEM((EDGE, D), F32),
        pltpu.VMEM((EDGE, D), F32),
        pltpu.VMEM((EDGE, D), BF16),
        pltpu.VMEM((EDGE, D), BF16),
        pltpu.VMEM((EDGE, D), BF16),
        pltpu.VMEM((PLANE, Z * 2, D // 2), BF16),
        pltpu.VMEM((PLANE, Z * 2, D // 2), BF16),
        pltpu.VMEM((Z, PLANE * 2, D // 2), BF16),
        pltpu.VMEM((Z, PLANE * 2, D // 2), BF16),
        pltpu.VMEM((Z, PLANE * 2, D // 2), BF16),
        pltpu.VMEM((Z, PLANE * 2, D // 2), BF16),
        pltpu.VMEM((PLANE, Z * 2, D // 2), BF16),
        pltpu.VMEM((PLANE, Z * 2, D // 2), BF16),
        pltpu.VMEM((Z, PLANE * 2, D), BF16),
        pltpu.VMEM((Z, PLANE * 2, D), BF16),
        pltpu.VMEM((PLANE, Z * 2, D), BF16),
        pltpu.VMEM((PLANE, Z * 2, D), BF16),
        pltpu.VMEM((EDGE, BANDS * GROUP), BF16),
        pltpu.VMEM((EDGE, D), BF16),
        pltpu.VMEM((BANDS, GROUP, D), F32),
        pltpu.VMEM((Y, X, ROWS, COLS), BF16),
        pltpu.VMEM((Y, X, ROWS, COLS), BF16),
        pltpu.VMEM((X, ROWS, D), BF16),
        pltpu.VMEM((X, ROWS, D), BF16),
        pltpu.VMEM((X, ROWS, COLS), BF16),
        pltpu.VMEM((X, ROWS, COLS), BF16),
        pltpu.VMEM((Y, ROWS, COLS), BF16),
        pltpu.VMEM((Y, ROWS, COLS), BF16),
        pltpu.VMEM((BANDS, PLANE, OWN_PAD, COLS), BF16),
        pltpu.VMEM((Z, OWN_PAD, COLS), BF16),
        pltpu.VMEM((OWN_PAD, COLS), F32),
        pltpu.VMEM((Y, OWN_PAD, COLS), F32),
        pltpu.VMEM((SUMS, LANES), F32),
        pltpu.VMEM((SUMS, LANES), F32),
        pltpu.VMEM((PLANE, SUMS, LANES), F32),
        pltpu.VMEM((SUMS, LANES), F32),
        pltpu.VMEM((Y, SUMS, LANES), F32),
        pltpu.VMEM((Z, SUMS, LANES), F32),
        pltpu.SemaphoreType.DMA((16,)),
        pltpu.SemaphoreType.DMA((STEPS,)),
        pltpu.SemaphoreType.DMA((STEPS,)),
    ]
    shapes = (
        jax.ShapeDtypeStruct((NODE, D), BF16),
        jax.ShapeDtypeStruct((NODE, D), BF16),
        jax.ShapeDtypeStruct((EDGE, D), BF16),
        jax.ShapeDtypeStruct((OWN, D), F32),
        jax.ShapeDtypeStruct((1, D), F32),
        jax.ShapeDtypeStruct((1, D), F32),
    )
    results = pl.pallas_call(
        functools.partial(kernel, (Z, X, Y, D, NODE, EDGE)),
        out_shape=shapes,
        in_specs=[anywhere] * 9 + [smem] * 2,
        out_specs=(anywhere,) * 6,
        scratch_shapes=scratch,
        compiler_params=pltpu.CompilerParams(
            collective_id=0, has_side_effects=True, vmem_limit_bytes=VMEM_BYTES
        ),
        name="edge_update",
    )(
        node_latents[0],
        outgoing,
        edge_latents[0],
        w_in,
        bias.reshape(1, D),
        receivers.reshape(1, EDGE),
        node_cotangent[0],
        senders.reshape(1, EDGE),
        gain.reshape(1, D),
        node_count,
        edge_count,
    )
    new_nodes, grad_nodes, grad_edges, grad_weights, grad_bias, grad_gain = pl.pallas_call(
        copy_out,
        out_shape=shapes,
        in_specs=[anywhere] * 6,
        out_specs=(anywhere,) * 6,
        scratch_shapes=[pltpu.VMEM(s.shape, s.dtype) for s in shapes]
        + [pltpu.SemaphoreType.DMA((12,))],
        compiler_params=pltpu.CompilerParams(vmem_limit_bytes=VMEM_BYTES),
        name="copy_out",
    )(*results)
    return (
        new_nodes[None],
        grad_nodes[None],
        grad_edges[None],
        grad_weights,
        grad_bias.reshape(D),
        grad_gain.reshape(D),
    )


def solution(mesh, x_chips=4):
    Y = mesh.shape["member"]
    Z = mesh.shape["dom"] // (x_chips * CORES)
    return jax.shard_map(
        functools.partial(shards, Z, x_chips, Y),
        mesh=mesh,
        in_specs=(
            P("member", "dom", None),
            P("member", "dom", None),
            P("member", "dom", None),
            P(),
            P(),
            P(),
            P("dom"),
            P("dom"),
            P("dom", None, None),
            P("dom"),
            P("dom"),
        ),
        out_specs=(
            P("member", "dom", None),
            P("member", "dom", None),
            P("member", "dom", None),
            P("dom", None),
            P(),
            P(),
        ),
        check_vma=False,
    )
```

```python
import functools

import jax
import jax.numpy as jnp
from jax import lax
from jax.experimental import pallas as pl
from jax.experimental.pallas import tpu as pltpu
from jax.sharding import PartitionSpec as P

epsilon = 1e-05
CORES = 2
LANES = 128
VMEM_BYTES = 63 * 1024 * 1024
F32 = jnp.float32
BF16 = jnp.bfloat16

FWD_PLANE, FWD_LINE, BWD_LINE, BWD_PLANE, FIRST_A, FIRST_B, SECOND_A, SECOND_B, OWNER, FINAL_Y = range(10)
PAIR_SUMS, PAIR_EARLY, PAIR_LATE, PAIR_P = range(10, 14)
FWD_LINE_B, FWD_PLANE_B = range(14, 16)
STEPS = 16


def dot(left, right):
    return jnp.dot(left, right, preferred_element_type=F32)


def contract_rows(left, right):
    return lax.dot_general(left, right, (((0,), (0,)), ((), ())), preferred_element_type=F32)


def apply_transpose(left, right):
    return lax.dot_general(left, right, (((1,), (1,)), ((), ())), preferred_element_type=F32)


def one_hot_rows(rows, index):
    return lax.broadcasted_iota(jnp.int32, (rows, index.shape[1]), 0) == index


def total(ref, count):
    acc = ref[0].astype(F32)
    for slot in range(1, count):
        acc = acc + ref[slot].astype(F32)
    return acc


def two_terms(pair, rows):
    high = pair.astype(BF16).astype(F32)
    zeros = [jnp.zeros((rows - 4, pair.shape[1]), F32)] if rows > 4 else []
    return jnp.concatenate([high, pair - high] + zeros, axis=0)


def split_transpose(rows, weights):
    high = rows.astype(BF16)
    low = (rows - high.astype(F32)).astype(BF16)
    return apply_transpose(high, weights) + apply_transpose(low, weights)


def kernel(
    sizes,
    nodes_hbm,
    outgoing_hbm,
    edges_hbm,
    w_hbm,
    bias_hbm,
    recv_hbm,
    cot_hbm,
    send_hbm,
    gain_hbm,
    node_count_ref,
    edge_count_ref,
    new_nodes_hbm,
    grad_nodes_hbm,
    grad_edges_hbm,
    gw_hbm,
    gb_hbm,
    gg_hbm,
    nodes_ref,
    outgoing_ref,
    bias_ref,
    recv_ref,
    cot_ref,
    send_ref,
    gain_ref,
    new_nodes_ref,
    grad_nodes_ref,
    gw_ref,
    gb_ref,
    gg_ref,
    w_ref,
    x_ref,
    pre_ref,
    up_ref,
    p_ref,
    ne_ref,
    ge_ref,
    outa,
    fwd1,
    fwd2,
    table,
    outb,
    mid1,
    mid2,
    table_b,
    bwd0,
    bwd1,
    bwd2,
    back,
    pair_x,
    pair_p,
    wt,
    a1,
    a1_in,
    b1,
    b1_in,
    a2,
    a2_in,
    b2,
    b2_in,
    zw,
    zw_in,
    fin,
    fin_y,
    sums,
    sums_in,
    local_sem,
    send_sem,
    recv_sem,
):
    Z, X, Y, D, NODE, EDGE = sizes
    PLANE = X * CORES
    TABLE = Z * PLANE * 2
    ROWS = 3 * D // Z
    OWN = ROWS // PLANE
    GROUP = X * ROWS
    BANDS = Z // X // CORES
    dom = lax.axis_index("dom")
    y = lax.axis_index("member")
    z = dom // PLANE
    plane = dom % PLANE
    x = plane // CORES
    core = plane % CORES

    def remote(src, dst, step, to_dom, to_y):
        return pltpu.make_async_remote_copy(
            src_ref=src,
            dst_ref=dst,
            send_sem=send_sem.at[step],
            recv_sem=recv_sem.at[step],
            device_id={"dom": to_dom, "member": to_y},
            device_id_type=pl.DeviceIdType.MESH,
        )

    def arrived(ref, step):
        pltpu.make_async_copy(ref, ref, recv_sem.at[step]).wait()

    def sent(ref, step):
        pltpu.make_async_copy(ref, ref, send_sem.at[step]).wait()

    def each_plane(act):
        def body(i, carry):
            peer = lax.rem(plane + PLANE // 2 + jnp.where(i < PLANE // 2, i, i + 1), PLANE)
            act(peer, z * PLANE + peer)
            return carry

        lax.fori_loop(0, PLANE - 1, body, 0)

    def each_line(act):
        def body(i, carry):
            off = Z // 2 + (1 - 2 * lax.rem(i, 2)) * ((i + 1) // 2)
            peer = lax.rem(z + off, Z)
            act(peer, peer * PLANE + plane)
            return carry

        lax.fori_loop(0, Z - 1, body, 0)

    def each_x(act):
        def body(i, carry):
            peer = lax.rem(x + 1 + i, X)
            act(peer, z * PLANE + peer * CORES + core)
            return carry

        lax.fori_loop(0, X - 1, body, 0)

    def each_y(act):
        def body(i, carry):
            act(lax.rem(y + 1 + i, Y))
            return carry

        lax.fori_loop(0, Y - 1, body, 0)

    loads = [
        pltpu.make_async_copy(src, dst, local_sem.at[i])
        for i, (src, dst) in enumerate(
            (
                (nodes_hbm, nodes_ref),
                (outgoing_hbm, outgoing_ref),
                (recv_hbm, recv_ref),
                (cot_hbm, cot_ref),
                (edges_hbm, x_ref.at[:, pl.ds(2 * D, D)]),
                (w_hbm.at[pl.ds(D, 2 * D)], w_ref.at[pl.ds(D, 2 * D)]),
                (bias_hbm, bias_ref),
                (send_hbm, send_ref),
                (gain_hbm, gain_ref),
                (w_hbm.at[pl.ds(0, D)], w_ref.at[pl.ds(0, D)]),
            )
        )
    ]
    stores = [
        pltpu.make_async_copy(src, dst, local_sem.at[len(loads) + i])
        for i, (src, dst) in enumerate(
            (
                (ge_ref, grad_edges_hbm),
                (new_nodes_ref, new_nodes_hbm),
                (grad_nodes_ref, grad_nodes_hbm),
                (gb_ref, gb_hbm),
                (gg_ref, gg_hbm),
                (gw_ref, gw_hbm),
            )
        )
    ]
    pending = []

    def finish():
        for wait in pending:
            wait()

    def store(i):
        stores[i].start()
        pending.append(stores[i].wait)

    for load in loads[:2]:
        load.start()

    barrier = pltpu.get_barrier_semaphore()

    def greet(to_dom, to_y):
        pl.semaphore_signal(
            barrier,
            inc=1,
            device_id={"dom": to_dom, "member": to_y},
            device_id_type=pl.DeviceIdType.MESH,
        )

    each_plane(lambda peer, to: greet(to, y))
    each_line(lambda peer, to: greet(to, y))
    each_y(lambda peer: greet(dom, peer))

    feeder = lax.rem(z, X) * CORES + z // X // BANDS
    feeds_self = feeder == plane

    for load in loads[2:]:
        load.start()

    parts = Z * PLANE
    width = PLANE * 2
    left, right = slice(0, D // 2), slice(D // 2, D)
    given = lax.broadcasted_iota(jnp.int32, (TABLE, TABLE), 0)
    placed = lax.broadcasted_iota(jnp.int32, (TABLE, TABLE), 1)
    slots = (placed % 2) * parts
    reorder = (given == slots + (placed // 2 % Z) * PLANE + placed // (2 * Z)).astype(BF16)
    in_order = (given == slots + placed // 2).astype(BF16)
    for load in loads[:2]:
        load.wait()
    nodes = nodes_ref[...]
    outgoing = outgoing_ref[...]
    slot_hot = jnp.concatenate([one_hot_rows(NODE, outgoing[k : k + 1]) for k in range(2)], axis=1)
    slot_hot = slot_hot.astype(BF16)
    order_hot = dot(slot_hot, in_order).astype(BF16)
    outb[...] = contract_rows(order_hot, nodes[:, right]).astype(BF16).reshape(Z, width, D // 2)
    out_hot = dot(slot_hot, reorder).astype(BF16)
    outa[...] = contract_rows(out_hot, nodes[:, left]).astype(BF16).reshape(PLANE, Z * 2, D // 2)

    pl.semaphore_wait(
        barrier,
        (PLANE - 1) + (Z - 1) + (Y - 1),
    )

    each_line(lambda peer, to: remote(outb.at[peer], mid1.at[z], FWD_LINE_B, to, y).start())
    pending.append(lambda: sent(outb.at[pl.ds(0, Z - 1)], FWD_LINE_B))
    each_plane(lambda peer, to: remote(outa.at[peer], fwd1.at[plane], FWD_PLANE, to, y).start())
    pending.append(lambda: sent(outa.at[pl.ds(0, PLANE - 1)], FWD_PLANE))
    mid1[z] = outb[z]
    fwd1[plane] = outa[plane]

    live = lax.broadcasted_iota(jnp.int32, (NODE, EDGE), 1) < edge_count_ref[0]
    for load in loads[2:]:
        load.wait()
    incidence = (one_hot_rows(NODE, recv_ref[...]) & live).astype(BF16)
    x_ref[:, D : 2 * D] = contract_rows(incidence, nodes).astype(BF16)
    up_ref[...] = contract_rows(incidence, cot_ref[...])
    partner = z * PLANE + x * CORES + (1 - core)
    early = remote(
        x_ref.at[:, pl.ds(pl.multiple_of(D + (1 - core) * (D // 2), LANES), D // 2)],
        pair_x.at[:, pl.ds(pl.multiple_of(core * D, LANES), D // 2)],
        PAIR_EARLY,
        partner,
        y,
    )
    early.start()
    pending.append(early.wait_send)
    pre_ref[...] = dot(x_ref[:, D:], w_ref[D:, :]) + bias_ref[...]

    to_row = lax.broadcasted_iota(jnp.int32, (TABLE, TABLE), 0)
    from_row = lax.broadcasted_iota(jnp.int32, (TABLE, TABLE), 1)
    source = ((to_row % width) // 2) * (Z * 2) + (to_row // width) * 2 + to_row % 2
    regroup = (source == from_row).astype(BF16)

    arrived(fwd1.at[pl.ds(0, PLANE - 1)], FWD_PLANE)
    fwd2[...] = dot(regroup, fwd1[...].reshape(TABLE, D // 2)).astype(BF16).reshape(Z, width, D // 2)
    each_line(lambda peer, to: remote(fwd2.at[peer], table.at[z], FWD_LINE, to, y).start())
    pending.append(lambda: sent(fwd2.at[pl.ds(0, Z - 1)], FWD_LINE))
    table[z] = fwd2[z]

    senders = send_ref[...]
    own_hot = one_hot_rows(NODE, senders).astype(BF16)
    table_hot = one_hot_rows(TABLE, senders - NODE).astype(BF16)
    table_hot_b = contract_rows(regroup, table_hot).astype(BF16)
    own_rows = contract_rows(own_hot, nodes)

    arrived(mid1.at[pl.ds(0, Z - 1)], FWD_LINE_B)
    swapped = contract_rows(regroup, mid1[...].reshape(TABLE, D // 2)).astype(BF16)
    mid2[...] = swapped.reshape(PLANE, Z * 2, D // 2)
    each_plane(lambda peer, to: remote(mid2.at[peer], table_b.at[plane], FWD_PLANE_B, to, y).start())
    pending.append(lambda: sent(mid2.at[pl.ds(0, PLANE - 1)], FWD_PLANE_B))
    table_b[plane] = mid2[plane]

    arrived(table_b.at[pl.ds(0, PLANE - 1)], FWD_PLANE_B)
    theirs = contract_rows(table_hot_b, table_b[...].reshape(TABLE, D // 2))
    x_ref[:, right] = (own_rows[:, right] + theirs).astype(BF16)
    arrived(table.at[pl.ds(0, Z - 1)], FWD_LINE)
    theirs = contract_rows(table_hot, table[...].reshape(TABLE, D // 2))
    x_ref[:, left] = (own_rows[:, left] + theirs).astype(BF16)
    late = remote(
        x_ref.at[:, pl.ds(pl.multiple_of((1 - core) * 2 * D, LANES), D)],
        pair_x.at[:, pl.ds(pl.multiple_of((1 - core) * (D // 2), LANES), D)],
        PAIR_LATE,
        partner,
        y,
    )
    late.start()
    pending.append(late.wait_send)
    pre_ref[...] += dot(x_ref[:, 0:D], w_ref[0:D, :])

    gain = gain_ref[...]
    bias_term = jnp.zeros((1, D), F32)
    gain_term = jnp.zeros((1, D), F32)
    chunk = EDGE // 4
    for start in range(0, EDGE, chunk):
        rows = slice(start, start + chunk)
        preact = pre_ref[rows, :]
        upstream = up_ref[rows, :]
        sigmoid = jax.nn.sigmoid(preact)
        activated = preact * sigmoid
        average = jnp.mean(activated, axis=1, keepdims=True)
        centred = activated - average
        variance = jnp.mean(centred * centred, axis=1, keepdims=True)
        inverse = lax.rsqrt(variance + epsilon)
        normed = centred * inverse
        ne_ref[rows, :] = (x_ref[rows, 2 * D :].astype(F32) + normed * gain).astype(BF16)
        gain_term += jnp.sum(upstream * normed, axis=0, keepdims=True)
        normed_grad = upstream * gain
        activated_grad = inverse * (
            normed_grad
            - jnp.mean(normed_grad, axis=1, keepdims=True)
            - normed * jnp.mean(normed_grad * normed, axis=1, keepdims=True)
        )
        preact_grad = (activated_grad * sigmoid * (1.0 + preact * (1.0 - sigmoid))).astype(BF16)
        p_ref[rows, :] = preact_grad
        near = pl.ds(start, chunk)
        remote(p_ref.at[near], pair_p.at[near], PAIR_P, partner, y).start()
        bias_term += jnp.sum(preact_grad.astype(F32), axis=0, keepdims=True)

    pending.append(lambda: sent(p_ref, PAIR_P))

    sums[...] = jnp.concatenate([bias_term, gain_term, jnp.zeros((6, D), F32)], axis=0)
    pair_sums = remote(sums, sums_in, PAIR_SUMS, partner, y)
    pair_sums.start()
    pending.append(pair_sums.wait_send)
    grad = p_ref[...]
    bwd0[...] = dot(table_hot, grad).astype(BF16).reshape(Z, width, D)
    each_line(lambda peer, to: remote(bwd0.at[peer], bwd1.at[z], BWD_LINE, to, y).start())
    pending.append(lambda: sent(bwd0.at[pl.ds(0, Z - 1)], BWD_LINE))
    bwd1[z] = bwd0[z]

    half = core * (BANDS * GROUP)
    for j in range(BANDS):
        cols = pl.ds(pl.multiple_of(half + j * GROUP, LANES), GROUP)
        wt[j] = contract_rows(x_ref[:, cols], grad)
    early.wait_recv()
    late.wait_recv()
    arrived(pair_p, PAIR_P)
    pair_sums.wait_recv()
    other_grad = pair_p[...]

    def band(j):
        term = wt[j] + contract_rows(pair_x[:, j * GROUP : (j + 1) * GROUP], other_grad)
        return term.astype(BF16).reshape(X, ROWS, D)

    term = band(0)
    pair_terms = two_terms(sums[0:2] + sums_in[0:2], 16).astype(BF16)
    for to in range(Y):
        cols = slice(to * (D // Y), (to + 1) * (D // Y))
        a1[to, 0 : X * ROWS] = term[:, :, cols].reshape(X * ROWS, D // Y)
        a1[to, X * ROWS :] = pair_terms[:, cols]
    each_y(lambda peer: remote(a1.at[peer], a1_in.at[y], FIRST_A, dom, peer).start())
    pending.append(lambda: sent(a1.at[pl.ds(0, Y - 1)], FIRST_A))
    a1_in[y] = a1[y]
    b1[...] = band(1)
    each_x(lambda peer, to: remote(b1.at[peer], b1_in.at[x], FIRST_B, to, y).start())
    pending.append(lambda: sent(b1.at[pl.ds(0, X - 1)], FIRST_B))
    b1_in[x] = b1[x]

    ge_ref[...] = (up_ref[...] + apply_transpose(grad, w_ref[2 * D :, :])).astype(BF16)
    store(0)
    new_nodes_ref[...] = (nodes.astype(F32) + dot(incidence, ne_ref[...])).astype(BF16)
    store(1)

    arrived(a1_in.at[pl.ds(0, Y - 1)], FIRST_A)
    summed = total(a1_in, Y)
    terms = summed[X * ROWS :]
    terms = two_terms(terms[0:2] + terms[2:4], 16).astype(BF16)
    summed = summed[0 : X * ROWS].astype(BF16)
    for to in range(X):
        a2[to, 0:ROWS] = summed[to * ROWS : (to + 1) * ROWS]
        a2[to, ROWS:] = terms
    each_x(lambda peer, to: remote(a2.at[peer], a2_in.at[x], SECOND_A, to, y).start())
    pending.append(lambda: sent(a2.at[pl.ds(0, X - 1)], SECOND_A))
    a2_in[x] = a2[x]
    arrived(b1_in.at[pl.ds(0, X - 1)], FIRST_B)
    summed = total(b1_in, X).astype(BF16)
    for to in range(Y):
        b2[to] = summed[:, to * (D // Y) : (to + 1) * (D // Y)]
    each_y(lambda peer: remote(b2.at[peer], b2_in.at[y], SECOND_B, dom, peer).start())
    pending.append(lambda: sent(b2.at[pl.ds(0, Y - 1)], SECOND_B))
    b2_in[y] = b2[y]

    node_live = lax.broadcasted_iota(jnp.int32, (NODE, D), 0) < node_count_ref[0]
    node_grad = jnp.where(node_live, cot_ref[...].astype(F32), 0.0)
    node_grad += split_transpose(dot(incidence, grad), w_ref[D : 2 * D, :])
    own_sum = dot(own_hot, grad)

    def pieces(j, rows, pad):
        for piece in range(PLANE):
            block = rows[piece * OWN : (piece + 1) * OWN, :]
            zw[j, piece] = jnp.concatenate([block, pad], axis=0).astype(BF16)

    arrived(a2_in.at[pl.ds(0, X - 1)], SECOND_A)
    rows = total(a2_in, X)
    terms = rows[ROWS:]
    pad = two_terms(terms[0:2] + terms[2:4], zw.shape[2] - OWN)
    pieces(0, rows, pad)
    arrived(b2_in.at[pl.ds(0, Y - 1)], SECOND_B)
    pieces(1, total(b2_in, Y), pad)

    def each_owner(act):
        def body(i, carry):
            j = lax.rem(i, BANDS)
            piece = lax.rem(i // BANDS + plane + 1, PLANE)
            to = ((core * BANDS + j) * X + x) * PLANE + piece

            @pl.when(to != dom)
            def _():
                act(remote(zw.at[j, piece], zw_in.at[z], OWNER, to, y))

            return carry

        lax.fori_loop(0, BANDS * PLANE, body, 0)

    each_owner(lambda copy: copy.start())
    pending.append(lambda: each_owner(lambda copy: copy.wait_send()))

    @pl.when(feeds_self)
    def _():
        zw_in[z] = zw[lax.rem(z // X, BANDS), plane]

    arrived(bwd1.at[pl.ds(0, Z - 1)], BWD_LINE)
    bwd2[...] = (
        contract_rows(regroup, bwd1[...].reshape(TABLE, D)).astype(BF16).reshape(PLANE, Z * 2, D)
    )
    each_plane(lambda peer, to: remote(bwd2.at[peer], back.at[plane], BWD_PLANE, to, y).start())
    pending.append(lambda: sent(bwd2.at[pl.ds(0, PLANE - 1)], BWD_PLANE))
    back[plane] = bwd2[plane]

    @pl.when(feeds_self)
    def _():
        arrived(zw_in.at[pl.ds(0, Z - 1)], OWNER)

    @pl.when(jnp.logical_not(feeds_self))
    def _():
        arrived(zw_in, OWNER)

    fin[...] = total(zw_in, Z)
    each_y(lambda peer: remote(fin, fin_y.at[y], FINAL_Y, dom, peer).start())
    pending.append(lambda: sent(fin_y.at[pl.ds(0, Y - 1)], FINAL_Y))
    fin_y[y] = fin[...]

    arrived(back.at[pl.ds(0, PLANE - 1)], BWD_PLANE)
    own_sum += dot(out_hot, back[...].reshape(TABLE, D))
    grad_nodes_ref[...] = (node_grad + split_transpose(own_sum, w_ref[0:D, :])).astype(BF16)
    store(2)

    arrived(fin_y.at[pl.ds(0, Y - 1)], FINAL_Y)
    for i in range(Y):
        cols = slice(i * (D // Y), (i + 1) * (D // Y))
        gw_ref[:, cols] = fin_y[i, 0:OWN, :]
        terms = fin_y[i, OWN : OWN + 2, :] + fin_y[i, OWN + 2 : OWN + 4, :]
        gb_ref[:, cols] = terms[0:1]
        gg_ref[:, cols] = terms[1:2]
    store(3)
    store(4)

    store(5)

    finish()


def copy_out(*refs):
    count = (len(refs) - 1) // 3
    source, result, held, sems = refs[:count], refs[count : 2 * count], refs[2 * count : -1], refs[-1]
    loads = [pltpu.make_async_copy(source[i], held[i], sems.at[i]) for i in range(count)]
    stores = [pltpu.make_async_copy(held[i], result[i], sems.at[count + i]) for i in range(count)]
    for load in loads:
        load.start()
    for load, store in zip(loads, stores):
        load.wait()
        store.start()
    for store in stores:
        store.wait()


def shards(
    Z,
    X,
    Y,
    node_latents,
    edge_latents,
    node_cotangent,
    w_in,
    bias,
    gain,
    receivers,
    senders,
    send_rows,
    node_count,
    edge_count,
):
    _, NODE, D = node_latents.shape
    EDGE = edge_latents.shape[1]
    PLANE = X * CORES
    TABLE = Z * PLANE * 2
    ROWS = 3 * D // Z
    OWN = ROWS // PLANE
    GROUP = X * ROWS
    BANDS = Z // X // CORES
    OWN_PAD = (OWN + 4 + 15) // 16 * 16
    COLS = D // Y
    outgoing = send_rows[0].T

    anywhere = pl.BlockSpec(memory_space=pl.ANY)
    smem = pl.BlockSpec(memory_space=pltpu.SMEM)
    scratch = [
        pltpu.VMEM((NODE, D), BF16),
        pltpu.VMEM((2, Z * PLANE), jnp.int32),
        pltpu.VMEM((1, D), F32),
        pltpu.VMEM((1, EDGE), jnp.int32),
        pltpu.VMEM((NODE, D), BF16),
        pltpu.VMEM((1, EDGE), jnp.int32),
        pltpu.VMEM((1, D), F32),
        pltpu.VMEM((NODE, D), BF16),
        pltpu.VMEM((NODE, D), BF16),
        pltpu.VMEM((OWN, D), F32),
        pltpu.VMEM((1, D), F32),
        pltpu.VMEM((1, D), F32),
        pltpu.VMEM((3 * D, D), BF16),
        pltpu.VMEM((EDGE, 3 * D), BF16),
        pltpu.VMEM((EDGE, D), F32),
        pltpu.VMEM((EDGE, D), F32),
        pltpu.VMEM((EDGE, D), BF16),
        pltpu.VMEM((EDGE, D), BF16),
        pltpu.VMEM((EDGE, D), BF16),
        pltpu.VMEM((PLANE, Z * 2, D // 2), BF16),
        pltpu.VMEM((PLANE, Z * 2, D // 2), BF16),
        pltpu.VMEM((Z, PLANE * 2, D // 2), BF16),
        pltpu.VMEM((Z, PLANE * 2, D // 2), BF16),
        pltpu.VMEM((Z, PLANE * 2, D // 2), BF16),
        pltpu.VMEM((Z, PLANE * 2, D // 2), BF16),
        pltpu.VMEM((PLANE, Z * 2, D // 2), BF16),
        pltpu.VMEM((PLANE, Z * 2, D // 2), BF16),
        pltpu.VMEM((Z, PLANE * 2, D), BF16),
        pltpu.VMEM((Z, PLANE * 2, D), BF16),
        pltpu.VMEM((PLANE, Z * 2, D), BF16),
        pltpu.VMEM((PLANE, Z * 2, D), BF16),
        pltpu.VMEM((EDGE, BANDS * GROUP), BF16),
        pltpu.VMEM((EDGE, D), BF16),
        pltpu.VMEM((BANDS, GROUP, D), F32),
        pltpu.VMEM((Y, X * ROWS + 16, COLS), BF16),
        pltpu.VMEM((Y, X * ROWS + 16, COLS), BF16),
        pltpu.VMEM((X, ROWS, D), BF16),
        pltpu.VMEM((X, ROWS, D), BF16),
        pltpu.VMEM((X, ROWS + 16, COLS), BF16),
        pltpu.VMEM((X, ROWS + 16, COLS), BF16),
        pltpu.VMEM((Y, ROWS, COLS), BF16),
        pltpu.VMEM((Y, ROWS, COLS), BF16),
        pltpu.VMEM((BANDS, PLANE, OWN_PAD, COLS), BF16),
        pltpu.VMEM((Z, OWN_PAD, COLS), BF16),
        pltpu.VMEM((OWN_PAD, COLS), F32),
        pltpu.VMEM((Y, OWN_PAD, COLS), F32),
        pltpu.VMEM((8, D), F32),
        pltpu.VMEM((8, D), F32),
        pltpu.SemaphoreType.DMA((16,)),
        pltpu.SemaphoreType.DMA((STEPS,)),
        pltpu.SemaphoreType.DMA((STEPS,)),
    ]
    shapes = (
        jax.ShapeDtypeStruct((NODE, D), BF16),
        jax.ShapeDtypeStruct((NODE, D), BF16),
        jax.ShapeDtypeStruct((EDGE, D), BF16),
        jax.ShapeDtypeStruct((OWN, D), F32),
        jax.ShapeDtypeStruct((1, D), F32),
        jax.ShapeDtypeStruct((1, D), F32),
    )
    results = pl.pallas_call(
        functools.partial(kernel, (Z, X, Y, D, NODE, EDGE)),
        out_shape=shapes,
        in_specs=[anywhere] * 9 + [smem] * 2,
        out_specs=(anywhere,) * 6,
        scratch_shapes=scratch,
        compiler_params=pltpu.CompilerParams(
            collective_id=0, has_side_effects=True, vmem_limit_bytes=VMEM_BYTES
        ),
        name="edge_update",
    )(
        node_latents[0],
        outgoing,
        edge_latents[0],
        w_in,
        bias.reshape(1, D),
        receivers.reshape(1, EDGE),
        node_cotangent[0],
        senders.reshape(1, EDGE),
        gain.reshape(1, D),
        node_count,
        edge_count,
    )
    new_nodes, grad_nodes, grad_edges, grad_weights, grad_bias, grad_gain = pl.pallas_call(
        copy_out,
        out_shape=shapes,
        in_specs=[anywhere] * 6,
        out_specs=(anywhere,) * 6,
        scratch_shapes=[pltpu.VMEM(s.shape, s.dtype) for s in shapes]
        + [pltpu.SemaphoreType.DMA((12,))],
        compiler_params=pltpu.CompilerParams(vmem_limit_bytes=VMEM_BYTES),
        name="copy_out",
    )(*results)
    return (
        new_nodes[None],
        grad_nodes[None],
        grad_edges[None],
        grad_weights,
        grad_bias.reshape(D),
        grad_gain.reshape(D),
    )


def solution(mesh, x_chips=4):
    Y = mesh.shape["member"]
    Z = mesh.shape["dom"] // (x_chips * CORES)
    return jax.shard_map(
        functools.partial(shards, Z, x_chips, Y),
        mesh=mesh,
        in_specs=(
            P("member", "dom", None),
            P("member", "dom", None),
            P("member", "dom", None),
            P(),
            P(),
            P(),
            P("dom"),
            P("dom"),
            P("dom", None, None),
            P("dom"),
            P("dom"),
        ),
        out_specs=(
            P("member", "dom", None),
            P("member", "dom", None),
            P("member", "dom", None),
            P("dom", None),
            P(),
            P(),
        ),
        check_vma=False,
    )
```

```python
import functools

import jax
import jax.numpy as jnp
from jax import lax
from jax.experimental import pallas as pl
from jax.experimental.pallas import tpu as pltpu
from jax.sharding import PartitionSpec as P

epsilon = 1e-05
CORES = 2
LANES = 128
VMEM_BYTES = 63 * 1024 * 1024
F32 = jnp.float32
BF16 = jnp.bfloat16

FWD_PLANE, FWD_LINE, BWD_LINE, BWD_PLANE, FIRST_A, FIRST_B, SECOND_A, SECOND_B, OWNER, FINAL_Y = range(10)
PAIR_SUMS, PAIR_EARLY, PAIR_LATE, PAIR_P = range(10, 14)
FWD_LINE_B, FWD_PLANE_B = range(14, 16)
STEPS = 16


def dot(left, right):
    return jnp.dot(left, right, preferred_element_type=F32)


def contract_rows(left, right):
    return lax.dot_general(left, right, (((0,), (0,)), ((), ())), preferred_element_type=F32)


def apply_transpose(left, right):
    return lax.dot_general(left, right, (((1,), (1,)), ((), ())), preferred_element_type=F32)


def one_hot_rows(rows, index):
    return lax.broadcasted_iota(jnp.int32, (rows, index.shape[1]), 0) == index


def total(ref, count):
    acc = ref[0].astype(F32)
    for slot in range(1, count):
        acc = acc + ref[slot].astype(F32)
    return acc


def two_terms(pair, rows):
    high = pair.astype(BF16).astype(F32)
    zeros = [jnp.zeros((rows - 4, pair.shape[1]), F32)] if rows > 4 else []
    return jnp.concatenate([high, pair - high] + zeros, axis=0)


def split_transpose(rows, weights):
    high = rows.astype(BF16)
    low = (rows - high.astype(F32)).astype(BF16)
    return apply_transpose(high, weights) + apply_transpose(low, weights)


def wrap(index, count):
    return jnp.where(index >= count, index - count, index)


def kernel(
    sizes,
    nodes_hbm,
    outgoing_hbm,
    edges_hbm,
    w_hbm,
    bias_hbm,
    recv_hbm,
    cot_hbm,
    send_hbm,
    gain_hbm,
    node_count_ref,
    edge_count_ref,
    new_nodes_hbm,
    grad_nodes_hbm,
    grad_edges_hbm,
    fin_y,
    nodes_ref,
    outgoing_ref,
    bias_ref,
    recv_ref,
    cot_ref,
    send_ref,
    gain_ref,
    new_nodes_ref,
    grad_nodes_ref,
    w_ref,
    x_ref,
    pre_ref,
    up_ref,
    p_ref,
    ne_ref,
    ge_ref,
    outa,
    fwd1,
    fwd2,
    table,
    outb,
    mid1,
    mid2,
    table_b,
    bwd0,
    bwd1,
    bwd2,
    back,
    pair_x,
    pair_p,
    wt,
    a1,
    a1_in,
    b1,
    b1_in,
    a2,
    a2_in,
    b2,
    b2_in,
    zw,
    zw_in,
    fin,
    table_pick,
    table_pick_b,
    sums,
    sums_in,
    local_sem,
    send_sem,
    recv_sem,
):
    Z, X, Y, D, NODE, EDGE = sizes
    PLANE = X * CORES
    TABLE = Z * PLANE * 2
    ROWS = 3 * D // Z
    OWN = ROWS // PLANE
    GROUP = X * ROWS
    BANDS = Z // X // CORES
    dom = lax.axis_index("dom")
    y = lax.axis_index("member")
    z = dom // PLANE
    plane = dom % PLANE
    x = plane // CORES
    core = plane % CORES

    def remote(src, dst, step, to_dom, to_y):
        return pltpu.make_async_remote_copy(
            src_ref=src,
            dst_ref=dst,
            send_sem=send_sem.at[step],
            recv_sem=recv_sem.at[step],
            device_id={"dom": to_dom, "member": to_y},
            device_id_type=pl.DeviceIdType.MESH,
        )

    def arrived(ref, step):
        pltpu.make_async_copy(ref, ref, recv_sem.at[step]).wait()

    def sent(ref, step):
        pltpu.make_async_copy(ref, ref, send_sem.at[step]).wait()

    def each_plane(act):
        def body(i, carry):
            peer = wrap(plane + 1 + lax.rem(i + PLANE // 2 - 1, PLANE - 1), PLANE)
            act(peer, z * PLANE + peer)
            return carry

        lax.fori_loop(0, PLANE - 1, body, 0, unroll=True)

    def each_line(act):
        def body(i, carry):
            off = Z // 2 + (1 - 2 * lax.rem(i, 2)) * ((i + 1) // 2)
            peer = wrap(z + off, Z)
            act(peer, peer * PLANE + plane)
            return carry

        lax.fori_loop(0, Z - 1, body, 0, unroll=True)

    def each_x(act):
        def body(i, carry):
            peer = wrap(x + 1 + i, X)
            act(peer, z * PLANE + peer * CORES + core)
            return carry

        lax.fori_loop(0, X - 1, body, 0, unroll=True)

    def each_y(act):
        def body(i, carry):
            act(wrap(y + 1 + i, Y))
            return carry

        lax.fori_loop(0, Y - 1, body, 0, unroll=True)

    loads = [
        pltpu.make_async_copy(src, dst, local_sem.at[i])
        for i, (src, dst) in enumerate(
            (
                (nodes_hbm, nodes_ref),
                (outgoing_hbm, outgoing_ref),
                (recv_hbm, recv_ref),
                (cot_hbm, cot_ref),
                (edges_hbm, x_ref.at[:, pl.ds(2 * D, D)]),
                (w_hbm.at[pl.ds(D, 2 * D)], w_ref.at[pl.ds(D, 2 * D)]),
                (bias_hbm, bias_ref),
                (send_hbm, send_ref),
                (gain_hbm, gain_ref),
                (w_hbm.at[pl.ds(0, D)], w_ref.at[pl.ds(0, D)]),
            )
        )
    ]
    stores = [
        pltpu.make_async_copy(src, dst, local_sem.at[len(loads) + i])
        for i, (src, dst) in enumerate(
            (
                (ge_ref, grad_edges_hbm),
                (new_nodes_ref, new_nodes_hbm),
                (grad_nodes_ref, grad_nodes_hbm),
                (fin, fin_y.at[y]),
            )
        )
    ]
    pending = []

    def finish():
        for wait in pending:
            wait()

    def store(i):
        stores[i].start()
        pending.append(stores[i].wait)

    for load in loads[:2]:
        load.start()

    barrier = pltpu.get_barrier_semaphore()

    def greet(to_dom, to_y):
        pl.semaphore_signal(
            barrier,
            inc=1,
            device_id={"dom": to_dom, "member": to_y},
            device_id_type=pl.DeviceIdType.MESH,
        )

    each_plane(lambda peer, to: greet(to, y))
    each_line(lambda peer, to: greet(to, y))
    each_y(lambda peer: greet(dom, peer))

    feeder = lax.rem(z, X) * CORES + z // X // BANDS
    feeds_self = feeder == plane

    for load in loads[2:]:
        load.start()

    parts = Z * PLANE
    width = PLANE * 2
    left, right = slice(0, D // 2), slice(D // 2, D)
    given = lax.broadcasted_iota(jnp.int32, (TABLE, TABLE), 0)
    placed = lax.broadcasted_iota(jnp.int32, (TABLE, TABLE), 1)
    slots = (placed % 2) * parts
    reorder = (given == slots + (placed // 2 % Z) * PLANE + placed // (2 * Z)).astype(BF16)
    in_order = (given == slots + placed // 2).astype(BF16)
    for load in loads[:2]:
        load.wait()
    nodes = nodes_ref[...]
    outgoing = outgoing_ref[...]
    slot_hot = jnp.concatenate([one_hot_rows(NODE, outgoing[k : k + 1]) for k in range(2)], axis=1)
    slot_hot = slot_hot.astype(BF16)
    order_hot = dot(slot_hot, in_order).astype(BF16)
    outb[...] = contract_rows(order_hot, nodes[:, right]).astype(BF16).reshape(Z, width, D // 2)
    out_hot = dot(slot_hot, reorder).astype(BF16)
    outa[...] = contract_rows(out_hot, nodes[:, left]).astype(BF16).reshape(PLANE, Z * 2, D // 2)

    pl.semaphore_wait(
        barrier,
        (PLANE - 1) + (Z - 1) + (Y - 1),
    )

    each_line(lambda peer, to: remote(outb.at[peer], mid1.at[z], FWD_LINE_B, to, y).start())
    pending.append(lambda: sent(outb.at[pl.ds(0, Z - 1)], FWD_LINE_B))
    each_plane(lambda peer, to: remote(outa.at[peer], fwd1.at[plane], FWD_PLANE, to, y).start())
    pending.append(lambda: sent(outa.at[pl.ds(0, PLANE - 1)], FWD_PLANE))
    mid1[z] = outb[z]
    fwd1[plane] = outa[plane]

    live = lax.broadcasted_iota(jnp.int32, (NODE, EDGE), 1) < edge_count_ref[0]
    for load in loads[2:]:
        load.wait()
    incidence = (one_hot_rows(NODE, recv_ref[...]) & live).astype(BF16)
    x_ref[:, D : 2 * D] = contract_rows(incidence, nodes).astype(BF16)
    up_ref[...] = contract_rows(incidence, cot_ref[...])
    partner = z * PLANE + x * CORES + (1 - core)
    early = remote(
        x_ref.at[:, pl.ds(pl.multiple_of(D + (1 - core) * (D // 2), LANES), D // 2)],
        pair_x.at[:, pl.ds(pl.multiple_of(core * D, LANES), D // 2)],
        PAIR_EARLY,
        partner,
        y,
    )
    early.start()
    pending.append(early.wait_send)
    pre_ref[...] = dot(x_ref[:, D:], w_ref[D:, :]) + bias_ref[...]

    to_row = lax.broadcasted_iota(jnp.int32, (TABLE, TABLE), 0)
    from_row = lax.broadcasted_iota(jnp.int32, (TABLE, TABLE), 1)
    source = ((to_row % width) // 2) * (Z * 2) + (to_row // width) * 2 + to_row % 2
    regroup = (source == from_row).astype(BF16)
    back_source = ((to_row % (Z * 2)) // 2) * width + (to_row // (Z * 2)) * 2 + to_row % 2
    ungroup = (back_source == from_row).astype(BF16)

    arrived(fwd1.at[pl.ds(0, PLANE - 1)], FWD_PLANE)
    fwd2[...] = dot(regroup, fwd1[...].reshape(TABLE, D // 2)).astype(BF16).reshape(Z, width, D // 2)
    each_line(lambda peer, to: remote(fwd2.at[peer], table.at[z], FWD_LINE, to, y).start())
    pending.append(lambda: sent(fwd2.at[pl.ds(0, Z - 1)], FWD_LINE))
    table[z] = fwd2[z]

    senders = send_ref[...]
    own_hot = one_hot_rows(NODE, senders).astype(BF16)
    table_hot = one_hot_rows(TABLE, senders - NODE).astype(BF16)
    table_pick[...] = table_hot.astype(F32).T.astype(BF16)
    table_pick_b[...] = dot(table_pick[...], regroup).astype(BF16)
    own_rows = contract_rows(own_hot, nodes)

    arrived(mid1.at[pl.ds(0, Z - 1)], FWD_LINE_B)
    swapped = dot(ungroup, mid1[...].reshape(TABLE, D // 2)).astype(BF16)
    mid2[...] = swapped.reshape(PLANE, Z * 2, D // 2)
    each_plane(lambda peer, to: remote(mid2.at[peer], table_b.at[plane], FWD_PLANE_B, to, y).start())
    pending.append(lambda: sent(mid2.at[pl.ds(0, PLANE - 1)], FWD_PLANE_B))
    table_b[plane] = mid2[plane]

    arrived(table_b.at[pl.ds(0, PLANE - 1)], FWD_PLANE_B)
    theirs = dot(table_pick_b[...], table_b[...].reshape(TABLE, D // 2))
    x_ref[:, right] = (own_rows[:, right] + theirs).astype(BF16)
    arrived(table.at[pl.ds(0, Z - 1)], FWD_LINE)
    theirs = dot(table_pick[...], table[...].reshape(TABLE, D // 2))
    x_ref[:, left] = (own_rows[:, left] + theirs).astype(BF16)
    late = remote(
        x_ref.at[:, pl.ds(pl.multiple_of((1 - core) * 2 * D, LANES), D)],
        pair_x.at[:, pl.ds(pl.multiple_of((1 - core) * (D // 2), LANES), D)],
        PAIR_LATE,
        partner,
        y,
    )
    late.start()
    pending.append(late.wait_send)
    pre_ref[...] += dot(x_ref[:, 0:D], w_ref[0:D, :])

    gain = gain_ref[...]
    bias_term = jnp.zeros((1, D), F32)
    gain_term = jnp.zeros((1, D), F32)
    chunk = EDGE // 4
    for start in range(0, EDGE, chunk):
        rows = slice(start, start + chunk)
        preact = pre_ref[rows, :]
        upstream = up_ref[rows, :]
        sigmoid = jax.nn.sigmoid(preact)
        activated = preact * sigmoid
        average = jnp.mean(activated, axis=1, keepdims=True)
        centred = activated - average
        variance = jnp.mean(centred * centred, axis=1, keepdims=True)
        inverse = lax.rsqrt(variance + epsilon)
        normed = centred * inverse
        ne_ref[rows, :] = (x_ref[rows, 2 * D :].astype(F32) + normed * gain).astype(BF16)
        gain_term += jnp.sum(upstream * normed, axis=0, keepdims=True)
        normed_grad = upstream * gain
        activated_grad = inverse * (
            normed_grad
            - jnp.mean(normed_grad, axis=1, keepdims=True)
            - normed * jnp.mean(normed_grad * normed, axis=1, keepdims=True)
        )
        preact_grad = (activated_grad * sigmoid * (1.0 + preact * (1.0 - sigmoid))).astype(BF16)
        p_ref[rows, :] = preact_grad
        near = pl.ds(start, chunk)
        remote(p_ref.at[near], pair_p.at[near], PAIR_P, partner, y).start()
        bias_term += jnp.sum(preact_grad.astype(F32), axis=0, keepdims=True)

    pending.append(lambda: sent(p_ref, PAIR_P))

    sums[...] = jnp.concatenate([bias_term, gain_term, jnp.zeros((6, D), F32)], axis=0)
    pair_sums = remote(sums, sums_in, PAIR_SUMS, partner, y)
    pair_sums.start()
    pending.append(pair_sums.wait_send)
    grad = p_ref[...]
    bwd0[...] = dot(table_hot, grad).astype(BF16).reshape(Z, width, D)
    each_line(lambda peer, to: remote(bwd0.at[peer], bwd1.at[z], BWD_LINE, to, y).start())
    pending.append(lambda: sent(bwd0.at[pl.ds(0, Z - 1)], BWD_LINE))
    bwd1[z] = bwd0[z]

    half = core * (BANDS * GROUP)
    for j in range(BANDS):
        cols = pl.ds(pl.multiple_of(half + j * GROUP, LANES), GROUP)
        wt[j] = contract_rows(x_ref[:, cols], grad)
    early.wait_recv()
    late.wait_recv()
    arrived(pair_p, PAIR_P)
    pair_sums.wait_recv()
    other_grad = pair_p[...]

    def band(j):
        term = wt[j] + contract_rows(pair_x[:, j * GROUP : (j + 1) * GROUP], other_grad)
        return term.astype(BF16).reshape(X, ROWS, D)

    term = band(0)
    pair_terms = two_terms(sums[0:2] + sums_in[0:2], 16).astype(BF16)
    for to in range(Y):
        cols = slice(to * (D // Y), (to + 1) * (D // Y))
        a1[to, 0 : X * ROWS] = term[:, :, cols].reshape(X * ROWS, D // Y)
        a1[to, X * ROWS :] = pair_terms[:, cols]
    each_y(lambda peer: remote(a1.at[peer], a1_in.at[y], FIRST_A, dom, peer).start())
    pending.append(lambda: sent(a1.at[pl.ds(0, Y - 1)], FIRST_A))
    a1_in[y] = a1[y]
    b1[...] = band(1)
    each_x(lambda peer, to: remote(b1.at[peer], b1_in.at[x], FIRST_B, to, y).start())
    pending.append(lambda: sent(b1.at[pl.ds(0, X - 1)], FIRST_B))
    b1_in[x] = b1[x]

    ge_ref[...] = (up_ref[...] + apply_transpose(grad, w_ref[2 * D :, :])).astype(BF16)
    store(0)
    new_nodes_ref[...] = (nodes.astype(F32) + dot(incidence, ne_ref[...])).astype(BF16)
    store(1)

    arrived(a1_in.at[pl.ds(0, Y - 1)], FIRST_A)
    summed = total(a1_in, Y)
    terms = summed[X * ROWS :]
    terms = two_terms(terms[0:2] + terms[2:4], 16).astype(BF16)
    summed = summed[0 : X * ROWS].astype(BF16)
    for to in range(X):
        a2[to, 0:ROWS] = summed[to * ROWS : (to + 1) * ROWS]
        a2[to, ROWS:] = terms
    each_x(lambda peer, to: remote(a2.at[peer], a2_in.at[x], SECOND_A, to, y).start())
    pending.append(lambda: sent(a2.at[pl.ds(0, X - 1)], SECOND_A))
    a2_in[x] = a2[x]
    arrived(b1_in.at[pl.ds(0, X - 1)], FIRST_B)
    summed = total(b1_in, X).astype(BF16)
    for to in range(Y):
        b2[to] = summed[:, to * (D // Y) : (to + 1) * (D // Y)]
    each_y(lambda peer: remote(b2.at[peer], b2_in.at[y], SECOND_B, dom, peer).start())
    pending.append(lambda: sent(b2.at[pl.ds(0, Y - 1)], SECOND_B))
    b2_in[y] = b2[y]

    node_live = lax.broadcasted_iota(jnp.int32, (NODE, D), 0) < node_count_ref[0]
    node_grad = jnp.where(node_live, cot_ref[...].astype(F32), 0.0)
    node_grad += split_transpose(dot(incidence, grad), w_ref[D : 2 * D, :])
    own_sum = dot(own_hot, grad)

    def pieces(j, rows, pad):
        for piece in range(PLANE):
            block = rows[piece * OWN : (piece + 1) * OWN, :]
            zw[j, piece] = jnp.concatenate([block, pad], axis=0).astype(BF16)

    def each_owner(j, act):
        def body(i, carry):
            piece = wrap(i + wrap(plane + 1, PLANE), PLANE)
            to = ((core * BANDS + j) * X + x) * PLANE + piece

            @pl.when(to != dom)
            def _():
                act(remote(zw.at[j, piece], zw_in.at[z], OWNER, to, y))

            return carry

        lax.fori_loop(0, PLANE, body, 0, unroll=True)

    arrived(a2_in.at[pl.ds(0, X - 1)], SECOND_A)
    rows = total(a2_in, X)
    terms = rows[ROWS:]
    pad = two_terms(terms[0:2] + terms[2:4], zw.shape[2] - OWN)
    pieces(0, rows, pad)
    each_owner(0, lambda copy: copy.start())
    arrived(b2_in.at[pl.ds(0, Y - 1)], SECOND_B)
    pieces(1, total(b2_in, Y), pad)
    each_owner(1, lambda copy: copy.start())
    for j in range(BANDS):
        pending.append(lambda j=j: each_owner(j, lambda copy: copy.wait_send()))

    @pl.when(feeds_self)
    def _():
        zw_in[z] = zw[lax.rem(z // X, BANDS), plane]

    arrived(bwd1.at[pl.ds(0, Z - 1)], BWD_LINE)
    bwd2[...] = (
        dot(ungroup, bwd1[...].reshape(TABLE, D)).astype(BF16).reshape(PLANE, Z * 2, D)
    )
    each_plane(lambda peer, to: remote(bwd2.at[peer], back.at[plane], BWD_PLANE, to, y).start())
    pending.append(lambda: sent(bwd2.at[pl.ds(0, PLANE - 1)], BWD_PLANE))
    back[plane] = bwd2[plane]

    @pl.when(feeds_self)
    def _():
        arrived(zw_in.at[pl.ds(0, Z - 1)], OWNER)

    @pl.when(jnp.logical_not(feeds_self))
    def _():
        arrived(zw_in, OWNER)

    fin[...] = total(zw_in, Z)
    each_y(lambda peer: remote(fin, fin_y.at[y], FINAL_Y, dom, peer).start())
    pending.append(lambda: sent(fin_y.at[pl.ds(0, Y - 1)], FINAL_Y))
    store(3)

    arrived(back.at[pl.ds(0, PLANE - 1)], BWD_PLANE)
    own_sum += dot(out_hot, back[...].reshape(TABLE, D))
    grad_nodes_ref[...] = (node_grad + split_transpose(own_sum, w_ref[0:D, :])).astype(BF16)
    store(2)

    arrived(fin_y.at[pl.ds(0, Y - 1)], FINAL_Y)
    finish()


def copy_out(*refs):
    source, result, held, built, sems = refs[:4], refs[4:10], refs[10:14], refs[14:17], refs[17]
    loads = [pltpu.make_async_copy(source[i], held[i], sems.at[i]) for i in range(4)]
    whole = tuple(held[:3]) + tuple(built)
    stores = [pltpu.make_async_copy(whole[i], result[i], sems.at[4 + i]) for i in range(6)]
    for load in loads:
        load.start()
    for i in range(3):
        loads[i].wait()
        stores[i].start()
    loads[3].wait()
    pieces = held[3]
    gw_ref, gb_ref, gg_ref = built
    count, _, width = pieces.shape
    own = gw_ref.shape[0]
    for i in range(count):
        cols = slice(i * width, (i + 1) * width)
        gw_ref[:, cols] = pieces[i, 0:own, :]
        terms = pieces[i, own : own + 2, :] + pieces[i, own + 2 : own + 4, :]
        gb_ref[:, cols] = terms[0:1]
        gg_ref[:, cols] = terms[1:2]
    for store in stores[3:]:
        store.start()
    for store in stores:
        store.wait()


def shards(
    Z,
    X,
    Y,
    node_latents,
    edge_latents,
    node_cotangent,
    w_in,
    bias,
    gain,
    receivers,
    senders,
    send_rows,
    node_count,
    edge_count,
):
    _, NODE, D = node_latents.shape
    EDGE = edge_latents.shape[1]
    PLANE = X * CORES
    TABLE = Z * PLANE * 2
    ROWS = 3 * D // Z
    OWN = ROWS // PLANE
    GROUP = X * ROWS
    BANDS = Z // X // CORES
    OWN_PAD = (OWN + 4 + 15) // 16 * 16
    COLS = D // Y
    outgoing = send_rows[0].T

    anywhere = pl.BlockSpec(memory_space=pl.ANY)
    smem = pl.BlockSpec(memory_space=pltpu.SMEM)
    scratch = [
        pltpu.VMEM((NODE, D), BF16),
        pltpu.VMEM((2, Z * PLANE), jnp.int32),
        pltpu.VMEM((1, D), F32),
        pltpu.VMEM((1, EDGE), jnp.int32),
        pltpu.VMEM((NODE, D), BF16),
        pltpu.VMEM((1, EDGE), jnp.int32),
        pltpu.VMEM((1, D), F32),
        pltpu.VMEM((NODE, D), BF16),
        pltpu.VMEM((NODE, D), BF16),
        pltpu.VMEM((3 * D, D), BF16),
        pltpu.VMEM((EDGE, 3 * D), BF16),
        pltpu.VMEM((EDGE, D), F32),
        pltpu.VMEM((EDGE, D), F32),
        pltpu.VMEM((EDGE, D), BF16),
        pltpu.VMEM((EDGE, D), BF16),
        pltpu.VMEM((EDGE, D), BF16),
        pltpu.VMEM((PLANE, Z * 2, D // 2), BF16),
        pltpu.VMEM((PLANE, Z * 2, D // 2), BF16),
        pltpu.VMEM((Z, PLANE * 2, D // 2), BF16),
        pltpu.VMEM((Z, PLANE * 2, D // 2), BF16),
        pltpu.VMEM((Z, PLANE * 2, D // 2), BF16),
        pltpu.VMEM((Z, PLANE * 2, D // 2), BF16),
        pltpu.VMEM((PLANE, Z * 2, D // 2), BF16),
        pltpu.VMEM((PLANE, Z * 2, D // 2), BF16),
        pltpu.VMEM((Z, PLANE * 2, D), BF16),
        pltpu.VMEM((Z, PLANE * 2, D), BF16),
        pltpu.VMEM((PLANE, Z * 2, D), BF16),
        pltpu.VMEM((PLANE, Z * 2, D), BF16),
        pltpu.VMEM((EDGE, BANDS * GROUP), BF16),
        pltpu.VMEM((EDGE, D), BF16),
        pltpu.VMEM((BANDS, GROUP, D), F32),
        pltpu.VMEM((Y, X * ROWS + 16, COLS), BF16),
        pltpu.VMEM((Y, X * ROWS + 16, COLS), BF16),
        pltpu.VMEM((X, ROWS, D), BF16),
        pltpu.VMEM((X, ROWS, D), BF16),
        pltpu.VMEM((X, ROWS + 16, COLS), BF16),
        pltpu.VMEM((X, ROWS + 16, COLS), BF16),
        pltpu.VMEM((Y, ROWS, COLS), BF16),
        pltpu.VMEM((Y, ROWS, COLS), BF16),
        pltpu.VMEM((BANDS, PLANE, OWN_PAD, COLS), BF16),
        pltpu.VMEM((Z, OWN_PAD, COLS), BF16),
        pltpu.VMEM((OWN_PAD, COLS), F32),
        pltpu.VMEM((EDGE, TABLE), BF16),
        pltpu.VMEM((EDGE, TABLE), BF16),
        pltpu.VMEM((8, D), F32),
        pltpu.VMEM((8, D), F32),
        pltpu.SemaphoreType.DMA((16,)),
        pltpu.SemaphoreType.DMA((STEPS,)),
        pltpu.SemaphoreType.DMA((STEPS,)),
    ]
    shapes = (
        jax.ShapeDtypeStruct((NODE, D), BF16),
        jax.ShapeDtypeStruct((NODE, D), BF16),
        jax.ShapeDtypeStruct((EDGE, D), BF16),
        jax.ShapeDtypeStruct((OWN, D), F32),
        jax.ShapeDtypeStruct((1, D), F32),
        jax.ShapeDtypeStruct((1, D), F32),
    )
    parts = shapes[:3] + (jax.ShapeDtypeStruct((Y, OWN_PAD, COLS), F32),)
    results = pl.pallas_call(
        functools.partial(kernel, (Z, X, Y, D, NODE, EDGE)),
        out_shape=parts,
        in_specs=[anywhere] * 9 + [smem] * 2,
        out_specs=(anywhere,) * 4,
        scratch_shapes=scratch,
        compiler_params=pltpu.CompilerParams(
            collective_id=0, has_side_effects=True, vmem_limit_bytes=VMEM_BYTES
        ),
        name="edge_update",
    )(
        node_latents[0],
        outgoing,
        edge_latents[0],
        w_in,
        bias.reshape(1, D),
        receivers.reshape(1, EDGE),
        node_cotangent[0],
        senders.reshape(1, EDGE),
        gain.reshape(1, D),
        node_count,
        edge_count,
    )
    new_nodes, grad_nodes, grad_edges, grad_weights, grad_bias, grad_gain = pl.pallas_call(
        copy_out,
        out_shape=shapes,
        in_specs=[anywhere] * 4,
        out_specs=(anywhere,) * 6,
        scratch_shapes=[pltpu.VMEM(s.shape, s.dtype) for s in parts + shapes[3:]]
        + [pltpu.SemaphoreType.DMA((10,))],
        compiler_params=pltpu.CompilerParams(vmem_limit_bytes=VMEM_BYTES),
        name="copy_out",
    )(*results)
    return (
        new_nodes[None],
        grad_nodes[None],
        grad_edges[None],
        grad_weights,
        grad_bias.reshape(D),
        grad_gain.reshape(D),
    )


def solution(mesh, x_chips=4):
    Y = mesh.shape["member"]
    Z = mesh.shape["dom"] // (x_chips * CORES)
    return jax.shard_map(
        functools.partial(shards, Z, x_chips, Y),
        mesh=mesh,
        in_specs=(
            P("member", "dom", None),
            P("member", "dom", None),
            P("member", "dom", None),
            P(),
            P(),
            P(),
            P("dom"),
            P("dom"),
            P("dom", None, None),
            P("dom"),
            P("dom"),
        ),
        out_specs=(
            P("member", "dom", None),
            P("member", "dom", None),
            P("member", "dom", None),
            P("dom", None),
            P(),
            P(),
        ),
        check_vma=False,
    )
```

```python
import functools

import jax
import jax.numpy as jnp
from jax import lax
from jax.experimental import pallas as pl
from jax.experimental.pallas import tpu as pltpu
from jax.sharding import PartitionSpec as P

epsilon = 1e-05
CORES = 2
LANES = 128
VMEM_BYTES = 63 * 1024 * 1024
F32 = jnp.float32
BF16 = jnp.bfloat16

FWD_PLANE, FWD_LINE, BWD_LINE, BWD_PLANE, FIRST_A, FIRST_B, SECOND_A, SECOND_B, OWNER, FINAL_Y = range(10)
PAIR_SUMS, PAIR_EARLY, PAIR_LATE, PAIR_P = range(10, 14)
FWD_LINE_B, FWD_PLANE_B = range(14, 16)
STEPS = 16


def dot(left, right):
    return jnp.dot(left, right, preferred_element_type=F32)


def contract_rows(left, right):
    return lax.dot_general(left, right, (((0,), (0,)), ((), ())), preferred_element_type=F32)


def apply_transpose(left, right):
    return lax.dot_general(left, right, (((1,), (1,)), ((), ())), preferred_element_type=F32)


def one_hot_rows(rows, index):
    return lax.broadcasted_iota(jnp.int32, (rows, index.shape[1]), 0) == index


def total(ref, count):
    acc = ref[0].astype(F32)
    for slot in range(1, count):
        acc = acc + ref[slot].astype(F32)
    return acc


def two_terms(pair, rows):
    high = pair.astype(BF16).astype(F32)
    zeros = [jnp.zeros((rows - 4, pair.shape[1]), F32)] if rows > 4 else []
    return jnp.concatenate([high, pair - high] + zeros, axis=0)


def split_transpose(rows, weights):
    high = rows.astype(BF16)
    low = (rows - high.astype(F32)).astype(BF16)
    return apply_transpose(high, weights) + apply_transpose(low, weights)


def wrap(index, count):
    return jnp.where(index >= count, index - count, index)


def kernel(
    sizes,
    nodes_hbm,
    outgoing_hbm,
    edges_hbm,
    w_hbm,
    bias_hbm,
    recv_hbm,
    cot_hbm,
    send_hbm,
    gain_hbm,
    node_count_ref,
    edge_count_ref,
    new_nodes_hbm,
    grad_nodes_hbm,
    grad_edges_hbm,
    fin_y,
    nodes_ref,
    outgoing_ref,
    bias_ref,
    recv_ref,
    cot_ref,
    send_ref,
    gain_ref,
    new_nodes_ref,
    grad_nodes_ref,
    w_ref,
    x_ref,
    pre_ref,
    up_ref,
    p_ref,
    ne_ref,
    ge_ref,
    outa,
    fwd1,
    fwd2,
    table,
    outb,
    mid1,
    mid2,
    table_b,
    bwd0,
    bwd1,
    bwd2,
    back,
    pair_x,
    pair_p,
    wt,
    a1,
    a1_in,
    b1,
    b1_in,
    a2,
    a2_in,
    b2,
    b2_in,
    zw,
    zw_in,
    fin,
    table_pick,
    table_pick_b,
    sums,
    sums_in,
    local_sem,
    send_sem,
    recv_sem,
):
    Z, X, Y, D, NODE, EDGE = sizes
    PLANE = X * CORES
    TABLE = Z * PLANE * 2
    ROWS = 3 * D // Z
    OWN = ROWS // PLANE
    GROUP = X * ROWS
    BANDS = Z // X // CORES
    dom = lax.axis_index("dom")
    y = lax.axis_index("member")
    z = dom // PLANE
    plane = dom % PLANE
    x = plane // CORES
    core = plane % CORES

    def remote(src, dst, step, to_dom, to_y):
        return pltpu.make_async_remote_copy(
            src_ref=src,
            dst_ref=dst,
            send_sem=send_sem.at[step],
            recv_sem=recv_sem.at[step],
            device_id={"dom": to_dom, "member": to_y},
            device_id_type=pl.DeviceIdType.MESH,
        )

    def arrived(ref, step):
        pltpu.make_async_copy(ref, ref, recv_sem.at[step]).wait()

    def sent(ref, step):
        pltpu.make_async_copy(ref, ref, send_sem.at[step]).wait()

    def each_plane(act):
        def body(i, carry):
            peer = wrap(plane + 1 + lax.rem(i + PLANE // 2 - 1, PLANE - 1), PLANE)
            act(peer, z * PLANE + peer)
            return carry

        lax.fori_loop(0, PLANE - 1, body, 0, unroll=True)

    def each_line(act):
        def body(i, carry):
            off = Z // 2 + (1 - 2 * lax.rem(i, 2)) * ((i + 1) // 2)
            peer = wrap(z + off, Z)
            act(peer, peer * PLANE + plane)
            return carry

        lax.fori_loop(0, Z - 1, body, 0, unroll=True)

    def each_x(act):
        def body(i, carry):
            peer = wrap(x + 1 + i, X)
            act(peer, z * PLANE + peer * CORES + core)
            return carry

        lax.fori_loop(0, X - 1, body, 0, unroll=True)

    def each_y(act):
        def body(i, carry):
            act(wrap(y + 1 + i, Y))
            return carry

        lax.fori_loop(0, Y - 1, body, 0, unroll=True)

    loads = [
        pltpu.make_async_copy(src, dst, local_sem.at[i])
        for i, (src, dst) in enumerate(
            (
                (nodes_hbm, nodes_ref),
                (outgoing_hbm, outgoing_ref),
                (recv_hbm, recv_ref),
                (cot_hbm, cot_ref),
                (edges_hbm, x_ref.at[:, pl.ds(2 * D, D)]),
                (w_hbm.at[pl.ds(D, 2 * D)], w_ref.at[pl.ds(D, 2 * D)]),
                (bias_hbm, bias_ref),
                (send_hbm, send_ref),
                (gain_hbm, gain_ref),
                (w_hbm.at[pl.ds(0, D)], w_ref.at[pl.ds(0, D)]),
            )
        )
    ]
    stores = [
        pltpu.make_async_copy(src, dst, local_sem.at[len(loads) + i])
        for i, (src, dst) in enumerate(
            (
                (ge_ref, grad_edges_hbm),
                (new_nodes_ref, new_nodes_hbm),
                (grad_nodes_ref, grad_nodes_hbm),
                (fin, fin_y.at[y]),
            )
        )
    ]
    pending = []

    def finish():
        for wait in pending:
            wait()

    def store(i):
        stores[i].start()
        pending.append(stores[i].wait)

    for load in loads[:2]:
        load.start()

    barrier = pltpu.get_barrier_semaphore()

    def greet(to_dom, to_y):
        pl.semaphore_signal(
            barrier,
            inc=1,
            device_id={"dom": to_dom, "member": to_y},
            device_id_type=pl.DeviceIdType.MESH,
        )

    each_plane(lambda peer, to: greet(to, y))
    each_line(lambda peer, to: greet(to, y))
    each_y(lambda peer: greet(dom, peer))

    feeder = lax.rem(z, X) * CORES + z // X // BANDS
    feeds_self = feeder == plane

    for load in loads[2:]:
        load.start()

    parts = Z * PLANE
    width = PLANE * 2
    left, right = slice(0, D // 2), slice(D // 2, D)
    given = lax.broadcasted_iota(jnp.int32, (TABLE, TABLE), 0)
    placed = lax.broadcasted_iota(jnp.int32, (TABLE, TABLE), 1)
    slots = (placed % 2) * parts
    reorder = (given == slots + (placed // 2 % Z) * PLANE + placed // (2 * Z)).astype(BF16)
    in_order = (given == slots + placed // 2).astype(BF16)
    for load in loads[:2]:
        load.wait()
    nodes = nodes_ref[...]
    outgoing = outgoing_ref[...]
    slot_hot = jnp.concatenate([one_hot_rows(NODE, outgoing[k : k + 1]) for k in range(2)], axis=1)
    slot_hot = slot_hot.astype(BF16)
    order_hot = dot(slot_hot, in_order).astype(BF16)
    outb[...] = contract_rows(order_hot, nodes[:, right]).astype(BF16).reshape(Z, width, D // 2)
    out_hot = dot(slot_hot, reorder).astype(BF16)
    outa[...] = contract_rows(out_hot, nodes[:, left]).astype(BF16).reshape(PLANE, Z * 2, D // 2)

    pl.semaphore_wait(
        barrier,
        (PLANE - 1) + (Z - 1) + (Y - 1),
    )

    each_line(lambda peer, to: remote(outb.at[peer], mid1.at[z], FWD_LINE_B, to, y).start())
    pending.append(lambda: sent(outb.at[pl.ds(0, Z - 1)], FWD_LINE_B))
    each_plane(lambda peer, to: remote(outa.at[peer], fwd1.at[plane], FWD_PLANE, to, y).start())
    pending.append(lambda: sent(outa.at[pl.ds(0, PLANE - 1)], FWD_PLANE))
    mid1[z] = outb[z]
    fwd1[plane] = outa[plane]

    live = lax.broadcasted_iota(jnp.int32, (NODE, EDGE), 1) < edge_count_ref[0]
    for load in loads[2:]:
        load.wait()
    incidence = (one_hot_rows(NODE, recv_ref[...]) & live).astype(BF16)
    x_ref[:, D : 2 * D] = contract_rows(incidence, nodes).astype(BF16)
    up_ref[...] = contract_rows(incidence, cot_ref[...])
    partner = z * PLANE + x * CORES + (1 - core)
    early = remote(
        x_ref.at[:, pl.ds(pl.multiple_of(D + (1 - core) * (D // 2), LANES), D // 2)],
        pair_x.at[:, pl.ds(pl.multiple_of(core * D, LANES), D // 2)],
        PAIR_EARLY,
        partner,
        y,
    )
    early.start()
    pending.append(early.wait_send)
    pre_ref[...] = dot(x_ref[:, D:], w_ref[D:, :]) + bias_ref[...]

    to_row = lax.broadcasted_iota(jnp.int32, (TABLE, TABLE), 0)
    from_row = lax.broadcasted_iota(jnp.int32, (TABLE, TABLE), 1)
    source = ((to_row % width) // 2) * (Z * 2) + (to_row // width) * 2 + to_row % 2
    regroup = (source == from_row).astype(BF16)
    back_source = ((to_row % (Z * 2)) // 2) * width + (to_row // (Z * 2)) * 2 + to_row % 2
    ungroup = (back_source == from_row).astype(BF16)

    arrived(fwd1.at[pl.ds(0, PLANE - 1)], FWD_PLANE)
    fwd2[...] = dot(regroup, fwd1[...].reshape(TABLE, D // 2)).astype(BF16).reshape(Z, width, D // 2)
    each_line(lambda peer, to: remote(fwd2.at[peer], table.at[z], FWD_LINE, to, y).start())
    pending.append(lambda: sent(fwd2.at[pl.ds(0, Z - 1)], FWD_LINE))
    table[z] = fwd2[z]

    senders = send_ref[...]
    own_hot = one_hot_rows(NODE, senders).astype(BF16)
    table_hot = one_hot_rows(TABLE, senders - NODE).astype(BF16)
    table_pick[...] = table_hot.astype(F32).T.astype(BF16)
    table_pick_b[...] = dot(table_pick[...], regroup).astype(BF16)
    own_rows = contract_rows(own_hot, nodes)

    arrived(mid1.at[pl.ds(0, Z - 1)], FWD_LINE_B)
    swapped = dot(ungroup, mid1[...].reshape(TABLE, D // 2)).astype(BF16)
    mid2[...] = swapped.reshape(PLANE, Z * 2, D // 2)
    each_plane(lambda peer, to: remote(mid2.at[peer], table_b.at[plane], FWD_PLANE_B, to, y).start())
    pending.append(lambda: sent(mid2.at[pl.ds(0, PLANE - 1)], FWD_PLANE_B))
    table_b[plane] = mid2[plane]

    arrived(table_b.at[pl.ds(0, PLANE - 1)], FWD_PLANE_B)
    theirs = dot(table_pick_b[...], table_b[...].reshape(TABLE, D // 2))
    x_ref[:, right] = (own_rows[:, right] + theirs).astype(BF16)
    arrived(table.at[pl.ds(0, Z - 1)], FWD_LINE)
    theirs = dot(table_pick[...], table[...].reshape(TABLE, D // 2))
    x_ref[:, left] = (own_rows[:, left] + theirs).astype(BF16)
    late = remote(
        x_ref.at[:, pl.ds(pl.multiple_of((1 - core) * 2 * D, LANES), D)],
        pair_x.at[:, pl.ds(pl.multiple_of((1 - core) * (D // 2), LANES), D)],
        PAIR_LATE,
        partner,
        y,
    )
    late.start()
    pending.append(late.wait_send)
    pre_ref[...] += dot(x_ref[:, 0:D], w_ref[0:D, :])

    gain = gain_ref[...]
    bias_term = jnp.zeros((1, D), F32)
    gain_term = jnp.zeros((1, D), F32)
    chunk = EDGE // 4
    for start in range(0, EDGE, chunk):
        rows = slice(start, start + chunk)
        preact = pre_ref[rows, :]
        upstream = up_ref[rows, :]
        sigmoid = jax.nn.sigmoid(preact)
        activated = preact * sigmoid
        average = jnp.mean(activated, axis=1, keepdims=True)
        centred = activated - average
        variance = jnp.mean(centred * centred, axis=1, keepdims=True)
        inverse = lax.rsqrt(variance + epsilon)
        normed = centred * inverse
        ne_ref[rows, :] = (x_ref[rows, 2 * D :].astype(F32) + normed * gain).astype(BF16)
        gain_term += jnp.sum(upstream * normed, axis=0, keepdims=True)
        normed_grad = upstream * gain
        activated_grad = inverse * (
            normed_grad
            - jnp.mean(normed_grad, axis=1, keepdims=True)
            - normed * jnp.mean(normed_grad * normed, axis=1, keepdims=True)
        )
        preact_grad = (activated_grad * sigmoid * (1.0 + preact * (1.0 - sigmoid))).astype(BF16)
        p_ref[rows, :] = preact_grad
        near = pl.ds(start, chunk)
        remote(p_ref.at[near], pair_p.at[near], PAIR_P, partner, y).start()
        bias_term += jnp.sum(preact_grad.astype(F32), axis=0, keepdims=True)

    pending.append(lambda: sent(p_ref, PAIR_P))

    sums[...] = jnp.concatenate([bias_term, gain_term, jnp.zeros((6, D), F32)], axis=0)
    pair_sums = remote(sums, sums_in, PAIR_SUMS, partner, y)
    pair_sums.start()
    pending.append(pair_sums.wait_send)
    grad = p_ref[...]
    half = core * (BANDS * GROUP)
    for j in range(BANDS):
        cols = pl.ds(pl.multiple_of(half + j * GROUP, LANES), GROUP)
        wt[j] = contract_rows(x_ref[:, cols], grad)
    early.wait_recv()
    late.wait_recv()
    arrived(pair_p, PAIR_P)
    pair_sums.wait_recv()
    other_grad = pair_p[...]

    def band(j):
        term = wt[j] + contract_rows(pair_x[:, j * GROUP : (j + 1) * GROUP], other_grad)
        return term.astype(BF16).reshape(X, ROWS, D)

    term = band(0)
    pair_terms = two_terms(sums[0:2] + sums_in[0:2], 16).astype(BF16)
    for to in range(Y):
        cols = slice(to * (D // Y), (to + 1) * (D // Y))
        a1[to, 0 : X * ROWS] = term[:, :, cols].reshape(X * ROWS, D // Y)
        a1[to, X * ROWS :] = pair_terms[:, cols]
    each_y(lambda peer: remote(a1.at[peer], a1_in.at[y], FIRST_A, dom, peer).start())
    pending.append(lambda: sent(a1.at[pl.ds(0, Y - 1)], FIRST_A))
    a1_in[y] = a1[y]
    bwd0[...] = dot(table_hot, grad).astype(BF16).reshape(Z, width, D)
    each_line(lambda peer, to: remote(bwd0.at[peer], bwd1.at[z], BWD_LINE, to, y).start())
    pending.append(lambda: sent(bwd0.at[pl.ds(0, Z - 1)], BWD_LINE))
    bwd1[z] = bwd0[z]

    b1[...] = band(1)
    each_x(lambda peer, to: remote(b1.at[peer], b1_in.at[x], FIRST_B, to, y).start())
    pending.append(lambda: sent(b1.at[pl.ds(0, X - 1)], FIRST_B))
    b1_in[x] = b1[x]

    ge_ref[...] = (up_ref[...] + apply_transpose(grad, w_ref[2 * D :, :])).astype(BF16)
    store(0)
    new_nodes_ref[...] = (nodes.astype(F32) + dot(incidence, ne_ref[...])).astype(BF16)
    store(1)

    arrived(a1_in.at[pl.ds(0, Y - 1)], FIRST_A)
    summed = total(a1_in, Y)
    terms = summed[X * ROWS :]
    terms = two_terms(terms[0:2] + terms[2:4], 16).astype(BF16)
    summed = summed[0 : X * ROWS].astype(BF16)
    for to in range(X):
        a2[to, 0:ROWS] = summed[to * ROWS : (to + 1) * ROWS]
        a2[to, ROWS:] = terms
    each_x(lambda peer, to: remote(a2.at[peer], a2_in.at[x], SECOND_A, to, y).start())
    pending.append(lambda: sent(a2.at[pl.ds(0, X - 1)], SECOND_A))
    a2_in[x] = a2[x]
    arrived(b1_in.at[pl.ds(0, X - 1)], FIRST_B)
    summed = total(b1_in, X).astype(BF16)
    for to in range(Y):
        b2[to] = summed[:, to * (D // Y) : (to + 1) * (D // Y)]
    each_y(lambda peer: remote(b2.at[peer], b2_in.at[y], SECOND_B, dom, peer).start())
    pending.append(lambda: sent(b2.at[pl.ds(0, Y - 1)], SECOND_B))
    b2_in[y] = b2[y]

    node_live = lax.broadcasted_iota(jnp.int32, (NODE, D), 0) < node_count_ref[0]
    node_grad = jnp.where(node_live, cot_ref[...].astype(F32), 0.0)
    node_grad += split_transpose(dot(incidence, grad), w_ref[D : 2 * D, :])
    own_sum = dot(own_hot, grad)

    def pieces(j, rows, pad):
        for piece in range(PLANE):
            block = rows[piece * OWN : (piece + 1) * OWN, :]
            zw[j, piece] = jnp.concatenate([block, pad], axis=0).astype(BF16)

    def each_owner(j, act):
        def body(i, carry):
            piece = wrap(i + wrap(plane + 1, PLANE), PLANE)
            to = ((core * BANDS + j) * X + x) * PLANE + piece

            @pl.when(to != dom)
            def _():
                act(remote(zw.at[j, piece], zw_in.at[z], OWNER, to, y))

            return carry

        lax.fori_loop(0, PLANE, body, 0, unroll=True)

    arrived(a2_in.at[pl.ds(0, X - 1)], SECOND_A)
    rows = total(a2_in, X)
    terms = rows[ROWS:]
    pad = two_terms(terms[0:2] + terms[2:4], zw.shape[2] - OWN)
    pieces(0, rows, pad)
    each_owner(0, lambda copy: copy.start())
    arrived(b2_in.at[pl.ds(0, Y - 1)], SECOND_B)
    pieces(1, total(b2_in, Y), pad)
    each_owner(1, lambda copy: copy.start())
    for j in range(BANDS):
        pending.append(lambda j=j: each_owner(j, lambda copy: copy.wait_send()))

    @pl.when(feeds_self)
    def _():
        zw_in[z] = zw[lax.rem(z // X, BANDS), plane]

    arrived(bwd1.at[pl.ds(0, Z - 1)], BWD_LINE)
    bwd2[...] = (
        dot(ungroup, bwd1[...].reshape(TABLE, D)).astype(BF16).reshape(PLANE, Z * 2, D)
    )
    each_plane(lambda peer, to: remote(bwd2.at[peer], back.at[plane], BWD_PLANE, to, y).start())
    pending.append(lambda: sent(bwd2.at[pl.ds(0, PLANE - 1)], BWD_PLANE))
    back[plane] = bwd2[plane]

    @pl.when(feeds_self)
    def _():
        arrived(zw_in.at[pl.ds(0, Z - 1)], OWNER)

    @pl.when(jnp.logical_not(feeds_self))
    def _():
        arrived(zw_in, OWNER)

    fin[...] = total(zw_in, Z)
    each_y(lambda peer: remote(fin, fin_y.at[y], FINAL_Y, dom, peer).start())
    pending.append(lambda: sent(fin_y.at[pl.ds(0, Y - 1)], FINAL_Y))
    store(3)

    arrived(back.at[pl.ds(0, PLANE - 1)], BWD_PLANE)
    own_sum += dot(out_hot, back[...].reshape(TABLE, D))
    grad_nodes_ref[...] = (node_grad + split_transpose(own_sum, w_ref[0:D, :])).astype(BF16)
    store(2)

    arrived(fin_y.at[pl.ds(0, Y - 1)], FINAL_Y)
    finish()


def copy_out(*refs):
    source, result, held, built, sems = refs[:4], refs[4:10], refs[10:14], refs[14:17], refs[17]
    loads = [pltpu.make_async_copy(source[i], held[i], sems.at[i]) for i in range(4)]
    whole = tuple(held[:3]) + tuple(built)
    stores = [pltpu.make_async_copy(whole[i], result[i], sems.at[4 + i]) for i in range(6)]
    for load in loads:
        load.start()
    for i in range(3):
        loads[i].wait()
        stores[i].start()
    loads[3].wait()
    pieces = held[3]
    gw_ref, gb_ref, gg_ref = built
    count, _, width = pieces.shape
    own = gw_ref.shape[0]
    for i in range(count):
        cols = slice(i * width, (i + 1) * width)
        gw_ref[:, cols] = pieces[i, 0:own, :]
        terms = pieces[i, own : own + 2, :] + pieces[i, own + 2 : own + 4, :]
        gb_ref[:, cols] = terms[0:1]
        gg_ref[:, cols] = terms[1:2]
    for store in stores[3:]:
        store.start()
    for store in stores:
        store.wait()


def shards(
    Z,
    X,
    Y,
    node_latents,
    edge_latents,
    node_cotangent,
    w_in,
    bias,
    gain,
    receivers,
    senders,
    send_rows,
    node_count,
    edge_count,
):
    _, NODE, D = node_latents.shape
    EDGE = edge_latents.shape[1]
    PLANE = X * CORES
    TABLE = Z * PLANE * 2
    ROWS = 3 * D // Z
    OWN = ROWS // PLANE
    GROUP = X * ROWS
    BANDS = Z // X // CORES
    OWN_PAD = (OWN + 4 + 15) // 16 * 16
    COLS = D // Y
    outgoing = send_rows[0].T

    anywhere = pl.BlockSpec(memory_space=pl.ANY)
    smem = pl.BlockSpec(memory_space=pltpu.SMEM)
    scratch = [
        pltpu.VMEM((NODE, D), BF16),
        pltpu.VMEM((2, Z * PLANE), jnp.int32),
        pltpu.VMEM((1, D), F32),
        pltpu.VMEM((1, EDGE), jnp.int32),
        pltpu.VMEM((NODE, D), BF16),
        pltpu.VMEM((1, EDGE), jnp.int32),
        pltpu.VMEM((1, D), F32),
        pltpu.VMEM((NODE, D), BF16),
        pltpu.VMEM((NODE, D), BF16),
        pltpu.VMEM((3 * D, D), BF16),
        pltpu.VMEM((EDGE, 3 * D), BF16),
        pltpu.VMEM((EDGE, D), F32),
        pltpu.VMEM((EDGE, D), F32),
        pltpu.VMEM((EDGE, D), BF16),
        pltpu.VMEM((EDGE, D), BF16),
        pltpu.VMEM((EDGE, D), BF16),
        pltpu.VMEM((PLANE, Z * 2, D // 2), BF16),
        pltpu.VMEM((PLANE, Z * 2, D // 2), BF16),
        pltpu.VMEM((Z, PLANE * 2, D // 2), BF16),
        pltpu.VMEM((Z, PLANE * 2, D // 2), BF16),
        pltpu.VMEM((Z, PLANE * 2, D // 2), BF16),
        pltpu.VMEM((Z, PLANE * 2, D // 2), BF16),
        pltpu.VMEM((PLANE, Z * 2, D // 2), BF16),
        pltpu.VMEM((PLANE, Z * 2, D // 2), BF16),
        pltpu.VMEM((Z, PLANE * 2, D), BF16),
        pltpu.VMEM((Z, PLANE * 2, D), BF16),
        pltpu.VMEM((PLANE, Z * 2, D), BF16),
        pltpu.VMEM((PLANE, Z * 2, D), BF16),
        pltpu.VMEM((EDGE, BANDS * GROUP), BF16),
        pltpu.VMEM((EDGE, D), BF16),
        pltpu.VMEM((BANDS, GROUP, D), F32),
        pltpu.VMEM((Y, X * ROWS + 16, COLS), BF16),
        pltpu.VMEM((Y, X * ROWS + 16, COLS), BF16),
        pltpu.VMEM((X, ROWS, D), BF16),
        pltpu.VMEM((X, ROWS, D), BF16),
        pltpu.VMEM((X, ROWS + 16, COLS), BF16),
        pltpu.VMEM((X, ROWS + 16, COLS), BF16),
        pltpu.VMEM((Y, ROWS, COLS), BF16),
        pltpu.VMEM((Y, ROWS, COLS), BF16),
        pltpu.VMEM((BANDS, PLANE, OWN_PAD, COLS), BF16),
        pltpu.VMEM((Z, OWN_PAD, COLS), BF16),
        pltpu.VMEM((OWN_PAD, COLS), F32),
        pltpu.VMEM((EDGE, TABLE), BF16),
        pltpu.VMEM((EDGE, TABLE), BF16),
        pltpu.VMEM((8, D), F32),
        pltpu.VMEM((8, D), F32),
        pltpu.SemaphoreType.DMA((16,)),
        pltpu.SemaphoreType.DMA((STEPS,)),
        pltpu.SemaphoreType.DMA((STEPS,)),
    ]
    shapes = (
        jax.ShapeDtypeStruct((NODE, D), BF16),
        jax.ShapeDtypeStruct((NODE, D), BF16),
        jax.ShapeDtypeStruct((EDGE, D), BF16),
        jax.ShapeDtypeStruct((OWN, D), F32),
        jax.ShapeDtypeStruct((1, D), F32),
        jax.ShapeDtypeStruct((1, D), F32),
    )
    parts = shapes[:3] + (jax.ShapeDtypeStruct((Y, OWN_PAD, COLS), F32),)
    results = pl.pallas_call(
        functools.partial(kernel, (Z, X, Y, D, NODE, EDGE)),
        out_shape=parts,
        in_specs=[anywhere] * 9 + [smem] * 2,
        out_specs=(anywhere,) * 4,
        scratch_shapes=scratch,
        compiler_params=pltpu.CompilerParams(
            collective_id=0, has_side_effects=True, vmem_limit_bytes=VMEM_BYTES
        ),
        name="edge_update",
    )(
        node_latents[0],
        outgoing,
        edge_latents[0],
        w_in,
        bias.reshape(1, D),
        receivers.reshape(1, EDGE),
        node_cotangent[0],
        senders.reshape(1, EDGE),
        gain.reshape(1, D),
        node_count,
        edge_count,
    )
    new_nodes, grad_nodes, grad_edges, grad_weights, grad_bias, grad_gain = pl.pallas_call(
        copy_out,
        out_shape=shapes,
        in_specs=[anywhere] * 4,
        out_specs=(anywhere,) * 6,
        scratch_shapes=[pltpu.VMEM(s.shape, s.dtype) for s in parts + shapes[3:]]
        + [pltpu.SemaphoreType.DMA((10,))],
        compiler_params=pltpu.CompilerParams(vmem_limit_bytes=VMEM_BYTES),
        name="copy_out",
    )(*results)
    return (
        new_nodes[None],
        grad_nodes[None],
        grad_edges[None],
        grad_weights,
        grad_bias.reshape(D),
        grad_gain.reshape(D),
    )


def solution(mesh, x_chips=4):
    Y = mesh.shape["member"]
    Z = mesh.shape["dom"] // (x_chips * CORES)
    return jax.shard_map(
        functools.partial(shards, Z, x_chips, Y),
        mesh=mesh,
        in_specs=(
            P("member", "dom", None),
            P("member", "dom", None),
            P("member", "dom", None),
            P(),
            P(),
            P(),
            P("dom"),
            P("dom"),
            P("dom", None, None),
            P("dom"),
            P("dom"),
        ),
        out_specs=(
            P("member", "dom", None),
            P("member", "dom", None),
            P("member", "dom", None),
            P("dom", None),
            P(),
            P(),
        ),
        check_vma=False,
    )
```
